32 devices in a mesh: seq: 16 (over z, x, core), batch: 2 (over y).
Axes of the slice: x: 2, y: 2, z: 4, core: 2. Of those that a mesh axis runs over, the one named last changes fastest.
Arguments:
- tokens: bfloat16 [2, 2, 2048, 512], P(None, 'batch', 'seq'), may hold values from -6 to 6
- lengths: int32 [2, 2, 64], P(None, 'batch'), may hold values from 0 to 1984, as said below
- groups: int32 [2, 2], P(None, 'batch'), may hold values from 0 to 7
- cotangent: bfloat16 [2, 2, 2048, 512], P(None, 'batch', 'seq'), may hold values from -6 to 6
- attn_weights: float32 [4, 512, 512], P(None, 'seq', 'batch')
- ffn_weights: float32 [2, 512, 2048], P(None, 'seq', 'batch')
- small_params: float32 [10240], P(('seq', 'batch'))
- attn_rows: float32 [4, 512], P(None, 'seq'), as said below
- attn_cols: float32 [4, 512], P(None, 'batch'), as said below
- ffn_rows: float32 [2, 512], P(None, 'seq'), as said below
- ffn_cols: float32 [2, 2048], P(None, 'batch'), as said below
- small_sq: float32 [10240], P(('seq', 'batch')), as said below
Outputs:
- output: bfloat16 [2, 2, 2048, 512], P(None, 'batch', 'seq')
- input_grad: bfloat16 [2, 2, 2048, 512], P(None, 'batch', 'seq')
- attn_grad: float32 [4, 512, 512], P(None, 'seq', 'batch')
- ffn_grad: float32 [2, 512, 2048], P(None, 'seq', 'batch')
- small_grad: float32 [10240], P(('seq', 'batch'))
- attn_new: float32 [4, 512, 512], P(None, 'seq', 'batch')
- ffn_new: float32 [2, 512, 2048], P(None, 'seq', 'batch')
- small_new: float32 [10240], P(('seq', 'batch'))
- attn_copy: bfloat16 [4, 512, 512], P(None, 'seq', 'batch')
- ffn_copy: bfloat16 [2, 512, 2048], P(None, 'seq', 'batch')
- small_copy: bfloat16 [10240], P(('seq', 'batch'))
- attn_rows_new: float32 [4, 512], P(None, 'seq')
- attn_cols_new: float32 [4, 512], P(None, 'batch')
- ffn_rows_new: float32 [2, 512], P(None, 'seq')
- ffn_cols_new: float32 [2, 2048], P(None, 'batch')
- small_sq_new: float32 [10240], P(('seq', 'batch'))
The draws below stay inside these ranges and needn't reach their ends.
Inputs may be any that keep to these rules, and one draw needn't show every extreme that they name: In each row, 64 slots hold the lengths of the packed pairs in order; they sum to at most 2048; positions past the sum are filler; slots past the last pair hold 0. `attn_rows`: Positive. `attn_cols`: Positive. `ffn_rows`: Positive. `ffn_cols`: Positive. `small_sq`: Positive.
All inputs are finite; a program needn't handle non-finite values.
Results may differ from the reference program's by a relative error of at most 0.02.
Values may be sent and summed in bfloat16 or wider, within the bound.
A program may use at most 128 MiB of HBM per device.

```python
import jax
import jax.numpy as jnp
from jax import lax

D = 512
H = 8
HD = 64
FF = 2048
GROUPS = 8
SEGS = 64
MICRO = 2
STEP = 10
SEQ_DEV = 128
RB = 1
L = 2048
ROWS = 2
NVEC = 10240


def draw_lengths(key, part):
    key = jax.random.fold_in(key, 11)
    cap_key, length_key, pick_key = jax.random.split(key, 3)
    row_caps = jax.random.randint(cap_key, (MICRO, ROWS, 1), L // SEGS, 2 * L // SEGS + 1)
    uncapped = jax.random.randint(length_key, (MICRO, ROWS, SEGS), 1, row_caps + 1)
    row_ends = jnp.minimum(jnp.cumsum(uncapped, axis=-1), L).astype(jnp.int32)
    row_starts = jnp.concatenate([jnp.zeros((MICRO, ROWS, 1), jnp.int32), row_ends[:, :, :-1]], axis=-1)
    drawn_rows = (row_ends - row_starts).astype(jnp.int32)
    chosen_slot = jax.random.randint(pick_key, (ROWS // RB,), 0, MICRO * RB)
    micro_place = jnp.arange(MICRO, dtype=jnp.int32)[:, None]
    row_place = jnp.arange(ROWS, dtype=jnp.int32)[None, :]
    chosen = micro_place * RB + row_place % RB == chosen_slot[row_place // RB]
    slot_place = jnp.arange(SEGS, dtype=jnp.int32)
    spanning = jnp.where(slot_place == 0, L - SEQ_DEV // 2, jnp.where(slot_place == 1, SEQ_DEV // 2, 0)).astype(jnp.int32)
    return jnp.where(chosen[:, :, None], spanning[None, None, :], drawn_rows).astype(jnp.int32)


def draw_attn_weights(key, part):
    key = jax.random.fold_in(key, 12)
    entries = jax.random.truncated_normal(key, -4.0, 4.0, (4, D, D), jnp.float32)
    scales = jnp.array([D ** (-0.5), D ** (-0.5), D ** (-0.5), max(D // 32, 1) ** (-0.5)], jnp.float32)
    return entries * scales[:, None, None]


def draw_ffn_weights(key, part):
    key = jax.random.fold_in(key, 13)
    entries = jax.random.truncated_normal(key, -4.0, 4.0, (2, D, FF), jnp.float32)
    scales = jnp.array([D ** (-0.5), FF ** (-0.5)], jnp.float32)
    return entries * scales[:, None, None]


def draw_small_params(key, part):
    key = jax.random.fold_in(key, 14)
    noise_key, first_key, second_key = jax.random.split(key, 3)
    noise_all = jax.random.truncated_normal(noise_key, -4.0, 4.0, (NVEC,), jnp.float32)
    bottom = 0.5
    ramp_values = bottom + jnp.arange(D, dtype=jnp.float32) / (D - 1)
    gain_one = ramp_values * jax.random.uniform(first_key, (D,), jnp.float32, 0.85, 1.15)
    gain_two = ramp_values * jax.random.uniform(second_key, (D,), jnp.float32, 0.85, 1.15)
    biases = 0.2 * noise_all[:4 * D + FF]
    shift_one = 0.1 * noise_all[4 * D + FF:5 * D + FF]
    shift_two = 0.1 * noise_all[5 * D + FF:6 * D + FF]
    language = 0.5 * noise_all[6 * D + FF:6 * D + FF + GROUPS * D]
    return jnp.concatenate([biases, gain_one, shift_one, gain_two, shift_two, language])


def moment_scale(key, kinds, shape):
    uniform_draw = jax.random.uniform(key, shape, jnp.float32, 0.0, 1.0)
    return 0.13 * MICRO * ROWS * L * kinds * jnp.exp(1.3862944 * uniform_draw)


def draw_attn_rows(key, part):
    key = jax.random.fold_in(key, 15)
    return moment_scale(key, jnp.array([0.28, 0.28, 0.3, 0.007], jnp.float32)[:, None], (4, D))


def draw_attn_cols(key, part):
    key = jax.random.fold_in(key, 16)
    return moment_scale(key, jnp.array([0.28, 0.28, 0.3, 0.007], jnp.float32)[:, None], (4, D))


def draw_ffn_rows(key, part):
    key = jax.random.fold_in(key, 17)
    return moment_scale(key, jnp.array([0.033, 0.15], jnp.float32)[:, None], (2, D))


def draw_ffn_cols(key, part):
    key = jax.random.fold_in(key, 18)
    return moment_scale(key, jnp.array([0.033, 0.15], jnp.float32)[:, None], (2, FF))


def draw_small_sq(key, part):
    key = jax.random.fold_in(key, 19)
    kinds = jnp.concatenate([jnp.full((D,), 0.23, jnp.float32), jnp.full((D,), 0.25, jnp.float32), jnp.full((D,), 0.22, jnp.float32), jnp.full((FF,), 0.033, jnp.float32), jnp.full((D,), 0.36, jnp.float32), jnp.full((D,), 0.5, jnp.float32), jnp.full((D,), 0.5, jnp.float32), jnp.full((D,), 0.7, jnp.float32), jnp.full((D,), 0.7, jnp.float32), jnp.full((GROUPS * D,), 1.0 / GROUPS, jnp.float32)])
    return moment_scale(key, kinds, (NVEC,))


def place_ends(values, rng, least, high):
    extent = values.shape
    place = [jax.random.randint(jax.random.fold_in(rng, axis), (), 0, extent[axis]) for axis in range(len(extent))]
    values = values.at[tuple(place)].set(least)
    longest = extent.index(max(extent))
    place[longest] = (place[longest] + 1) % extent[longest]
    return values.at[tuple(place)].set(high)


def block_scale(rng, shape, cuts, least, high):
    def one(axis_at, parts):
        draws = jax.random.uniform(jax.random.fold_in(jax.random.fold_in(rng, 6), axis_at), (parts,), jnp.float32, least / len(cuts), high / len(cuts))
        return jnp.repeat(jnp.exp(draws), shape[axis_at] // parts).reshape((-1,) + (1,) * (len(shape) - axis_at - 1))

    level = one(*cuts[0])
    for cut in cuts[1:]:
        level = level * one(*cut)
    return level


def gaussian(own_key, dims, scale, bound, shards=(), held_as=jnp.bfloat16):
    drawn = scale * jax.random.normal(own_key, dims, jnp.float32)
    if shards:
        drawn = drawn * block_scale(own_key, dims, shards, -0.22, 0.18)
    return jnp.clip(drawn, -bound, bound).astype(held_as)


def setup_inputs(seed: int = 0) -> dict:
    arg_keys = jax.random.split(jax.random.key(seed), 13)
    return {
        "tokens": gaussian(arg_keys[0], (MICRO, ROWS, L, D), 1.0, 6.0, ((1, 2), (2, 16))),
        "lengths": draw_lengths(jax.random.fold_in(arg_keys[12], 71), 0),
        "groups": place_ends(jax.random.randint(arg_keys[2], (MICRO, ROWS), 0, GROUPS), jax.random.fold_in(arg_keys[2], 1), 0, GROUPS - 1).astype(jnp.int32),
        "cotangent": gaussian(arg_keys[3], (MICRO, ROWS, L, D), 1.0, 6.0, ((1, 2), (2, 16))),
        "attn_weights": draw_attn_weights(jax.random.fold_in(arg_keys[12], 71), 0),
        "ffn_weights": draw_ffn_weights(jax.random.fold_in(arg_keys[12], 71), 0),
        "small_params": draw_small_params(jax.random.fold_in(arg_keys[12], 71), 0),
        "attn_rows": draw_attn_rows(jax.random.fold_in(arg_keys[12], 71), 0),
        "attn_cols": draw_attn_cols(jax.random.fold_in(arg_keys[12], 71), 0),
        "ffn_rows": draw_ffn_rows(jax.random.fold_in(arg_keys[12], 71), 0),
        "ffn_cols": draw_ffn_cols(jax.random.fold_in(arg_keys[12], 71), 0),
        "small_sq": draw_small_sq(jax.random.fold_in(arg_keys[12], 71), 0),
    }


NEG = -1e+30
EPS = 1e-05
EPS_ONE = 1e-30
LEARN = 1.0
HIGHEST = lax.Precision.HIGHEST

@jax.custom_vjp
def low(v):
    return lax.optimization_barrier(v.astype(jnp.bfloat16)).astype(jnp.float32)

@jax.custom_vjp
def low_back(v):
    return v

def low_keep(v):
    return (low(v), None)

def low_pass(kept, grad):
    return (grad,)

def back_keep(v):
    return (v, None)

def back_low(kept, grad):
    return (low(grad),)
low.defvjp(low_keep, low_pass)
low_back.defvjp(back_keep, back_low)

def unpack_small(vector):
    widths = (D, D, D, FF, D, D, D, D, D)
    pieces = []
    offset = 0
    for amount in widths:
        pieces.append(vector[offset:offset + amount])
        offset = offset + amount
    pieces.append(vector[offset:].reshape(GROUPS, D))
    return pieces

def layer_norm(values, norm_gain, norm_shift):
    center = values - lax.optimization_barrier(jnp.mean(values, axis=-1, keepdims=True))
    inverse = lax.rsqrt(lax.optimization_barrier(jnp.mean(center * center, axis=-1, keepdims=True)) + EPS)
    return center * inverse * norm_gain + norm_shift

def segment_ids(lengths_row):
    row_ends = jnp.cumsum(lengths_row).astype(jnp.int32)
    places = jnp.arange(L, dtype=jnp.int32)
    return lax.optimization_barrier(jnp.sum((row_ends[None, :] <= places[:, None]).astype(jnp.int32), axis=1)).astype(jnp.int32)

def attend_row(queries, key_rows, value_rows, seg_row):
    span_query = min(512, L)
    places = jnp.arange(L, dtype=jnp.int32)

    def one_block(offset):
        query_block = lax.dynamic_slice_in_dim(queries, offset, span_query, 0)
        seg_query = lax.dynamic_slice_in_dim(seg_row, offset, span_query, 0)
        pos_query = offset + jnp.arange(span_query, dtype=jnp.int32)
        scores = jnp.einsum('qhd,khd->hqk', query_block, key_rows, precision=HIGHEST) * HD ** (-0.5)
        scores = low_back(scores)
        allowed = (seg_query[:, None] == seg_row[None, :]) & (seg_row[None, :] < SEGS) | (pos_query[:, None] == places[None, :])
        prob_block = jax.nn.softmax(jnp.where(allowed[None], scores, NEG), axis=-1)
        return jnp.einsum('hqk,khd->qhd', low(prob_block), value_rows, precision=HIGHEST)
    offsets = jnp.arange(L // span_query, dtype=jnp.int32) * span_query
    return lax.map(jax.checkpoint(one_block), offsets).reshape(L, D)

def forward(flat_tokens, attn_weights, ffn_weights, small_params, seg_ids, group_flat):
    attn_low = low(attn_weights)
    ffn_low = low(ffn_weights)
    small_low = low(small_params)
    bias_q, bias_v, bias_o, bias_in, bias_back, gain_one, shift_one, gain_two, shift_two, lang_table = unpack_small(small_low)

    def row_pass(inputs):
        tokens_row, seg_row, group_id = inputs
        mixed_in = tokens_row + lang_table[group_id]
        attn_in = low(mixed_in)
        queries = low(low_back(jnp.dot(attn_in, attn_low[0], precision=HIGHEST) + bias_q))
        key_rows = low(low_back(jnp.dot(attn_in, attn_low[1], precision=HIGHEST)))
        value_rows = low(low_back(jnp.dot(attn_in, attn_low[2], precision=HIGHEST) + bias_v))
        mixed = attend_row(queries.reshape(L, H, HD), key_rows.reshape(L, H, HD), value_rows.reshape(L, H, HD), seg_row)
        mixed = low(low_back(mixed))
        attn_out = low_back(jnp.dot(mixed, attn_low[3], precision=HIGHEST) + bias_o)
        hidden = layer_norm(mixed_in + attn_out, gain_one, shift_one)
        gate_pre = low_back(jnp.dot(low(hidden), ffn_low[0], precision=HIGHEST) + bias_in)
        active = low(jax.nn.gelu(gate_pre))
        branch = low_back(jnp.dot(active, ffn_low[1].T, precision=HIGHEST) + bias_back)
        return layer_norm(hidden + branch + mixed_in, gain_two, shift_two)
    return lax.map(jax.checkpoint(row_pass), (flat_tokens, seg_ids, group_flat))

def factored_update(grad, weight, rows_old, cols_old, decay):
    square = grad * grad + EPS_ONE
    rows_new = decay * rows_old + (1.0 - decay) * lax.optimization_barrier(jnp.mean(square, axis=-1))
    cols_new = decay * cols_old + (1.0 - decay) * lax.optimization_barrier(jnp.mean(square, axis=-2))
    rows_rel = rows_new / lax.optimization_barrier(jnp.mean(rows_new, axis=-1, keepdims=True))
    update = grad * lax.rsqrt(rows_rel[:, :, None] * cols_new[:, None, :])
    update_rms = jnp.sqrt(lax.optimization_barrier(jnp.mean(update * update, axis=(1, 2), keepdims=True)))
    weight_rms = jnp.sqrt(lax.optimization_barrier(jnp.mean(weight * weight, axis=(1, 2), keepdims=True)))
    new_weight = weight - LEARN * weight_rms * update / jnp.maximum(1.0, update_rms)
    return (new_weight, rows_new, cols_new)

def reference(tokens, lengths, groups, cotangent, attn_weights, ffn_weights, small_params, attn_rows, attn_cols, ffn_rows, ffn_cols, small_sq):
    count_rows = MICRO * ROWS
    flat_tokens = tokens.astype(jnp.float32).reshape(count_rows, L, D)
    seg_ids = jax.vmap(segment_ids)(lengths.reshape(count_rows, SEGS))
    group_flat = groups.reshape(count_rows)

    def wrapped(tokens_in, attn_in, ffn_in, small_in):
        return forward(tokens_in, attn_in, ffn_in, small_in, seg_ids, group_flat)
    outputs, pullback = jax.vjp(wrapped, flat_tokens, attn_weights, ffn_weights, small_params)
    cotangent_live = cotangent.astype(jnp.float32).reshape(count_rows, L, D) * (seg_ids < SEGS).astype(jnp.float32)[:, :, None]
    input_grad, attn_grad, ffn_grad, small_grad = pullback(cotangent_live)
    decay = 1.0 - STEP ** (-0.8)
    attn_new, attn_rows_new, attn_cols_new = factored_update(attn_grad, attn_weights, attn_rows, attn_cols, decay)
    ffn_new, ffn_rows_new, ffn_cols_new = factored_update(ffn_grad, ffn_weights, ffn_rows, ffn_cols, decay)
    small_sq_new = decay * small_sq + (1.0 - decay) * (small_grad * small_grad + EPS_ONE)
    small_update = small_grad * lax.rsqrt(small_sq_new)
    small_rms = jnp.sqrt(jnp.mean(small_params * small_params))
    small_new = small_params - LEARN * small_rms * small_update / jnp.maximum(1.0, jnp.sqrt(jnp.mean(small_update * small_update)))
    return (outputs.reshape(tokens.shape).astype(jnp.bfloat16), input_grad.reshape(tokens.shape).astype(jnp.bfloat16), attn_grad, ffn_grad, small_grad, attn_new, ffn_new, small_new, attn_new.astype(jnp.bfloat16), ffn_new.astype(jnp.bfloat16), small_new.astype(jnp.bfloat16), attn_rows_new, attn_cols_new, ffn_rows_new, ffn_cols_new, small_sq_new)
```

```python
import functools

import jax
import jax.numpy as jnp
from jax import lax
from jax.experimental import pallas as pl
from jax.experimental.pallas import tpu as pltpu
from jax.sharding import PartitionSpec as P

D = 512
H = 8
HD = 64
FF = 2048
GROUPS = 8
SEGS = 64
STEP = 10
NVEC = 10240
LANES = 128

NEG = -1e30
EPS = 1e-05
EPS_ONE = 1e-30
LEARN = 1.0
DECAY = 1.0 - STEP ** (-0.8)
SCALE = HD ** (-0.5)
LOG2E = 1.4426950408889634
FRAMES = 16
FRAME_ROWS = NVEC // FRAMES // LANES
GROUP = 4
BF = jnp.bfloat16
F32 = jnp.float32
VMEM_SPEC = pl.BlockSpec(memory_space=pltpu.VMEM)
SMEM_SPEC = pl.BlockSpec(memory_space=pltpu.SMEM)

ROW_BQ, ROW_BV, ROW_BO, ROW_B1, ROW_B2 = 0, 4, 8, 12, 28
ROW_G1, ROW_S1, ROW_G2, ROW_S2, ROW_E = 32, 36, 40, 44, 48


def mm(a, b):
    return lax.dot_general(a, b, (((1,), (0,)), ((), ())), preferred_element_type=F32)


def mm_nt(a, b):
    return lax.dot_general(a, b, (((1,), (1,)), ((), ())), preferred_element_type=F32)


def mm_tn(a, b):
    return lax.dot_general(a, b, (((0,), (0,)), ((), ())), preferred_element_type=F32)


def small_piece(small_ref, row, count):
    parts = [small_ref[r // FRAME_ROWS, pl.ds(r % FRAME_ROWS, 1), :] for r in range(row, row + count)]
    return jnp.concatenate(parts, axis=1)


def add_small(ref, row, values):
    for k in range(values.shape[1] // LANES):
        r = row + k
        ref[r // FRAME_ROWS, pl.ds(r % FRAME_ROWS, 1), :] += values[:, k * LANES : (k + 1) * LANES]


def low_half():
    return lax.broadcasted_iota(jnp.int32, (1, LANES), 1) < HD


def swap_halves(x):
    return pltpu.roll(x, HD, 1)


def heads_to_rows(tiles):
    low = low_half()
    first, second = [], []
    for j in range(H // 2):
        a, b = tiles[2 * j], tiles[2 * j + 1]
        first.append(jnp.where(low, a, swap_halves(b)))
        second.append(jnp.where(low, swap_halves(a), b))
    return jnp.concatenate(first, axis=1), jnp.concatenate(second, axis=1)


def rows_to_heads(first, second):
    low = low_half()
    tiles = []
    for j in range(H // 2):
        a = first[:, j * LANES : (j + 1) * LANES]
        b = second[:, j * LANES : (j + 1) * LANES]
        tiles.append(jnp.where(low, a, swap_halves(b)))
        tiles.append(jnp.where(low, swap_halves(a), b))
    return tiles


def wrap(value, count):
    return value - jnp.where(value >= count, count, 0)


def outwards(count):
    return sorted(range(1, count), key=lambda k: (abs(2 * k - count), k))


class Place:
    def __init__(self):
        self.n_s, self.n_b = lax.axis_size("seq"), lax.axis_size("batch")
        self.s, self.b = lax.axis_index("seq"), lax.axis_index("batch")
        self.n_z, self.parts = self.n_s // 4, self.n_s // H
        self.z, self.xc = self.s // 4, self.s % 4
        self.x, self.c = self.xc // 2, self.xc % 2
        self.other_x = (1 - self.x) * 2 + self.c
        self.other_c = self.x * 2 + 1 - self.c
        self.h, self.g = self.s // self.parts, self.s % self.parts
        self.z_ahead = [wrap(self.z + k, self.n_z) for k in range(self.n_z)]
        self.b_ahead = [wrap(self.b + k, self.n_b) for k in range(self.n_b)]
        self.xc_ahead = [wrap(self.xc + k, 4) for k in range(4)]
        self.h_ahead = [wrap(self.h + k, H) for k in range(H)]
        self.g_ahead = [wrap(self.g + k, self.parts) for k in range(self.parts)]
        self.at_z = [z * 4 + self.xc for z in self.z_ahead]
        self.at_x, self.at_core = self.z * 4 + self.other_x, self.z * 4 + self.other_c
        self.at_head = [h * self.parts + self.g for h in self.h_ahead]
        self.at_part = [self.h * self.parts + g for g in self.g_ahead]

    def along_z(self, k):
        return (self.at_z[k], self.b)

    def across_x(self):
        return (self.at_x, self.b)

    def across_core(self):
        return (self.at_core, self.b)

    def batch_ahead(self, k):
        return self.b_ahead[k]

    def batch_behind(self, k):
        return self.b_ahead[(self.n_b - k) % self.n_b]

    def across_batch(self, k):
        return (self.s, self.b_ahead[k])

    def head_ahead(self, k):
        return self.h_ahead[k % H] if isinstance(k, int) else wrap(self.h + k, H)

    def head_behind(self, k):
        return self.h_ahead[(H - k) % H] if isinstance(k, int) else wrap(self.h + H - k, H)

    def across_heads(self, k):
        return (self.at_head[k] if isinstance(k, int) else self.head_ahead(k) * self.parts + self.g, self.b)

    def part_ahead(self, k):
        return self.g_ahead[k]

    def across_parts(self, k):
        return (self.at_part[k], self.b)


def greet(peers):
    barrier = pltpu.get_barrier_semaphore()
    for peer in peers:
        pl.semaphore_signal(barrier, inc=1, device_id=peer, device_id_type=pl.DeviceIdType.MESH)
    pl.semaphore_wait(barrier, len(peers))


def greet_all(place):
    barrier = pltpu.get_barrier_semaphore()

    def hello(b, i, carry):
        peer = (wrap(place.s + i, place.n_s), b)
        pl.semaphore_signal(barrier, inc=1, device_id=peer, device_id_type=pl.DeviceIdType.MESH)
        return carry

    for k, b in enumerate(place.b_ahead):
        lax.fori_loop(0 if k else 1, place.n_s, functools.partial(hello, b), 0)
    pl.semaphore_wait(barrier, place.n_s * place.n_b - 1)


def far_first(i):
    if isinstance(i, int) and i in (0, H):
        return i
    return H // 2 + i // 2 * (1 - i % 2 * 2)


class Copy:
    def __init__(self, wire, i, build):
        self.wire, self.i, self.build = wire, i, build

    def made(self):
        return self.wire.make(self.i, *self.build())

    def start(self):
        self.made().start()

    def wait_recv(self):
        self.made().wait_recv()

    def wait_send(self):
        self.made().wait_send()


class Wire:
    def __init__(self, send_sems, recv_sems):
        self.send_sems, self.recv_sems, self.copies, self.used = send_sems, recv_sems, [], 0

    def reserve(self, count):
        self.used += count
        return self.used - count

    def make(self, i, src, dst, peer):
        return pltpu.make_async_remote_copy(
            src_ref=src,
            dst_ref=dst,
            send_sem=self.send_sems.at[i],
            recv_sem=self.recv_sems.at[i],
            device_id=peer,
            device_id_type=pl.DeviceIdType.MESH,
        )

    def plan(self, build):
        return Copy(self, self.reserve(1), build)

    def send(self, build):
        copy = self.plan(build)
        copy.start()
        self.copies.append(copy)
        return copy

    def drain(self):
        for copy in self.copies:
            copy.wait_send()
        self.copies = []


def received(copies):
    for copy in copies:
        copy.wait_recv()


class Gather:
    def __init__(self, place, wire, src, dst, own_sem, cut):
        self.place, self.wire, self.src, self.dst, self.cut, self.own_sem = place, wire, src, dst, cut, own_sem
        self.own().start()
        self.along = [wire.send(lambda k=k: (src, self.slot(place.z), place.along_z(k))) for k in range(1, place.n_z)]

    def slot(self, z):
        return self.dst.at[self.place.b, :, z, self.place.xc]

    def own(self):
        return pltpu.make_async_copy(self.src, self.slot(self.place.z), self.own_sem)

    def forward(self, part, *peers):
        return [self.wire.send(lambda peer=peer: (part(), part(), peer())) for peer in peers]

    def column(self, b, xc):
        return lambda: self.dst.at[b(), :, :, xc]

    def half(self, b, xc, second):
        span = pl.ds(self.cut, self.place.n_z - self.cut) if second else pl.ds(0, self.cut)
        return lambda: self.dst.at[b(), :, span, xc]

    def batch_peers(self):
        return [lambda k=k: self.place.across_batch(k) for k in range(1, self.place.n_b)]

    def to_plane(self):
        p = self.place
        self.own().wait()
        received(self.along)
        peers = [p.across_x, p.across_core] + self.batch_peers()
        self.plane = self.forward(self.column(lambda: p.b, p.xc), *peers)

    def to_diagonal(self):
        p = self.place
        self.plane[0].wait_recv()
        self.diagonal = self.forward(self.half(lambda: p.b, p.other_x, 0), *self.batch_peers())
        self.cores = [self.plane[1]] + self.forward(self.column(lambda: p.b, p.other_x), p.across_core)
        for k in range(1, p.n_b):
            b = lambda k=k: p.batch_behind(k)
            self.plane[1 + k].wait_recv()
            self.diagonal += self.forward(self.half(b, p.xc, 1), p.across_x)
            self.cores += self.forward(self.column(b, p.xc), p.across_core)

    def to_cores(self):
        p = self.place
        for k in range(1, p.n_b):
            for second in range(2):
                self.diagonal[(p.n_b - 1) * second + k - 1].wait_recv()
                part = self.half(lambda k=k: p.batch_behind(k), p.other_x, second)
                self.cores += self.forward(part, p.across_core)

    def finish(self):
        received(self.cores)


class ShortGather(Gather):
    def to_plane(self):
        p = self.place
        self.own().wait()
        received(self.along)
        diagonal = [
            lambda k=k: (p.z * 4 + p.other_x, p.batch_ahead(k)) for k in range(1, p.n_b)
        ]
        peers = [p.across_core, p.across_x] + self.batch_peers() + diagonal
        self.plane = self.forward(self.column(lambda: p.b, p.xc), *peers)

    def to_cores(self):
        p = self.place
        behind = [lambda k=k: p.batch_behind(k) for k in range(1, p.n_b)]
        columns = [(lambda: p.b, p.other_x)] + [(b, p.xc) for b in behind] + [(b, p.other_x) for b in behind]
        self.cores = [self.plane[0]]
        for copy, (b, xc) in zip(self.plane[1:], columns):
            copy.wait_recv()
            self.cores += self.forward(self.column(b, xc), p.across_core)


def normed_of(values):
    center = values - jnp.mean(values, axis=-1, keepdims=True)
    inverse = lax.rsqrt(jnp.mean(center * center, axis=-1, keepdims=True) + EPS)
    return center * inverse, inverse


def norm_back(grad_norm, normed, inverse):
    return inverse * (
        grad_norm
        - jnp.mean(grad_norm, axis=-1, keepdims=True)
        - normed * jnp.mean(grad_norm * normed, axis=-1, keepdims=True)
    )


def gelu_pair(z):
    c = 0.7978845608028654
    z2 = z * z
    t = jnp.tanh(c * z * (1.0 + 0.044715 * z2))
    half = 0.5 * (1.0 + t)
    slope = half + 0.5 * z * (1.0 - t * t) * (c * (1.0 + 3 * 0.044715 * z2))
    return z * half, slope


def language_rows(groups_ref, small_ref, rows):
    table = [small_piece(small_ref, ROW_E + 4 * e, 4) for e in range(GROUPS)]
    out = []
    for m in range(rows):
        acc = jnp.zeros_like(table[0])
        for e in range(GROUPS):
            acc = acc + jnp.where(groups_ref[m] == e, table[e], 0.0)
        out.append(acc)
    return out


def column_sum(x):
    return jnp.sum(x, axis=0, keepdims=True)


class Scatter:
    def __init__(self, place, wire, part, core, acc, far, near, plane_x, plane_b, column):
        self.begin(place, wire, part, core, acc, column)
        self.far, self.near, self.plane_x, self.plane_b = far, near, plane_x, plane_b
        self.cut = far.shape[2]

    def begin(self, place, wire, part, core, acc, column):
        self.place, self.wire = place, wire
        self.part, self.core, self.acc, self.column = part, core, acc, column
        self.kind = part.dtype
        self.x, self.c = place.x, place.c
        self.slabs = part.shape[1]

    def add(self, target, *others):
        total = target[...].astype(F32)
        for other in others:
            total = total + other[...].astype(F32)
        target[...] = total.astype(self.kind)

    def each(self, body, first=0, last=None):
        for j in range(self.slabs):

            def step(z, carry, j=j):
                body(j, z)
                return carry

            lax.fori_loop(first, self.place.n_z if last is None else last, step, 0)

    def to_core(self):
        p = self.place
        self.moved = [self.wire.send(lambda: (self.part.at[:, :, :, :, 1 - self.c], self.core, p.across_core()))]

    def join(self):
        p = self.place
        received(self.moved)
        for j in range(self.slabs):

            def body(b, carry, j=j):
                def at_z(z, carry):
                    for x in range(2):
                        total = self.part[b, j, z, x, self.c].astype(F32) + self.core[b, j, z, x].astype(F32)
                        self.acc[b, j, z, x] = total.astype(self.kind)
                    return carry

                return lax.fori_loop(0, p.n_z, at_z, carry)

            lax.fori_loop(0, p.n_b, body, 0)

    def to_diagonal(self):
        p = self.place
        self.join()
        cut, rest = pl.ds(0, self.cut), pl.ds(self.cut, p.n_z - self.cut)
        self.moved_far, self.moved_near = [], []
        for k in range(1, p.n_b):
            diagonal = lambda k=k: self.acc.at[p.batch_ahead(k), :, :, 1 - self.x]
            self.moved_far.append(
                self.wire.send(
                    lambda k=k, part=diagonal: (part().at[:, cut], self.far.at[k - 1], p.across_batch(k))
                )
            )
            self.moved_near.append(
                self.wire.send(lambda k=k, part=diagonal: (part().at[:, rest], self.near.at[k - 1], p.across_x()))
            )

    def to_plane(self):
        p = self.place
        for k in range(1, p.n_b):
            self.moved_near[k - 1].wait_recv()
            self.each(
                lambda j, z, k=k: self.add(
                    self.acc.at[p.batch_ahead(k), j, z, self.x], self.near.at[k - 1, j, z - self.cut]
                ),
                self.cut,
            )
        received(self.moved_far)
        self.each(
            lambda j, z: self.add(
                self.acc.at[p.b, j, z, 1 - self.x], *[self.far.at[k - 1, j, z] for k in range(1, p.n_b)]
            ),
            0,
            self.cut,
        )
        self.moved = [self.wire.send(lambda: (self.acc.at[p.b, :, :, 1 - self.x], self.plane_x, p.across_x()))]
        self.moved += [
            self.wire.send(
                lambda k=k: (
                    self.acc.at[p.batch_ahead(k), :, :, self.x],
                    self.plane_b.at[k - 1],
                    p.across_batch(k),
                )
            )
            for k in range(1, p.n_b)
        ]

    def others(self, j, z):
        return [self.plane_x.at[j, z]] + [self.plane_b.at[k - 1, j, z] for k in range(1, self.place.n_b)]

    def to_owner(self):
        p = self.place
        received(self.moved)
        self.each(lambda j, z: self.add(self.acc.at[p.b, j, z, self.x], *self.others(j, z)))
        self.moved = [
            self.wire.send(
                lambda k=k: (
                    self.acc.at[p.b, :, p.z_ahead[k], self.x],
                    self.column.at[k - 1],
                    p.along_z(k),
                )
            )
            for k in range(1, p.n_z)
        ]

    def total(self, j):
        p = self.place
        out = self.acc[p.b, j, p.z, self.x].astype(F32)
        for k in range(1, p.n_z):
            out = out + self.column[k - 1, j].astype(F32)
        return out

    def finish(self):
        received(self.moved)


class ShortScatter(Scatter):
    def __init__(self, place, wire, part, core, acc, plane, column):
        self.begin(place, wire, part, core, acc, column)
        self.plane = plane

    def to_plane(self):
        p = self.place
        self.join()
        self.moved = []
        for k in range(p.n_b):
            for dx in range(2):
                if k or dx:

                    def build(k=k, dx=dx, slot=len(self.moved)):
                        x = self.x if dx == 0 else 1 - self.x
                        to = p.z * 4 + (p.other_x if dx else p.xc)
                        b = p.batch_ahead(k)
                        return (self.acc.at[b, :, :, x], self.plane.at[slot], (to, b))

                    self.moved.append(self.wire.send(build))

    def others(self, j, z):
        return [self.plane.at[k, j, z] for k in range(2 * self.place.n_b - 1)]


def short_scratch(n_b, slabs, n_z, r, cols, kind):
    return [
        pltpu.VMEM((n_b, slabs, n_z, 2, r, cols), kind),
        pltpu.VMEM((n_b, slabs, n_z, 2, r, cols), kind),
        pltpu.VMEM((2 * n_b - 1, slabs, n_z, r, cols), kind),
        pltpu.VMEM((n_z - 1, slabs, r, cols), kind),
    ]


def scatter_scratch(n_b, slabs, n_z, r, cols, kind):
    return [
        pltpu.VMEM((n_b, slabs, n_z, 2, r, cols), kind),
        pltpu.VMEM((n_b, slabs, n_z, 2, r, cols), kind),
        pltpu.VMEM((n_b - 1, slabs, n_z - n_z // 4, r, cols), kind),
        pltpu.VMEM((n_b - 1, slabs, n_z // 4, r, cols), kind),
        pltpu.VMEM((slabs, n_z, r, cols), kind),
        pltpu.VMEM((n_b - 1, slabs, n_z, r, cols), kind),
        pltpu.VMEM((n_z - 1, slabs, r, cols), kind),
    ]


SCATTER_SCRATCH, SHORT_SCRATCH = 7, 4
SLABS = 6


def lanes_of(values):
    lane = lax.broadcasted_iota(jnp.int32, (8, LANES), 1)
    row = lax.broadcasted_iota(jnp.int32, (8, LANES), 0)
    tile = jnp.zeros((8, LANES), F32)
    for j, value in enumerate(values):
        if value is not None:
            tile = tile + jnp.where((lane == j) & (row == 0), value, 0.0)
    return tile


def sum_all(x):
    return jnp.sum(jnp.sum(x, axis=1, keepdims=True), axis=0, keepdims=True)


def to_frame(values, at):
    wide = jnp.concatenate([values, jnp.zeros((1, 8 * LANES - values.shape[1]), F32)], axis=1)
    wide = pltpu.roll(wide, at, 1)
    return jnp.concatenate([wide[:, k * LANES : (k + 1) * LANES] for k in range(8)], axis=0)


def from_frame(tile, at, chunk):
    wide = jnp.concatenate([tile[k : k + 1] for k in range(8)], axis=1)
    return pltpu.roll(wide, 8 * LANES - at, 1)[:, :chunk]


def own_place(chunk):
    index = lax.axis_index("seq") * lax.axis_size("batch") + lax.axis_index("batch")
    return lax.rem(index * chunk, FRAME_ROWS * LANES)


def segment_ids(lengths, idk_ref, idq_ref, place, tokens):
    rows, length = idk_ref.shape[0], idk_ref.shape[1]
    upto = lax.broadcasted_iota(jnp.int32, (SEGS, LANES), 0) <= lax.broadcasted_iota(jnp.int32, (SEGS, LANES), 1)
    upto = jnp.where(upto, 1.0, 0.0).astype(BF)
    values = lengths.astype(F32)
    high = jnp.floor(values * (1.0 / 64))
    low = (values - 64.0 * high).astype(BF)
    high = high.astype(BF)
    ends = mm(high, upto) * 64.0 + mm(low, upto)
    ends = jnp.where(lax.broadcasted_iota(jnp.int32, (rows, LANES), 1) < SEGS, ends, 1e9)
    upto = upto[:, :SEGS]
    ends_down = lax.dot_general(upto, high, (((0,), (1,)), ((), ())), preferred_element_type=F32) * 64.0
    ends_down = ends_down + lax.dot_general(upto, low, (((0,), (1,)), ((), ())), preferred_element_type=F32)
    ones = jnp.ones((LANES, LANES), BF)
    span = 256
    for m in range(rows):

        def fill(i, carry, m=m):
            at = pl.multiple_of(i * span, span)
            places = (at + lax.broadcasted_iota(jnp.int32, (span, LANES), 0)).astype(F32)
            passed = jnp.where(ends[m : m + 1] <= places, 1.0, 0.0).astype(BF)
            seg = mm(passed, ones)
            idk_ref[m, pl.ds(at, span), :] = jnp.where(seg < SEGS, seg, SEGS + places)
            return carry

        lax.fori_loop(0, length // span, fill, 0)
        for h in range(H):
            first = ((h * place.parts + place.g) * tokens + lax.broadcasted_iota(jnp.int32, (1, tokens), 1)).astype(F32)
            seg = column_sum(jnp.where(ends_down[:, m : m + 1] <= first, 1.0, 0.0))
            group, k = h // GROUP, h % GROUP
            idq_ref[m, group, :, k * tokens : (k + 1) * tokens] = jnp.where(seg < SEGS, seg, SEGS + first)


def layer_kernel(
    groups_ref, lengths_ref, tok_ref, cot_ref, attn_ref, ffn_ref, params_ref, arows_ref, acols_ref, frows_ref,
    fcols_ref, sq_ref,
    out_hbm, du_hbm, agrad_hbm, fgrad_hbm, update_a_hbm, update_f_hbm, scales_ref, rows_new_ref, acols_new_ref,
    fcols_new_ref, own_new_ref,
    *scratch,
):
    place = Place()
    scratch = list(scratch)
    own_sems, recv_sems, send_sems = scratch.pop(), scratch.pop(), scratch.pop()
    wire = Wire(send_sems, recv_sems)

    def take(count):
        taken = scratch[:count]
        del scratch[:count]
        return taken

    pack_low, kv_low, wo_low, ffn_low, own_ref, small_ref, pack_ref, wkv_ref, wo_ref, w1_ref, w2_ref = take(11)
    idk_ref, idq_ref, q_ref, kv_ref, qsend_ref, kvsend_ref, qm_ref, dom_ref = take(8)
    peak_ref, acc_ref, ot_ref, lse_ref, delta_ref, o_ref, otile_ref, dotile_ref, do_ref = take(9)
    act_ref, slope_ref, dz_ref, sum_ref, frames_ref = take(5)
    dqt_ref, part_ref, near_ref, dkv_sum, dq_ref, dq_back, dkv_back = take(7)
    dwo_ref, dw1_ref, dw2_ref, dkv_w_ref, dq_w_ref, dsmall_ref = take(6)
    cols_plane, rows_plane, all_z, late_cols, late_rows, late_sums, all_sums = take(7)
    out_ref, du_ref, agrad_ref, fgrad_ref, update_a, update_f = take(6)
    written = [
        pltpu.make_async_copy(src, dst, own_sems.at[5 + i])
        for i, (src, dst) in enumerate(
            (
                (out_ref, out_hbm),
                (du_ref, du_hbm),
                (agrad_ref, agrad_hbm),
                (fgrad_ref, fgrad_hbm),
                (update_a, update_a_hbm),
                (update_f, update_f_hbm),
            )
        )
    ]
    n_z, n_b, parts = place.n_z, place.n_b, place.parts
    rows = 2
    count = tok_ref.shape[0]
    tokens = count // rows
    r, cols = attn_ref.shape[1:]
    cols_f = ffn_ref.shape[2]
    groups = H // GROUP
    width = GROUP * tokens
    keys = parts * tokens
    scale2 = SCALE * LOG2E
    low = low_half()

    plane = [(dx, db) for db in range(n_b) for dx in range(4) if dx or db]

    def plane_peer(dx, db):
        return (place.z * 4 + place.xc_ahead[dx], place.batch_ahead(db))

    along = [place.along_z(k) for k in range(1, n_z)]
    greet_all(place)

    chunk = params_ref.shape[0]
    own_at = own_place(chunk)
    own = to_frame(params_ref[...].reshape(1, chunk), own_at)
    own_ref[...] = own
    pack_low[0, :r] = attn_ref[0].astype(BF)
    tile = jnp.concatenate([own, jnp.zeros((8, LANES), F32)], axis=0)
    if cols < LANES:
        tile = jnp.concatenate([own[:, :cols], own[:, cols:]], axis=0)
    if cols > LANES:
        tile = jnp.concatenate([tile, jnp.zeros((16, cols - LANES), F32)], axis=1)
    pack_low[0, r:] = tile.astype(BF)
    pack = ShortGather(place, wire, pack_low, pack_ref, own_sems.at[0], n_z)
    kv_low[...] = attn_ref[1:3].astype(BF)
    kv_w = ShortGather(place, wire, kv_low, wkv_ref, own_sems.at[4], n_z)
    wo_low[0] = attn_ref[3].astype(BF)
    ffn_low[...] = ffn_ref[...].astype(BF)
    segment_ids(lengths_ref[...], idk_ref, idq_ref, place, tokens)
    for i in range(rows * groups):
        peak_ref[i] = jnp.full((1, width), NEG, F32)
        acc_ref[i] = jnp.zeros((HD + 16, width), F32)
    frames_ref[...] = jnp.zeros_like(frames_ref)
    dqt_ref[...] = jnp.zeros_like(dqt_ref)
    pack.to_plane()
    kv_w.to_plane()
    most = n_z - n_z // 4
    first = Gather(place, wire, ffn_low.at[pl.ds(0, 1)], w1_ref, own_sems.at[1], most)
    out_w = Gather(place, wire, wo_low, wo_ref, own_sems.at[2], most)
    second = Gather(place, wire, ffn_low.at[pl.ds(1, 1)], w2_ref, own_sems.at[3], most)
    pack.to_cores()
    pack.finish()
    frame = place.n_s * n_b // FRAMES
    for f in range(FRAMES):
        total = None
        for i in range(f * frame, (f + 1) * frame):
            s, b = i // n_b, i % n_b
            tile = pack_ref[b, 0, s // 4, s % 4, r:].astype(F32)
            if cols < LANES:
                tile = jnp.concatenate([tile[:8], tile[8:]], axis=1)
            tile = tile[:8, :LANES]
            total = tile if total is None else total + tile
        small_ref[f] = total
    lang = language_rows(groups_ref, small_ref, rows)

    def inputs():
        return jnp.concatenate(
            [tok_ref[m * tokens : (m + 1) * tokens].astype(F32) + lang[m] for m in range(rows)], axis=0
        )

    def w_qkv(b, j):
        w = wkv_ref[b, j - 1] if j else pack_ref[b, 0, :, :, :r]
        return w.reshape(D, cols)

    a = inputs().astype(BF)

    def project(j, bias):
        out = jnp.concatenate([mm(a, w_qkv(b, j)) for b in range(n_b)], axis=1)
        if bias is not None:
            out = out + small_piece(small_ref, bias, 4)
        return [t.astype(BF) for t in rows_to_heads(out[:tokens], out[tokens:])]

    for h, t in enumerate(project(0, ROW_BQ)):
        qsend_ref[h] = t
    q_ref[place.h] = qsend_ref[place.h]
    def to_heads(src, dst):
        return [
            wire.send(lambda k=k: (src.at[place.head_ahead(k)], dst.at[place.h], place.across_heads(k)))
            for k in outwards(H)
        ]

    moved_q = to_heads(qsend_ref, q_ref)
    kv_w.to_cores()
    first.to_plane()
    out_w.to_plane()
    kv_w.finish()
    for j, bias in ((0, None), (1, ROW_BV)):
        for h, t in enumerate(project(1 + j, bias)):
            kvsend_ref[h, j] = t
    kv_ref[place.s] = kvsend_ref[place.h]
    kv_sems = wire.reserve(H)
    share_sems = wire.reserve(H * (parts - 1))

    def moved_kv(i):
        k = far_first(i)
        return wire.make(
            kv_sems + i, kvsend_ref.at[place.head_ahead(k)], kv_ref.at[place.s], place.across_heads(k)
        )

    def ordered(i):
        return far_first(i) if isinstance(i, int) else jnp.where(i == 0, 0, far_first(i))

    def shared_kv(i, j):
        slot = kv_ref.at[place.head_behind(ordered(i)) * parts + place.g]
        return wire.make(share_sems + i * (parts - 1) + j - 1, slot, slot, place.across_parts(j))

    for j in range(1, parts):
        shared_kv(0, j).start()
    for k in range(1, H):
        moved_kv(k).start()
    second.to_plane()

    def masked_rows(src_ref, dst_ref):
        for g in range(groups):
            both = src_ref[g * GROUP : (g + 1) * GROUP].reshape(width, LANES)
            zero = jnp.zeros_like(both)
            dst_ref[0, g] = jnp.where(low, both, zero)
            dst_ref[1, g] = jnp.where(low, zero, both)

    received(moved_q)
    masked_rows(q_ref, qm_ref)

    def pair(h):
        kv = kv_ref[pl.ds(h * parts, parts)]
        return kv[:, 0].reshape(keys, LANES), kv[:, 1].reshape(keys, LANES)

    def key_ids(h, m):
        ids = idk_ref[m, pl.ds(pl.multiple_of(h * keys, keys), keys), :]
        return jnp.concatenate([ids] * (width // LANES), axis=1)

    def attend(k):
        h = place.head_behind(ordered(k))
        ids = [key_ids(h, m) for m in range(rows)]
        for j in range(1, parts):
            shared_kv(k, j).wait_recv()
        key, value = pair(h)
        value_t = value.T
        ones = jnp.ones((16, keys), BF)
        for g in range(groups):
            for m in range(rows):
                i = g * rows + m
                s = jnp.where(ids[m] == idq_ref[m, g], mm_nt(key, qm_ref[m, g]) * scale2, NEG)
                new = jnp.maximum(peak_ref[i], jnp.max(s, axis=0, keepdims=True))
                p = jnp.exp2(s - new).astype(BF)
                alpha = jnp.exp2(peak_ref[i] - new)
                left = jnp.concatenate([value_t[m * HD : (m + 1) * HD], ones], axis=0)
                acc_ref[i] = acc_ref[i] * alpha + mm(left, p)
                peak_ref[i] = new

    def meanwhile(k, *stages):
        for at, stage in stages:
            pl.when(k == at)(stage)

    def forward_step(k, carry):
        moved_kv(k).wait_recv()
        for j in range(1, parts):
            shared_kv(k, j).start()
        attend(k - 1)
        meanwhile(
            k,
            (2, first.to_diagonal),
            (2, out_w.to_diagonal),
            (6, second.to_diagonal),
        )
        return carry

    lax.fori_loop(1, H, forward_step, 0)
    attend(H - 1)
    for g in range(groups):
        for m in range(rows):
            i = g * rows + m
            total = acc_ref[i, HD : HD + 1]
            ot_ref[g, m * HD : (m + 1) * HD] = acc_ref[i, :HD] * (1.0 / total)
            lse_ref[i] = peak_ref[i] + jnp.log2(total)
        o_ref[g * GROUP : (g + 1) * GROUP] = ot_ref[g].T.astype(BF).reshape(GROUP, tokens, LANES)
    moved = to_heads(o_ref, otile_ref)
    otile_ref[place.h] = o_ref[place.h]
    for piece in (out_w, first, second):
        piece.to_cores()

    tiles, wide = act_ref.shape[0], act_ref.shape[2]
    per_b = cols_f // wide
    bias_1 = [small_piece(small_ref, ROW_B1 + i * wide // LANES, wide // LANES) for i in range(tiles)]
    gain1, shift1 = small_piece(small_ref, ROW_G1, 4), small_piece(small_ref, ROW_S1, 4)
    gain2, shift2 = small_piece(small_ref, ROW_G2, 4), small_piece(small_ref, ROW_S2, 4)
    bias_o, bias_2 = small_piece(small_ref, ROW_BO, 4), small_piece(small_ref, ROW_B2, 4)

    def block(ref, i):
        at = i % per_b * wide
        return ref[i // per_b, 0, :, :, :, at : at + wide].reshape(D, wide)

    live = jnp.concatenate(
        [idk_ref[m, pl.ds(pl.multiple_of(place.s * tokens, tokens), tokens), :] for m in range(rows)], axis=0
    )
    live = jnp.where(live < SEGS, 1.0, 0.0)
    u = inputs()
    out_w.finish()
    first.finish()
    received(moved)
    mixed = jnp.concatenate(heads_to_rows([otile_ref[h].astype(F32) for h in range(H)]), axis=0).astype(BF)
    attn_out = jnp.concatenate([mm(mixed, wo_ref[b, 0].reshape(D, cols)) for b in range(n_b)], axis=1)
    normed1, inverse1 = normed_of(u + (attn_out + bias_o))
    hidden = normed1 * gain1 + shift1
    hb = hidden.astype(BF)
    for i in range(tiles):
        act, slope = gelu_pair(mm(hb, block(w1_ref, i)) + bias_1[i])
        slope_ref[i] = slope
        act_ref[i] = act.astype(BF)
    second.finish()
    total = hidden + u + bias_2
    for i in range(tiles):
        total = total + mm_nt(act_ref[i], block(w2_ref, i))

    normed2, inverse2 = normed_of(total)
    out_ref[...] = (normed2 * gain2 + shift2).astype(BF)
    c = cot_ref[...].astype(F32) * jnp.concatenate([live] * (D // LANES), axis=1)
    dr = norm_back(c * gain2, normed2, inverse2)
    df = dr.astype(BF)

    def scatter(part):
        return Scatter(place, wire, part, *take(SCATTER_SCRATCH))

    g_first, g_second, g_out = scatter(dw1_ref), scatter(dw2_ref), scatter(dwo_ref)
    g_kv = scatter(dkv_w_ref)
    g_q = ShortScatter(place, wire, dq_w_ref, *take(SHORT_SCRATCH))
    g_small = ShortScatter(place, wire, dsmall_ref, *take(SHORT_SCRATCH))

    def weight_grad(left, right_ref, dst_ref):
        left = left.T
        for i in range(tiles):
            at = i % per_b * wide
            grad = mm(left, right_ref[i]).astype(BF).reshape(n_z, 2, 2, r, wide)
            dst_ref[i // per_b, 0, :, :, :, :, at : at + wide] = grad

    weight_grad(df, act_ref, dw2_ref)
    g_second.to_core()
    dh = dr
    for i in range(tiles):
        dz = (mm(df, block(w2_ref, i)) * slope_ref[i]).astype(BF)
        dz_ref[i] = dz
        dh = dh + mm_nt(dz, block(w1_ref, i))
    dpre = norm_back(dh * gain1, normed1, inverse1)
    dattn = dpre.astype(BF)
    do = mm_nt(dattn[:, :cols], wo_ref[0, 0].reshape(D, cols))
    for b in range(1, n_b):
        do = do + mm_nt(dattn[:, b * cols : (b + 1) * cols], wo_ref[b, 0].reshape(D, cols))
    for h, t in enumerate(rows_to_heads(do[:tokens], do[tokens:])):
        dotile_ref[h] = t.astype(BF)
    moved = to_heads(dotile_ref, do_ref)
    written[0].start()
    do_ref[place.h] = dotile_ref[place.h]
    sum_ref[...] = dpre + dr

    g_second.to_diagonal()
    weight_grad(hb, dz_ref, dw1_ref)
    g_first.to_core()
    mixed_t = mixed.T
    for b in range(n_b):
        dwo = mm(mixed_t, dattn[:, b * cols : (b + 1) * cols]).astype(BF)
        dwo_ref[b, 0] = dwo.reshape(n_z, 2, 2, r, cols)
    g_out.to_core()
    for k in range(H):
        for j in range(1, parts):
            shared_kv(k, j).wait_send()
        if k:
            moved_kv(k).wait_send()
    wire.drain()

    g_first.to_diagonal()
    g_out.to_diagonal()
    add_small(frames_ref, ROW_G2, column_sum(c * normed2))
    add_small(frames_ref, ROW_S2, column_sum(c))
    add_small(frames_ref, ROW_B2, column_sum(df.astype(F32)))
    for i in range(tiles):
        add_small(frames_ref, ROW_B1 + i * wide // LANES, column_sum(dz_ref[i].astype(F32)))
    add_small(frames_ref, ROW_G1, column_sum(dh * normed1))
    add_small(frames_ref, ROW_S1, column_sum(dh))
    add_small(frames_ref, ROW_BO, column_sum(dattn.astype(F32)))
    received(moved)
    masked_rows(do_ref, dom_ref)
    g_second.to_plane()
    for g in range(groups):
        product = do_ref[g * GROUP : (g + 1) * GROUP].reshape(width, LANES).astype(F32).T * ot_ref[g]
        for m in range(rows):
            delta_ref[g * rows + m] = column_sum(product[m * HD : (m + 1) * HD])

    near_sems = wire.reserve(H * (parts - 1))
    back_sems = wire.reserve(H)

    def target(k):
        far = far_first(k) if isinstance(k, int) else jnp.where(k == H, H, far_first(k))
        return place.head_ahead(far)

    def near_kv(k, j):
        h = target(k)
        return wire.make(
            near_sems + (k - 1) * (parts - 1) + j - 1,
            part_ref.at[h, place.part_ahead(j)],
            near_ref.at[j - 1, h],
            place.across_parts(j),
        )

    def back_kv(k):
        h = target(k)
        return wire.make(back_sems + k - 1, dkv_sum.at[h], dkv_back.at[place.h], (h * parts + place.g, place.b))

    def fold(k):
        h = target(k)
        total = part_ref[h, place.g].astype(F32)
        for j in range(1, parts):
            near_kv(k, j).wait_recv()
            total = total + near_ref[j - 1, h].astype(F32)
        return total.astype(BF)

    def key_step(k):
        h = target(k)
        key, value = pair(h)
        key_t = key.T
        ids = [key_ids(h, m) for m in range(rows)]
        dk = jnp.zeros((keys, LANES), F32)
        dv = jnp.zeros((keys, LANES), F32)
        for g in range(groups):
            for m in range(rows):
                i = g * rows + m
                p = jnp.exp2(mm_nt(key, qm_ref[m, g]) * scale2 - lse_ref[i])
                p = jnp.where(ids[m] == idq_ref[m, g], p, 0.0)
                ds = (p * (mm_nt(value, dom_ref[m, g]) - delta_ref[i])).astype(BF)
                dv = dv + mm(p.astype(BF), dom_ref[m, g])
                dk = dk + mm(ds, qm_ref[m, g])
                dqt_ref[g, m * HD : (m + 1) * HD] += mm(key_t[m * HD : (m + 1) * HD], ds)
        part_ref[h, :, 0] = (dk * SCALE).astype(BF).reshape(parts, tokens, LANES)
        part_ref[h, :, 1] = dv.astype(BF).reshape(parts, tokens, LANES)
        for j in range(1, parts):
            near_kv(k, j).start()

    def backward_step(k, carry):
        key_step(k)
        dkv_sum[target(k - 1)] = fold(k - 1)
        back_kv(k - 1).start()
        meanwhile(
            k,
            (6, g_first.to_plane),
            (6, g_out.to_plane),
        )
        return carry

    token_pieces = (g_second, g_first, g_out)
    key_step(1)
    lax.fori_loop(2, H + 1, backward_step, 0)
    for g in range(groups):
        dq_ref[g * GROUP : (g + 1) * GROUP] = (dqt_ref[g] * SCALE).T.astype(BF).reshape(GROUP, tokens, LANES)
    moved = to_heads(dq_ref, dq_back)
    dq_back[place.h] = dq_ref[place.h]
    dkv_back[place.h] = fold(H)
    g_second.to_owner()

    def to_rows(parts_of):
        return jnp.concatenate(heads_to_rows([t.astype(F32) for t in parts_of]), axis=0).astype(BF)

    def grad_of(left, right, b):
        return mm(left, right[:, b * cols : (b + 1) * cols]).astype(BF).reshape(n_z, 2, 2, r, cols)

    def back_through(total, right, j):
        for b in range(n_b):
            total = total + mm_nt(right[:, b * cols : (b + 1) * cols], w_qkv(b, j))
        return total

    for k in range(1, H):
        back_kv(k).wait_recv()
    a_t = inputs().astype(BF).T
    dk = to_rows([dkv_back[h, 0] for h in range(H)])
    dv = to_rows([dkv_back[h, 1] for h in range(H)])
    for b in range(n_b):
        dkv_w_ref[b, 0] = grad_of(a_t, dk, b)
        dkv_w_ref[b, 1] = grad_of(a_t, dv, b)
    g_kv.to_core()
    add_small(frames_ref, ROW_BV, column_sum(dv.astype(F32)))
    du = back_through(back_through(sum_ref[...], dk, 1), dv, 2)
    g_kv.to_diagonal()
    g_first.to_owner()
    g_out.to_owner()
    received(moved)
    dq = to_rows([dq_back[h] for h in range(H)])
    for b in range(n_b):
        dq_w_ref[b, 0] = grad_of(a_t, dq, b)
    g_q.to_core()
    du = back_through(du, dq, 0)
    add_small(frames_ref, ROW_BQ, column_sum(dq.astype(F32)))
    sums = [column_sum(du[m * tokens : (m + 1) * tokens]) for m in range(rows)]
    for e in range(GROUPS):
        total = jnp.zeros_like(sums[0])
        for m in range(rows):
            total = total + jnp.where(groups_ref[m] == e, sums[m], 0.0)
        add_small(frames_ref, ROW_E + 4 * e, total)
    for s in range(place.n_s):
        for b in range(n_b):
            dsmall_ref[b, 0, s // 4, s // 2 % 2, s % 2] = frames_ref[(s * n_b + b) // frame]
    g_small.to_core()
    g_q.to_plane()
    g_kv.to_plane()
    g_small.to_plane()
    du_ref[...] = du.astype(BF)
    written[1].start()
    g_kv.to_owner()

    weights = [attn_ref.at[j] for j in range(4)] + [ffn_ref.at[j] for j in range(2)]
    outs = [agrad_ref.at[j] for j in range(4)] + [fgrad_ref.at[j] for j in range(2)]
    updates = [update_a.at[j] for j in range(4)] + [update_f.at[j] for j in range(2)]
    old_cols = [acols_ref[j : j + 1] for j in range(4)] + [fcols_ref[j : j + 1] for j in range(2)]
    owners = [(g_q, 0), (g_kv, 0), (g_kv, 1), (g_out, 0), (g_first, 0), (g_second, 0)]
    spans = [cols] * 4 + [cols_f] * 2
    places, used = [], 0
    for span in spans:
        places.append(used)
        used += -(-span // LANES)
    pad = cols_plane.shape[1]
    late = 3
    mine = cols_plane.at[place.xc]
    mine_rows = rows_plane.at[place.b, place.xc]
    mine_late = late_cols.at[place.s]
    mine_late_rows = late_rows.at[place.b]
    mine_sums = late_sums.at[place.b, place.s]
    mine[...] = jnp.zeros((pad, LANES), F32)
    mine_late[...] = jnp.zeros((8, LANES), F32)
    lane = lax.broadcasted_iota(jnp.int32, (r, LANES), 1)
    square_sums = [None] * SLABS
    old_rows = jnp.concatenate([arows_ref[...], frows_ref[...], jnp.zeros((2, r), F32)], axis=0).T
    old_rows = [old_rows[:, j : j + 1] for j in range(SLABS)]
    row_sums_old = [sum_all(x) for x in old_rows]
    weight_squares = [sum_all(w[...] * w[...]) for w in weights]
    own = own_ref[...]
    entry = lax.broadcasted_iota(jnp.int32, (8, LANES), 0) * LANES + lax.broadcasted_iota(jnp.int32, (8, LANES), 1)
    own_mask = jnp.where((entry >= own_at) & (entry < own_at + chunk), 1.0, 0.0)
    weight_squares.append(sum_all(own * own))
    rows_tiles = []

    def gradient(j):
        owner, slab = owners[j]
        grad = owner.total(slab)
        outs[j][...] = grad
        square = grad * grad + EPS_ONE
        row_sum = jnp.sum(square, axis=1, keepdims=True)
        col_sum = column_sum(square)
        ref = mine_late if j < late else mine
        for k in range(0, spans[j], LANES):
            span = min(LANES, spans[j] - k)
            ref[pl.ds(places[j] + k // LANES, 1), pl.ds(0, span)] = col_sum[:, k : k + span]
        square_sums[j] = sum_all(row_sum)
        return jnp.where(lane == j, row_sum, 0.0)

    def renewed(j, row_total, sums, square_total, old_total):
        length = D if j < 4 else FF
        new_rows = DECAY * old_rows[j] + (1.0 - DECAY) * row_total[:, j : j + 1] * (1.0 / length)
        rows_tiles.append(jnp.where(lane == j, new_rows, 0.0))
        mean_rows = (DECAY / n_b * old_total + (1.0 - DECAY) * (1.0 / length) * square_total) * (1.0 / D)
        pieces = [
            sums[places[j] + k // LANES : places[j] + k // LANES + 1, : min(LANES, spans[j] - k)]
            for k in range(0, spans[j], LANES)
        ]
        col_sum = pieces[0] if len(pieces) == 1 else jnp.concatenate(pieces, axis=1)
        new = DECAY * old_cols[j] + (1.0 - DECAY) * (1.0 / D) * col_sum
        if j < 4:
            acols_new_ref[j : j + 1, :] = new
        else:
            fcols_new_ref[j - 4 : j - 3, :] = new
        update = outs[j][...] * lax.rsqrt((new_rows / mean_rows) * new)
        updates[j][...] = update
        return sum_all(update * update)

    def pick(tile, j):
        return tile[0:1, j : j + 1]

    def fan(i, ref, offsets):
        for db in offsets:
            b = place.batch_ahead(db)

            def one(k, carry=0, b=b):
                wire.make(i, ref, ref, (wrap(place.s + k, place.n_s), b)).start()
                return carry

            if place.n_s > 16:
                lax.fori_loop(0 if db else 1, place.n_s, one, 0)
            else:
                for k in outwards(place.n_s) + [0] * (db > 0):
                    one(k)

    near, others = [0], list(range(1, n_b))
    one_peer = place.along_z(1)

    for piece in token_pieces:
        piece.finish()
    mine_rows[pl.ds(0, r), :] = gradient(5) + gradient(4) + gradient(3)
    tail = pl.ds(r, 8)
    mine_rows[tail, :] = lanes_of(square_sums + row_sums_old + weight_squares)
    moved = []
    for dx, db in plane:
        peer = plane_peer(dx, db)
        if db == 0:
            moved.append(wire.send(lambda peer=peer: (mine, mine, peer)))
        if dx == 0:
            moved.append(wire.send(lambda peer=peer: (mine_rows, mine_rows, peer)))
        else:
            moved.append(wire.send(lambda peer=peer: (mine_rows.at[tail], mine_rows.at[tail], peer)))
    g_q.to_owner()
    g_small.to_owner()
    g_kv.finish()
    row_tile = gradient(1) + gradient(2)
    received(moved)
    mine_z = all_z.at[place.z]
    mine_z[pl.ds(0, pad), :] = cols_plane[0] + cols_plane[1] + cols_plane[2] + cols_plane[3]
    scalars = jnp.zeros((8, LANES), F32)
    row_total = jnp.zeros((r, LANES), F32)
    for b in range(n_b):
        for xc in range(4):
            scalars = scalars + rows_plane[b, xc, tail, :]
        row_total = row_total + rows_plane[b, place.xc, pl.ds(0, r), :]
    mine_z[pl.ds(pad, 8), :] = scalars
    moved = [wire.send(lambda peer=peer: (mine_z, mine_z, peer)) for peer in along]

    g_q.finish()
    mine_late_rows[...] = row_tile + gradient(0)
    written[2].start()
    written[3].start()
    sums = lanes_of(square_sums[:late])[0:1]
    mine_late[7:8, :] = sums
    late_sums[place.b] = jnp.zeros((place.n_s, 1, LANES), F32)
    mine_sums[...] = sums
    late_i, sums_i, all_i = wire.reserve(1), wire.reserve(1), wire.reserve(1)
    moved_rows = [
        wire.send(lambda k=k: (mine_late_rows, mine_late_rows, place.across_batch(k))) for k in range(1, n_b)
    ]
    fan(late_i, mine_late, near)
    fan(sums_i, mine_sums, others)

    received(moved)
    reduced = all_z[0]
    for z in range(1, n_z):
        reduced = reduced + all_z[z]
    tile = reduced[pad:]

    def scalar(j):
        return pick(tile, j)

    update_squares = [None] * SLABS
    for j in range(late, SLABS):
        update_squares[j] = renewed(j, row_total, reduced, scalar(j), scalar(SLABS + j))
    g_small.finish()
    own_grad = g_small.total(0) * own_mask
    own_sq = DECAY * to_frame(sq_ref[...].reshape(1, chunk), own_at) + (1.0 - DECAY) * (own_grad * own_grad + EPS_ONE)
    own_update = own_grad * lax.rsqrt(own_sq)
    update_squares.append(sum_all(own_update * own_update))
    for k in range(1, H + 1):
        for j in range(1, parts):
            near_kv(k, j).wait_send()
        if k < H:
            back_kv(k).wait_send()
    wire.drain()

    late_part = late_cols.at[pl.ds(0, place.n_s - 1)]
    sums_part = late_sums.at[pl.ds(0, n_b - 1)]
    wire.make(late_i, late_part, late_part, one_peer).wait_recv()
    wire.make(sums_i, sums_part, sums_part, one_peer).wait_recv()
    received(moved_rows)
    sums = late_cols[0]
    for s in range(1, place.n_s):
        sums = sums + late_cols[s]
    totals = jnp.zeros((1, LANES), F32)
    row_total = jnp.zeros((r, LANES), F32)
    for b in range(n_b):
        other = late_sums[b, 0]
        for s in range(1, place.n_s):
            other = other + late_sums[b, s]
        totals = totals + jnp.where(place.b == b, sums[7:8], other)
        row_total = row_total + late_rows[b]
    for j in range(late):
        update_squares[j] = renewed(j, row_total, sums, pick(totals, j), scalar(SLABS + j))
    written[4].start()
    written[5].start()
    rows_new_ref[...] = sum(rows_tiles[1:], rows_tiles[0])
    mine_u = all_sums.at[place.b * place.n_s + place.s]
    mine_u[...] = lanes_of(update_squares)[0:1]
    fan(all_i, mine_u, near + others)
    wire.make(late_i, late_part, late_part, one_peer).wait_send()
    wire.make(sums_i, sums_part, sums_part, one_peer).wait_send()
    all_part = all_sums.at[pl.ds(0, place.n_s * n_b - 1)]
    copy = wire.make(all_i, all_part, all_part, one_peer)
    copy.wait_send()
    copy.wait_recv()
    update_tile = jnp.zeros((1, LANES), F32)
    for i in range(place.n_s * n_b):
        update_tile = update_tile + all_sums[i]
    sizes = [D * D] * 4 + [D * FF] * 2 + [NVEC]

    def scale(j):
        weight = jnp.sqrt(scalar(2 * SLABS + j) * (1.0 / sizes[j]))
        return LEARN * weight / jnp.maximum(1.0, jnp.sqrt(update_tile[0:1, j : j + 1] * (1.0 / sizes[j])))

    scales_ref[...] = lanes_of([scale(j) for j in range(SLABS)])
    own_new_ref[0] = own_grad
    own_new_ref[1] = own - scale(SLABS) * own_update
    own_new_ref[2] = own_sq
    for copy in written:
        copy.wait()
    wire.drain()


def layer_part(groups, lengths, tok, cot, attn, ffn, params, arows, acols, frows, fcols, sq):
    n_s, n_b = lax.axis_size("seq"), lax.axis_size("batch")
    n_z, parts = n_s // 4, n_s // H
    count = tok.shape[0]
    tokens = count // 2
    rows = 2
    _, r, cols = attn.shape
    cols_f = ffn.shape[2]
    groups_q = H // GROUP
    width = GROUP * tokens
    length = tokens * n_s
    wide = min(512, cols_f)
    tiles = FF // wide
    pad = 4 * -(-cols // LANES) + 2 * (cols_f // LANES)
    pad = -(-pad // 8) * 8
    gather = (n_z - 1) + (1 + n_b) + 2 * (n_b - 1) + 1 + (n_b - 1) + 2 * (n_b - 1)
    copies = 5 * gather + 7 * (H - 1) + 2 * H + 2 * H * (parts - 1)
    copies += 6 * (1 + 2 * (n_b - 1) + n_b + n_z - 1)
    copies += 6 + 4 * n_b + (n_z - 1) + (n_b - 1) + 3

    def shape(dims, kind):
        return jax.ShapeDtypeStruct(dims, kind)

    out = (
        shape(tok.shape, BF),
        shape(tok.shape, BF),
        shape(attn.shape, F32),
        shape(ffn.shape, F32),
        shape(attn.shape, F32),
        shape(ffn.shape, F32),
        shape((8, LANES), F32),
        shape((r, LANES), F32),
        shape(acols.shape, F32),
        shape(fcols.shape, F32),
        shape((3, 8, LANES), F32),
    )
    vmem = pltpu.VMEM
    heads = (H, tokens, LANES)
    scratch = [
        vmem((1, r + 16, cols), BF),
        vmem((2, r, cols), BF),
        vmem((1, r, cols), BF),
        vmem(ffn.shape, BF),
        vmem((8, LANES), F32),
        vmem((FRAMES, 8, LANES), F32),
        vmem((n_b, 1, n_z, 4, r + 16, cols), BF),
        vmem((n_b, 2, n_z, 4, r, cols), BF),
        vmem((n_b, 1, n_z, 4, r, cols), BF),
        vmem((n_b, 1, n_z, 4, r, cols_f), BF),
        vmem((n_b, 1, n_z, 4, r, cols_f), BF),
        vmem((rows, length, LANES), F32),
        vmem((rows, groups_q, 1, width), F32),
        vmem(heads, BF),
        vmem((n_s, 2, tokens, LANES), BF),
        vmem(heads, BF),
        vmem((H, 2, tokens, LANES), BF),
        vmem((rows, groups_q, width, LANES), BF),
        vmem((rows, groups_q, width, LANES), BF),
        vmem((rows * groups_q, 1, width), F32),
        vmem((rows * groups_q, HD + 16, width), F32),
        vmem((groups_q, LANES, width), F32),
        vmem((rows * groups_q, 1, width), F32),
        vmem((rows * groups_q, 1, width), F32),
        vmem(heads, BF),
        vmem(heads, BF),
        vmem(heads, BF),
        vmem(heads, BF),
        vmem((tiles, count, wide), BF),
        vmem((tiles, count, wide), F32),
        vmem((tiles, count, wide), BF),
        vmem((count, D), F32),
        vmem((FRAMES, 8, LANES), F32),
        vmem((groups_q, LANES, width), F32),
        vmem((H, parts, 2, tokens, LANES), BF),
        vmem((parts - 1, H, 2, tokens, LANES), BF),
        vmem((H, 2, tokens, LANES), BF),
        vmem(heads, BF),
        vmem(heads, BF),
        vmem((H, 2, tokens, LANES), BF),
        vmem((n_b, 1, n_z, 2, 2, r, cols), BF),
        vmem((n_b, 1, n_z, 2, 2, r, cols_f), BF),
        vmem((n_b, 1, n_z, 2, 2, r, cols_f), BF),
        vmem((n_b, 2, n_z, 2, 2, r, cols), BF),
        vmem((n_b, 1, n_z, 2, 2, r, cols), BF),
        vmem((n_b, 1, n_z, 2, 2, 8, LANES), F32),
        vmem((4, pad, LANES), F32),
        vmem((n_b, 4, r + 8, LANES), F32),
        vmem((n_z, pad + 8, LANES), F32),
        vmem((n_s, 8, LANES), F32),
        vmem((n_b, r, LANES), F32),
        vmem((n_b, n_s, 1, LANES), F32),
        vmem((n_b * n_s, 1, LANES), F32),
        vmem(tok.shape, BF),
        vmem(tok.shape, BF),
        vmem(attn.shape, F32),
        vmem(ffn.shape, F32),
        vmem(attn.shape, F32),
        vmem(ffn.shape, F32),
    ]
    scratch += scatter_scratch(n_b, 1, n_z, r, cols_f, BF) * 2
    scratch += scatter_scratch(n_b, 1, n_z, r, cols, BF)
    scratch += scatter_scratch(n_b, 2, n_z, r, cols, BF)
    scratch += short_scratch(n_b, 1, n_z, r, cols, BF)
    scratch += short_scratch(n_b, 1, n_z, 8, LANES, F32)
    dma = pltpu.SemaphoreType.DMA
    scratch += [dma((copies,)), dma((copies,)), dma((11,))]
    return pl.pallas_call(
        layer_kernel,
        out_shape=out,
        in_specs=[SMEM_SPEC] + [VMEM_SPEC] * 11,
        out_specs=(pl.BlockSpec(memory_space=pl.ANY),) * 6 + (VMEM_SPEC,) * 5,
        scratch_shapes=scratch,
        compiler_params=pltpu.CompilerParams(
            vmem_limit_bytes=63 * 2**20, collective_id=0, has_side_effects=True
        ),
    )(groups, lengths, tok, cot, attn, ffn, params, arows, acols, frows, fcols, sq)


def result_kernel(
    out_in, du_in, agrad_in, fgrad_in, update_a, update_f, scales_ref, rows_ref, acols_in, fcols_in, own_ref,
    attn_ref, ffn_ref,
    out_ref, du_ref, agrad_ref, fgrad_ref, grad_ref, anew_ref, fnew_ref, new_ref, acopy_ref, fcopy_ref, copy_ref,
    arows_ref, acols_ref, frows_ref, fcols_ref, sq_ref,
    sems,
):
    pairs = ((out_in, out_ref), (du_in, du_ref), (agrad_in, agrad_ref), (fgrad_in, fgrad_ref))
    copies = [pltpu.make_async_copy(src, dst, sems.at[i]) for i, (src, dst) in enumerate(pairs)]
    for copy in copies:
        copy.start()
    for j in range(4):
        new = attn_ref[j] - scales_ref[0:1, j : j + 1] * update_a[j]
        anew_ref[j] = new
        acopy_ref[j] = new.astype(BF)
    for j in range(2):
        new = ffn_ref[j] - scales_ref[0:1, 4 + j : 5 + j] * update_f[j]
        fnew_ref[j] = new
        fcopy_ref[j] = new.astype(BF)
    rows = rows_ref[...].T
    arows_ref[...] = rows[0:4]
    frows_ref[...] = rows[4:6]
    acols_ref[...] = acols_in[...]
    fcols_ref[...] = fcols_in[...]
    chunk = grad_ref.shape[0]
    at = own_place(chunk)
    grad_ref[...] = from_frame(own_ref[0], at, chunk).reshape(chunk)
    new = from_frame(own_ref[1], at, chunk)
    new_ref[...] = new.reshape(chunk)
    copy_ref[...] = new.astype(BF).reshape(chunk)
    sq_ref[...] = from_frame(own_ref[2], at, chunk).reshape(chunk)
    for copy in copies:
        copy.wait()


def result_part(made, attn, ffn, chunk):
    out, _, agrad, fgrad, _, _, _, rows, acols, fcols, _ = made
    r = rows.shape[0]

    def shape(dims, kind):
        return jax.ShapeDtypeStruct(dims, kind)

    shapes = (
        shape(out.shape, BF),
        shape(out.shape, BF),
        shape(attn.shape, F32),
        shape(ffn.shape, F32),
        shape((chunk,), F32),
        shape(attn.shape, F32),
        shape(ffn.shape, F32),
        shape((chunk,), F32),
        shape(attn.shape, BF),
        shape(ffn.shape, BF),
        shape((chunk,), BF),
        shape((4, r), F32),
        shape(acols.shape, F32),
        shape((2, r), F32),
        shape(fcols.shape, F32),
        shape((chunk,), F32),
    )
    return pl.pallas_call(
        result_kernel,
        out_shape=shapes,
        in_specs=[VMEM_SPEC] * 13,
        out_specs=(pl.BlockSpec(memory_space=pl.ANY),) * 4 + (VMEM_SPEC,) * 12,
        scratch_shapes=[pltpu.SemaphoreType.DMA((4,))],
        compiler_params=pltpu.CompilerParams(vmem_limit_bytes=60 * 2**20),
    )(*made, attn, ffn)


def shards(
    tokens, lengths, groups, cotangent, attn_weights, ffn_weights, small_params,
    attn_rows, attn_cols, ffn_rows, ffn_cols, small_sq,
):
    micro, rb, toks, _ = tokens.shape
    rows = micro * rb
    chunk = small_params.shape[0]
    made = layer_part(
        groups.reshape(rows),
        lengths.reshape(rows, SEGS),
        tokens.reshape(rows * toks, D),
        cotangent.reshape(rows * toks, D),
        attn_weights,
        ffn_weights,
        small_params,
        attn_rows,
        attn_cols,
        ffn_rows,
        ffn_cols,
        small_sq,
    )
    results = list(result_part(made, attn_weights, ffn_weights, chunk))
    for i in (0, 1):
        results[i] = results[i].reshape(tokens.shape)
    return tuple(results)


def solution(mesh):
    acts = P(None, "batch", "seq", None)
    weights = P(None, "seq", "batch")
    small = P(("seq", "batch"))
    rows, cols = P(None, "seq"), P(None, "batch")
    return jax.shard_map(
        shards,
        mesh=mesh,
        in_specs=(acts, P(None, "batch", None), P(None, "batch"), acts, weights, weights, small)
        + (rows, cols, rows, cols, small),
        out_specs=(acts, acts, weights, weights, small, weights, weights, small, weights, weights, small)
        + (rows, cols, rows, cols, small),
        check_vma=False,
    )
```

```python
import functools

import jax
import jax.numpy as jnp
from jax import lax
from jax.experimental import pallas as pl
from jax.experimental.pallas import tpu as pltpu
from jax.sharding import PartitionSpec as P

D = 512
H = 8
HD = 64
FF = 2048
GROUPS = 8
SEGS = 64
STEP = 10
NVEC = 10240
LANES = 128

NEG = -1e30
EPS = 1e-05
EPS_ONE = 1e-30
LEARN = 1.0
DECAY = 1.0 - STEP ** (-0.8)
SCALE = HD ** (-0.5)
LOG2E = 1.4426950408889634
FRAMES = 16
FRAME_ROWS = NVEC // FRAMES // LANES
GROUP = 4
BF = jnp.bfloat16
F32 = jnp.float32
VMEM_SPEC = pl.BlockSpec(memory_space=pltpu.VMEM)
SMEM_SPEC = pl.BlockSpec(memory_space=pltpu.SMEM)

ROW_BQ, ROW_BV, ROW_BO, ROW_B1, ROW_B2 = 0, 4, 8, 12, 28
ROW_G1, ROW_S1, ROW_G2, ROW_S2, ROW_E = 32, 36, 40, 44, 48


def mm(a, b):
    return lax.dot_general(a, b, (((1,), (0,)), ((), ())), preferred_element_type=F32)


def mm_nt(a, b):
    return lax.dot_general(a, b, (((1,), (1,)), ((), ())), preferred_element_type=F32)


def mm_tn(a, b):
    return lax.dot_general(a, b, (((0,), (0,)), ((), ())), preferred_element_type=F32)


def small_piece(small_ref, row, count):
    parts = [small_ref[r // FRAME_ROWS, pl.ds(r % FRAME_ROWS, 1), :] for r in range(row, row + count)]
    return jnp.concatenate(parts, axis=1)


def add_small(ref, row, values):
    for k in range(values.shape[1] // LANES):
        r = row + k
        ref[r // FRAME_ROWS, pl.ds(r % FRAME_ROWS, 1), :] += values[:, k * LANES : (k + 1) * LANES]


def low_half():
    return lax.broadcasted_iota(jnp.int32, (1, LANES), 1) < HD


def swap_halves(x):
    return pltpu.roll(x, HD, 1)


def heads_to_rows(tiles):
    low = low_half()
    first, second = [], []
    for j in range(H // 2):
        a, b = tiles[2 * j], tiles[2 * j + 1]
        first.append(jnp.where(low, a, swap_halves(b)))
        second.append(jnp.where(low, swap_halves(a), b))
    return jnp.concatenate(first, axis=1), jnp.concatenate(second, axis=1)


def rows_to_heads(first, second):
    low = low_half()
    tiles = []
    for j in range(H // 2):
        a = first[:, j * LANES : (j + 1) * LANES]
        b = second[:, j * LANES : (j + 1) * LANES]
        tiles.append(jnp.where(low, a, swap_halves(b)))
        tiles.append(jnp.where(low, swap_halves(a), b))
    return tiles


def wrap(value, count):
    return value - jnp.where(value >= count, count, 0)


def outwards(count):
    return sorted(range(1, count), key=lambda k: (abs(2 * k - count), k))


class Place:
    def __init__(self):
        self.n_s, self.n_b = lax.axis_size("seq"), lax.axis_size("batch")
        self.s, self.b = lax.axis_index("seq"), lax.axis_index("batch")
        self.n_z, self.parts = self.n_s // 4, self.n_s // H
        self.z, self.xc = self.s // 4, self.s % 4
        self.x, self.c = self.xc // 2, self.xc % 2
        self.other_x = (1 - self.x) * 2 + self.c
        self.other_c = self.x * 2 + 1 - self.c
        self.h, self.g = self.s // self.parts, self.s % self.parts
        self.z_ahead = [wrap(self.z + k, self.n_z) for k in range(self.n_z)]
        self.b_ahead = [wrap(self.b + k, self.n_b) for k in range(self.n_b)]
        self.xc_ahead = [wrap(self.xc + k, 4) for k in range(4)]
        self.h_ahead = [wrap(self.h + k, H) for k in range(H)]
        self.g_ahead = [wrap(self.g + k, self.parts) for k in range(self.parts)]
        self.z_pair = self.z + 1 - self.z % 2 * 2
        self.z_pair_ahead = [wrap(self.z_pair + k, self.n_z) for k in range(self.n_z)]
        self.at_z = [z * 4 + self.xc for z in self.z_ahead]
        self.at_x, self.at_core = self.z * 4 + self.other_x, self.z * 4 + self.other_c
        self.at_head = [h * self.parts + self.g for h in self.h_ahead]
        self.at_part = [self.h * self.parts + g for g in self.g_ahead]

    def along_z(self, k):
        return (self.at_z[k], self.b)

    def across_z(self):
        return (self.z_pair * 4 + self.xc, self.b)

    def across_x(self):
        return (self.at_x, self.b)

    def across_core(self):
        return (self.at_core, self.b)

    def batch_ahead(self, k):
        return self.b_ahead[k]

    def batch_behind(self, k):
        return self.b_ahead[(self.n_b - k) % self.n_b]

    def across_batch(self, k):
        return (self.s, self.b_ahead[k])

    def head_ahead(self, k):
        return self.h_ahead[k % H] if isinstance(k, int) else wrap(self.h + k, H)

    def head_behind(self, k):
        return self.h_ahead[(H - k) % H] if isinstance(k, int) else wrap(self.h + H - k, H)

    def across_heads(self, k):
        return (self.at_head[k] if isinstance(k, int) else self.head_ahead(k) * self.parts + self.g, self.b)

    def part_ahead(self, k):
        return self.g_ahead[k]

    def across_parts(self, k):
        return (self.at_part[k], self.b)


def greet(peers):
    barrier = pltpu.get_barrier_semaphore()
    for peer in peers:
        pl.semaphore_signal(barrier, inc=1, device_id=peer, device_id_type=pl.DeviceIdType.MESH)
    pl.semaphore_wait(barrier, len(peers))


def greet_all(place):
    barrier = pltpu.get_barrier_semaphore()

    def hello(b, i, carry):
        peer = (wrap(place.s + i, place.n_s), b)
        pl.semaphore_signal(barrier, inc=1, device_id=peer, device_id_type=pl.DeviceIdType.MESH)
        return carry

    for k, b in enumerate(place.b_ahead):
        lax.fori_loop(0 if k else 1, place.n_s, functools.partial(hello, b), 0)
    pl.semaphore_wait(barrier, place.n_s * place.n_b - 1)


def far_first(i):
    if isinstance(i, int) and i in (0, H):
        return i
    return H // 2 + i // 2 * (1 - i % 2 * 2)


class Copy:
    def __init__(self, wire, i, build):
        self.wire, self.i, self.build = wire, i, build

    def made(self):
        return self.wire.make(self.i, *self.build())

    def start(self):
        self.made().start()

    def wait_recv(self):
        self.made().wait_recv()

    def wait_send(self):
        self.made().wait_send()


class Wire:
    def __init__(self, send_sems, recv_sems):
        self.send_sems, self.recv_sems, self.copies, self.used = send_sems, recv_sems, [], 0

    def reserve(self, count):
        self.used += count
        return self.used - count

    def make(self, i, src, dst, peer):
        return pltpu.make_async_remote_copy(
            src_ref=src,
            dst_ref=dst,
            send_sem=self.send_sems.at[i],
            recv_sem=self.recv_sems.at[i],
            device_id=peer,
            device_id_type=pl.DeviceIdType.MESH,
        )

    def plan(self, build):
        return Copy(self, self.reserve(1), build)

    def send(self, build):
        copy = self.plan(build)
        copy.start()
        self.copies.append(copy)
        return copy

    def drain(self):
        for copy in self.copies:
            copy.wait_send()
        self.copies = []


def received(copies):
    for copy in copies:
        copy.wait_recv()


class Gather:
    def __init__(self, place, wire, src, dst, own_sem, cut):
        self.place, self.wire, self.src, self.dst, self.cut, self.own_sem = place, wire, src, dst, cut, own_sem
        self.own().start()
        self.begin()

    def begin(self):
        p = self.place
        self.along = [self.wire.send(lambda k=k: (self.src, self.slot(p.z), p.along_z(k))) for k in range(1, p.n_z)]

    def slot(self, z):
        return self.dst.at[self.place.b, :, z, self.place.xc]

    def own(self):
        return pltpu.make_async_copy(self.src, self.slot(self.place.z), self.own_sem)

    def forward(self, part, *peers):
        return [self.wire.send(lambda peer=peer: (part(), part(), peer())) for peer in peers]

    def column(self, b, xc):
        return lambda: self.dst.at[b(), :, :, xc]

    def half(self, b, xc, second):
        span = pl.ds(self.cut, self.place.n_z - self.cut) if second else pl.ds(0, self.cut)
        return lambda: self.dst.at[b(), :, span, xc]

    def batch_peers(self):
        return [lambda k=k: self.place.across_batch(k) for k in range(1, self.place.n_b)]

    def to_plane(self):
        p = self.place
        self.own().wait()
        received(self.along)
        peers = [p.across_x, p.across_core] + self.batch_peers()
        self.plane = self.forward(self.column(lambda: p.b, p.xc), *peers)

    def to_diagonal(self):
        p = self.place
        self.plane[0].wait_recv()
        self.diagonal = self.forward(self.half(lambda: p.b, p.other_x, 0), *self.batch_peers())
        self.cores = [self.plane[1]] + self.forward(self.column(lambda: p.b, p.other_x), p.across_core)
        for k in range(1, p.n_b):
            b = lambda k=k: p.batch_behind(k)
            self.plane[1 + k].wait_recv()
            self.diagonal += self.forward(self.half(b, p.xc, 1), p.across_x)
            self.cores += self.forward(self.column(b, p.xc), p.across_core)

    def to_cores(self):
        p = self.place
        for k in range(1, p.n_b):
            for second in range(2):
                self.diagonal[(p.n_b - 1) * second + k - 1].wait_recv()
                part = self.half(lambda k=k: p.batch_behind(k), p.other_x, second)
                self.cores += self.forward(part, p.across_core)

    def finish(self):
        received(self.cores)


class PairGather(Gather):

    def begin(self):
        p, self.far = self.place, range(2, self.place.n_z, 2)
        self.along = [self.wire.send(lambda: (self.src, self.slot(p.z), p.across_z()))]
        self.arriving = [self.wire.send(lambda k=k: (self.src, self.slot(p.z), p.along_z(k))) for k in self.far]

    def to_pair(self):
        p = self.place
        for copy, k in zip(self.arriving, self.far):
            copy.wait_recv()
            z = p.z_ahead[p.n_z - k]
            self.along.append(self.wire.send(lambda z=z: (self.slot(z), self.slot(z), p.across_z())))


class ShortGather(Gather):
    def to_plane(self):
        p = self.place
        self.own().wait()
        received(self.along)
        diagonal = [
            lambda k=k: (p.z * 4 + p.other_x, p.batch_ahead(k)) for k in range(1, p.n_b)
        ]
        peers = [p.across_core, p.across_x] + self.batch_peers() + diagonal
        self.plane = self.forward(self.column(lambda: p.b, p.xc), *peers)

    def to_cores(self):
        p = self.place
        behind = [lambda k=k: p.batch_behind(k) for k in range(1, p.n_b)]
        columns = [(lambda: p.b, p.other_x)] + [(b, p.xc) for b in behind] + [(b, p.other_x) for b in behind]
        self.cores = [self.plane[0]]
        for copy, (b, xc) in zip(self.plane[1:], columns):
            copy.wait_recv()
            self.cores += self.forward(self.column(b, xc), p.across_core)


def normed_of(values):
    center = values - jnp.mean(values, axis=-1, keepdims=True)
    inverse = lax.rsqrt(jnp.mean(center * center, axis=-1, keepdims=True) + EPS)
    return center * inverse, inverse


def norm_back(grad_norm, normed, inverse):
    return inverse * (
        grad_norm
        - jnp.mean(grad_norm, axis=-1, keepdims=True)
        - normed * jnp.mean(grad_norm * normed, axis=-1, keepdims=True)
    )


def gelu_pair(z):
    c = 0.7978845608028654
    z2 = z * z
    t = jnp.tanh(c * z * (1.0 + 0.044715 * z2))
    half = 0.5 * (1.0 + t)
    slope = half + 0.5 * z * (1.0 - t * t) * (c * (1.0 + 3 * 0.044715 * z2))
    return z * half, slope


def language_rows(groups_ref, small_ref, rows):
    table = [small_piece(small_ref, ROW_E + 4 * e, 4) for e in range(GROUPS)]
    out = []
    for m in range(rows):
        acc = jnp.zeros_like(table[0])
        for e in range(GROUPS):
            acc = acc + jnp.where(groups_ref[m] == e, table[e], 0.0)
        out.append(acc)
    return out


def column_sum(x):
    return jnp.sum(x, axis=0, keepdims=True)


class Scatter:
    def __init__(self, place, wire, part, core, acc, far, near, plane_x, plane_b, column):
        self.begin(place, wire, part, core, acc, column)
        self.far, self.near, self.plane_x, self.plane_b = far, near, plane_x, plane_b
        self.cut = far.shape[2]

    def begin(self, place, wire, part, core, acc, column):
        self.place, self.wire = place, wire
        self.part, self.core, self.acc, self.column = part, core, acc, column
        self.kind = part.dtype
        self.x, self.c = place.x, place.c
        self.slabs = part.shape[1]

    def add(self, target, *others):
        total = target[...].astype(F32)
        for other in others:
            total = total + other[...].astype(F32)
        target[...] = total.astype(self.kind)

    def each(self, body, first=0, last=None):
        for j in range(self.slabs):

            def step(z, carry, j=j):
                body(j, z)
                return carry

            lax.fori_loop(first, self.place.n_z if last is None else last, step, 0)

    def to_core(self):
        p = self.place
        self.moved = [self.wire.send(lambda: (self.part.at[:, :, :, :, 1 - self.c], self.core, p.across_core()))]

    def join(self):
        p = self.place
        received(self.moved)
        for j in range(self.slabs):

            def body(b, carry, j=j):
                def at_z(z, carry):
                    for x in range(2):
                        total = self.part[b, j, z, x, self.c].astype(F32) + self.core[b, j, z, x].astype(F32)
                        self.acc[b, j, z, x] = total.astype(self.kind)
                    return carry

                return lax.fori_loop(0, p.n_z, at_z, carry)

            lax.fori_loop(0, p.n_b, body, 0)

    def to_diagonal(self):
        p = self.place
        self.join()
        cut, rest = pl.ds(0, self.cut), pl.ds(self.cut, p.n_z - self.cut)
        self.moved_far, self.moved_near = [], []
        for k in range(1, p.n_b):
            diagonal = lambda k=k: self.acc.at[p.batch_ahead(k), :, :, 1 - self.x]
            self.moved_far.append(
                self.wire.send(
                    lambda k=k, part=diagonal: (part().at[:, cut], self.far.at[k - 1], p.across_batch(k))
                )
            )
            self.moved_near.append(
                self.wire.send(lambda k=k, part=diagonal: (part().at[:, rest], self.near.at[k - 1], p.across_x()))
            )

    def to_plane(self):
        p = self.place
        for k in range(1, p.n_b):
            self.moved_near[k - 1].wait_recv()
            self.each(
                lambda j, z, k=k: self.add(
                    self.acc.at[p.batch_ahead(k), j, z, self.x], self.near.at[k - 1, j, z - self.cut]
                ),
                self.cut,
            )
        received(self.moved_far)
        self.each(
            lambda j, z: self.add(
                self.acc.at[p.b, j, z, 1 - self.x], *[self.far.at[k - 1, j, z] for k in range(1, p.n_b)]
            ),
            0,
            self.cut,
        )
        self.moved = [self.wire.send(lambda: (self.acc.at[p.b, :, :, 1 - self.x], self.plane_x, p.across_x()))]
        self.moved += [
            self.wire.send(
                lambda k=k: (
                    self.acc.at[p.batch_ahead(k), :, :, self.x],
                    self.plane_b.at[k - 1],
                    p.across_batch(k),
                )
            )
            for k in range(1, p.n_b)
        ]

    def others(self, j, z):
        return [self.plane_x.at[j, z]] + [self.plane_b.at[k - 1, j, z] for k in range(1, self.place.n_b)]

    def to_owner(self):
        p = self.place
        received(self.moved)
        self.each(lambda j, z: self.add(self.acc.at[p.b, j, z, self.x], *self.others(j, z)))
        self.moved = [
            self.wire.send(
                lambda k=k: (
                    self.acc.at[p.b, :, p.z_ahead[k], self.x],
                    self.column.at[k - 1],
                    p.along_z(k),
                )
            )
            for k in range(1, p.n_z)
        ]

    def total(self, j):
        p = self.place
        out = self.acc[p.b, j, p.z, self.x].astype(F32)
        for k in range(1, p.n_z):
            out = out + self.column[k - 1, j].astype(F32)
        return out

    def finish(self):
        received(self.moved)


class PairScatter(Scatter):

    def to_owner(self):
        p = self.place
        received(self.moved)
        self.each(lambda j, z: self.add(self.acc.at[p.b, j, z, self.x], *self.others(j, z)))
        self.moved = [
            self.wire.send(
                lambda i=i: (
                    self.acc.at[p.b, :, p.z_pair_ahead[2 * i], self.x],
                    self.column.at[i],
                    p.across_z(),
                )
            )
            for i in range(p.n_z // 2)
        ]

    def to_far(self):
        p = self.place
        half = p.n_z // 2
        received(self.moved)
        for i in range(half):
            for j in range(self.slabs):
                self.add(self.acc.at[p.b, j, p.z_ahead[2 * i], self.x], self.column.at[i, j])
        self.moved = [
            self.wire.send(
                lambda i=i: (
                    self.acc.at[p.b, :, p.z_ahead[2 * i], self.x],
                    self.column.at[half + i - 1],
                    p.along_z(2 * i),
                )
            )
            for i in range(1, half)
        ]

    def total(self, j):
        p = self.place
        out = self.acc[p.b, j, p.z, self.x].astype(F32)
        for k in range(p.n_z // 2, p.n_z - 1):
            out = out + self.column[k, j].astype(F32)
        return out


class ShortScatter(Scatter):
    def __init__(self, place, wire, part, core, acc, plane, column):
        self.begin(place, wire, part, core, acc, column)
        self.plane = plane

    def to_plane(self):
        p = self.place
        self.join()
        self.moved = []
        for k in range(p.n_b):
            for dx in range(2):
                if k or dx:

                    def build(k=k, dx=dx, slot=len(self.moved)):
                        x = self.x if dx == 0 else 1 - self.x
                        to = p.z * 4 + (p.other_x if dx else p.xc)
                        b = p.batch_ahead(k)
                        return (self.acc.at[b, :, :, x], self.plane.at[slot], (to, b))

                    self.moved.append(self.wire.send(build))

    def others(self, j, z):
        return [self.plane.at[k, j, z] for k in range(2 * self.place.n_b - 1)]


def short_scratch(n_b, slabs, n_z, r, cols, kind):
    return [
        pltpu.VMEM((n_b, slabs, n_z, 2, r, cols), kind),
        pltpu.VMEM((n_b, slabs, n_z, 2, r, cols), kind),
        pltpu.VMEM((2 * n_b - 1, slabs, n_z, r, cols), kind),
        pltpu.VMEM((n_z - 1, slabs, r, cols), kind),
    ]


def scatter_scratch(n_b, slabs, n_z, r, cols, kind):
    return [
        pltpu.VMEM((n_b, slabs, n_z, 2, r, cols), kind),
        pltpu.VMEM((n_b, slabs, n_z, 2, r, cols), kind),
        pltpu.VMEM((n_b - 1, slabs, n_z - n_z // 4, r, cols), kind),
        pltpu.VMEM((n_b - 1, slabs, n_z // 4, r, cols), kind),
        pltpu.VMEM((slabs, n_z, r, cols), kind),
        pltpu.VMEM((n_b - 1, slabs, n_z, r, cols), kind),
        pltpu.VMEM((n_z - 1, slabs, r, cols), kind),
    ]


SCATTER_SCRATCH, SHORT_SCRATCH = 7, 4
SLABS = 6


def lanes_of(values):
    lane = lax.broadcasted_iota(jnp.int32, (8, LANES), 1)
    row = lax.broadcasted_iota(jnp.int32, (8, LANES), 0)
    tile = jnp.zeros((8, LANES), F32)
    for j, value in enumerate(values):
        if value is not None:
            tile = tile + jnp.where((lane == j) & (row == 0), value, 0.0)
    return tile


def sum_all(x):
    return jnp.sum(jnp.sum(x, axis=1, keepdims=True), axis=0, keepdims=True)


def to_frame(values, at):
    wide = jnp.concatenate([values, jnp.zeros((1, 8 * LANES - values.shape[1]), F32)], axis=1)
    wide = pltpu.roll(wide, at, 1)
    return jnp.concatenate([wide[:, k * LANES : (k + 1) * LANES] for k in range(8)], axis=0)


def from_frame(tile, at, chunk):
    wide = jnp.concatenate([tile[k : k + 1] for k in range(8)], axis=1)
    return pltpu.roll(wide, 8 * LANES - at, 1)[:, :chunk]


def own_place(chunk):
    index = lax.axis_index("seq") * lax.axis_size("batch") + lax.axis_index("batch")
    return lax.rem(index * chunk, FRAME_ROWS * LANES)


def segment_ids(lengths, idk_ref, idq_ref, place, tokens):
    rows, length = idk_ref.shape[0], idk_ref.shape[1]
    upto = lax.broadcasted_iota(jnp.int32, (SEGS, LANES), 0) <= lax.broadcasted_iota(jnp.int32, (SEGS, LANES), 1)
    upto = jnp.where(upto, 1.0, 0.0).astype(BF)
    values = lengths.astype(F32)
    high = jnp.floor(values * (1.0 / 64))
    low = (values - 64.0 * high).astype(BF)
    high = high.astype(BF)
    ends = mm(high, upto) * 64.0 + mm(low, upto)
    ends = jnp.where(lax.broadcasted_iota(jnp.int32, (rows, LANES), 1) < SEGS, ends, 1e9)
    upto = upto[:, :SEGS]
    ends_down = lax.dot_general(upto, high, (((0,), (1,)), ((), ())), preferred_element_type=F32) * 64.0
    ends_down = ends_down + lax.dot_general(upto, low, (((0,), (1,)), ((), ())), preferred_element_type=F32)
    ones = jnp.ones((LANES, LANES), BF)
    span = 256
    for m in range(rows):

        def fill(i, carry, m=m):
            at = pl.multiple_of(i * span, span)
            places = (at + lax.broadcasted_iota(jnp.int32, (span, LANES), 0)).astype(F32)
            passed = jnp.where(ends[m : m + 1] <= places, 1.0, 0.0).astype(BF)
            seg = mm(passed, ones)
            idk_ref[m, pl.ds(at, span), :] = jnp.where(seg < SEGS, seg, SEGS + places)
            return carry

        lax.fori_loop(0, length // span, fill, 0)
        for h in range(H):
            first = ((h * place.parts + place.g) * tokens + lax.broadcasted_iota(jnp.int32, (1, tokens), 1)).astype(F32)
            seg = column_sum(jnp.where(ends_down[:, m : m + 1] <= first, 1.0, 0.0))
            group, k = h // GROUP, h % GROUP
            idq_ref[m, group, :, k * tokens : (k + 1) * tokens] = jnp.where(seg < SEGS, seg, SEGS + first)


def layer_kernel(
    groups_ref, lengths_ref, tok_ref, cot_ref, attn_ref, ffn_ref, params_ref, arows_ref, acols_ref, frows_ref,
    fcols_ref, sq_ref,
    out_hbm, du_hbm, agrad_hbm, fgrad_hbm, update_a_hbm, update_f_hbm, scales_ref, rows_new_ref, acols_new_ref,
    fcols_new_ref, own_new_ref,
    *scratch,
):
    place = Place()
    scratch = list(scratch)
    own_sems, recv_sems, send_sems = scratch.pop(), scratch.pop(), scratch.pop()
    wire = Wire(send_sems, recv_sems)

    def take(count):
        taken = scratch[:count]
        del scratch[:count]
        return taken

    pack_low, kv_low, wo_low, ffn_low, own_ref, small_ref, pack_ref, wkv_ref, wo_ref, w1_ref, w2_ref = take(11)
    idk_ref, idq_ref, q_ref, kv_ref, qsend_ref, kvsend_ref, qm_ref, dom_ref = take(8)
    peak_ref, acc_ref, ot_ref, lse_ref, delta_ref, o_ref, otile_ref, dotile_ref, do_ref = take(9)
    act_ref, slope_ref, dz_ref, sum_ref, frames_ref = take(5)
    dqt_ref, part_ref, near_ref, dkv_sum, dq_ref, dq_back, dkv_back = take(7)
    dwo_ref, dw1_ref, dw2_ref, dkv_w_ref, dq_w_ref, dsmall_ref = take(6)
    cols_plane, rows_plane, all_z, late_cols, late_rows, late_sums, all_sums = take(7)
    out_ref, du_ref, agrad_ref, fgrad_ref, update_a, update_f = take(6)
    written = [
        pltpu.make_async_copy(src, dst, own_sems.at[5 + i])
        for i, (src, dst) in enumerate(
            (
                (out_ref, out_hbm),
                (du_ref, du_hbm),
                (agrad_ref, agrad_hbm),
                (fgrad_ref, fgrad_hbm),
                (update_a, update_a_hbm),
                (update_f, update_f_hbm),
            )
        )
    ]
    n_z, n_b, parts = place.n_z, place.n_b, place.parts
    rows = 2
    count = tok_ref.shape[0]
    tokens = count // rows
    r, cols = attn_ref.shape[1:]
    cols_f = ffn_ref.shape[2]
    groups = H // GROUP
    width = GROUP * tokens
    keys = parts * tokens
    scale2 = SCALE * LOG2E
    low = low_half()

    plane = [(dx, db) for db in range(n_b) for dx in range(4) if dx or db]

    def plane_peer(dx, db):
        return (place.z * 4 + place.xc_ahead[dx], place.batch_ahead(db))

    along = [place.along_z(k) for k in range(1, n_z)]
    greet_all(place)

    chunk = params_ref.shape[0]
    own_at = own_place(chunk)
    own = to_frame(params_ref[...].reshape(1, chunk), own_at)
    own_ref[...] = own
    pack_low[0, :r] = attn_ref[0].astype(BF)
    tile = jnp.concatenate([own, jnp.zeros((8, LANES), F32)], axis=0)
    if cols < LANES:
        tile = jnp.concatenate([own[:, :cols], own[:, cols:]], axis=0)
    if cols > LANES:
        tile = jnp.concatenate([tile, jnp.zeros((16, cols - LANES), F32)], axis=1)
    pack_low[0, r:] = tile.astype(BF)
    pack = ShortGather(place, wire, pack_low, pack_ref, own_sems.at[0], n_z)
    kv_low[...] = attn_ref[1:3].astype(BF)
    kv_w = ShortGather(place, wire, kv_low, wkv_ref, own_sems.at[4], n_z)
    wo_low[0] = attn_ref[3].astype(BF)
    ffn_low[...] = ffn_ref[...].astype(BF)
    segment_ids(lengths_ref[...], idk_ref, idq_ref, place, tokens)
    for i in range(rows * groups):
        peak_ref[i] = jnp.full((1, width), NEG, F32)
        acc_ref[i] = jnp.zeros((HD + 16, width), F32)
    frames_ref[...] = jnp.zeros_like(frames_ref)
    dqt_ref[...] = jnp.zeros_like(dqt_ref)
    pack.to_plane()
    kv_w.to_plane()
    most = n_z - n_z // 4
    first = Gather(place, wire, ffn_low.at[pl.ds(0, 1)], w1_ref, own_sems.at[1], most)
    out_w = Gather(place, wire, wo_low, wo_ref, own_sems.at[2], most)
    second = PairGather(place, wire, ffn_low.at[pl.ds(1, 1)], w2_ref, own_sems.at[3], most)
    pack.to_cores()
    pack.finish()
    frame = place.n_s * n_b // FRAMES
    for f in range(FRAMES):
        total = None
        for i in range(f * frame, (f + 1) * frame):
            s, b = i // n_b, i % n_b
            tile = pack_ref[b, 0, s // 4, s % 4, r:].astype(F32)
            if cols < LANES:
                tile = jnp.concatenate([tile[:8], tile[8:]], axis=1)
            tile = tile[:8, :LANES]
            total = tile if total is None else total + tile
        small_ref[f] = total
    lang = language_rows(groups_ref, small_ref, rows)

    def inputs():
        return jnp.concatenate(
            [tok_ref[m * tokens : (m + 1) * tokens].astype(F32) + lang[m] for m in range(rows)], axis=0
        )

    def w_qkv(b, j):
        w = wkv_ref[b, j - 1] if j else pack_ref[b, 0, :, :, :r]
        return w.reshape(D, cols)

    a = inputs().astype(BF)

    def project(j, bias):
        out = jnp.concatenate([mm(a, w_qkv(b, j)) for b in range(n_b)], axis=1)
        if bias is not None:
            out = out + small_piece(small_ref, bias, 4)
        return [t.astype(BF) for t in rows_to_heads(out[:tokens], out[tokens:])]

    for h, t in enumerate(project(0, ROW_BQ)):
        qsend_ref[h] = t
    q_ref[place.h] = qsend_ref[place.h]
    def to_heads(src, dst):
        return [
            wire.send(lambda k=k: (src.at[place.head_ahead(k)], dst.at[place.h], place.across_heads(k)))
            for k in outwards(H)
        ]

    moved_q = to_heads(qsend_ref, q_ref)
    second.to_pair()
    kv_w.to_cores()
    first.to_plane()
    out_w.to_plane()
    kv_w.finish()
    for j, bias in ((0, None), (1, ROW_BV)):
        for h, t in enumerate(project(1 + j, bias)):
            kvsend_ref[h, j] = t
    kv_ref[place.s] = kvsend_ref[place.h]
    kv_sems = wire.reserve(H)
    share_sems = wire.reserve(H * (parts - 1))

    def moved_kv(i):
        k = far_first(i)
        return wire.make(
            kv_sems + i, kvsend_ref.at[place.head_ahead(k)], kv_ref.at[place.s], place.across_heads(k)
        )

    def ordered(i):
        return far_first(i) if isinstance(i, int) else jnp.where(i == 0, 0, far_first(i))

    def shared_kv(i, j):
        slot = kv_ref.at[place.head_behind(ordered(i)) * parts + place.g]
        return wire.make(share_sems + i * (parts - 1) + j - 1, slot, slot, place.across_parts(j))

    for j in range(1, parts):
        shared_kv(0, j).start()
    for k in range(1, H):
        moved_kv(k).start()
    second.to_plane()

    def masked_rows(src_ref, dst_ref):
        for g in range(groups):
            both = src_ref[g * GROUP : (g + 1) * GROUP].reshape(width, LANES)
            zero = jnp.zeros_like(both)
            dst_ref[0, g] = jnp.where(low, both, zero)
            dst_ref[1, g] = jnp.where(low, zero, both)

    received(moved_q)
    masked_rows(q_ref, qm_ref)

    def pair(h):
        kv = kv_ref[pl.ds(h * parts, parts)]
        return kv[:, 0].reshape(keys, LANES), kv[:, 1].reshape(keys, LANES)

    def key_ids(h, m):
        ids = idk_ref[m, pl.ds(pl.multiple_of(h * keys, keys), keys), :]
        return jnp.concatenate([ids] * (width // LANES), axis=1)

    def attend(k):
        h = place.head_behind(ordered(k))
        ids = [key_ids(h, m) for m in range(rows)]
        for j in range(1, parts):
            shared_kv(k, j).wait_recv()
        key, value = pair(h)
        value_t = value.T
        ones = jnp.ones((16, keys), BF)
        for g in range(groups):
            for m in range(rows):
                i = g * rows + m
                s = jnp.where(ids[m] == idq_ref[m, g], mm_nt(key, qm_ref[m, g]) * scale2, NEG)
                new = jnp.maximum(peak_ref[i], jnp.max(s, axis=0, keepdims=True))
                p = jnp.exp2(s - new).astype(BF)
                alpha = jnp.exp2(peak_ref[i] - new)
                left = jnp.concatenate([value_t[m * HD : (m + 1) * HD], ones], axis=0)
                acc_ref[i] = acc_ref[i] * alpha + mm(left, p)
                peak_ref[i] = new

    def meanwhile(k, *stages):
        for at, stage in stages:
            pl.when(k == at)(stage)

    def forward_step(k, carry):
        moved_kv(k).wait_recv()
        for j in range(1, parts):
            shared_kv(k, j).start()
        attend(k - 1)
        meanwhile(
            k,
            (2, first.to_diagonal),
            (2, out_w.to_diagonal),
            (6, second.to_diagonal),
        )
        return carry

    lax.fori_loop(1, H, forward_step, 0)
    attend(H - 1)
    for g in range(groups):
        for m in range(rows):
            i = g * rows + m
            total = acc_ref[i, HD : HD + 1]
            ot_ref[g, m * HD : (m + 1) * HD] = acc_ref[i, :HD] * (1.0 / total)
            lse_ref[i] = peak_ref[i] + jnp.log2(total)
        o_ref[g * GROUP : (g + 1) * GROUP] = ot_ref[g].T.astype(BF).reshape(GROUP, tokens, LANES)
    moved = to_heads(o_ref, otile_ref)
    otile_ref[place.h] = o_ref[place.h]
    for piece in (out_w, first, second):
        piece.to_cores()

    tiles, wide = act_ref.shape[0], act_ref.shape[2]
    per_b = cols_f // wide
    bias_1 = [small_piece(small_ref, ROW_B1 + i * wide // LANES, wide // LANES) for i in range(tiles)]
    gain1, shift1 = small_piece(small_ref, ROW_G1, 4), small_piece(small_ref, ROW_S1, 4)
    gain2, shift2 = small_piece(small_ref, ROW_G2, 4), small_piece(small_ref, ROW_S2, 4)
    bias_o, bias_2 = small_piece(small_ref, ROW_BO, 4), small_piece(small_ref, ROW_B2, 4)

    def block(ref, i):
        at = i % per_b * wide
        return ref[i // per_b, 0, :, :, :, at : at + wide].reshape(D, wide)

    live = jnp.concatenate(
        [idk_ref[m, pl.ds(pl.multiple_of(place.s * tokens, tokens), tokens), :] for m in range(rows)], axis=0
    )
    live = jnp.where(live < SEGS, 1.0, 0.0)
    u = inputs()
    out_w.finish()
    first.finish()
    received(moved)
    mixed = jnp.concatenate(heads_to_rows([otile_ref[h].astype(F32) for h in range(H)]), axis=0).astype(BF)
    attn_out = jnp.concatenate([mm(mixed, wo_ref[b, 0].reshape(D, cols)) for b in range(n_b)], axis=1)
    normed1, inverse1 = normed_of(u + (attn_out + bias_o))
    hidden = normed1 * gain1 + shift1
    hb = hidden.astype(BF)
    for i in range(tiles):
        act, slope = gelu_pair(mm(hb, block(w1_ref, i)) + bias_1[i])
        slope_ref[i] = slope
        act_ref[i] = act.astype(BF)
    second.finish()
    total = hidden + u + bias_2
    for i in range(tiles):
        total = total + mm_nt(act_ref[i], block(w2_ref, i))

    normed2, inverse2 = normed_of(total)
    out_ref[...] = (normed2 * gain2 + shift2).astype(BF)
    c = cot_ref[...].astype(F32) * jnp.concatenate([live] * (D // LANES), axis=1)
    dr = norm_back(c * gain2, normed2, inverse2)
    df = dr.astype(BF)

    def scatter(part):
        return PairScatter(place, wire, part, *take(SCATTER_SCRATCH))

    g_first, g_second, g_out = scatter(dw1_ref), scatter(dw2_ref), scatter(dwo_ref)
    g_kv = Scatter(place, wire, dkv_w_ref, *take(SCATTER_SCRATCH))
    g_q = ShortScatter(place, wire, dq_w_ref, *take(SHORT_SCRATCH))
    g_small = ShortScatter(place, wire, dsmall_ref, *take(SHORT_SCRATCH))

    def weight_grad(left, right_ref, dst_ref):
        left = left.T
        for i in range(tiles):
            at = i % per_b * wide
            grad = mm(left, right_ref[i]).astype(BF).reshape(n_z, 2, 2, r, wide)
            dst_ref[i // per_b, 0, :, :, :, :, at : at + wide] = grad

    weight_grad(df, act_ref, dw2_ref)
    g_second.to_core()
    dh = dr
    for i in range(tiles):
        dz = (mm(df, block(w2_ref, i)) * slope_ref[i]).astype(BF)
        dz_ref[i] = dz
        dh = dh + mm_nt(dz, block(w1_ref, i))
    dpre = norm_back(dh * gain1, normed1, inverse1)
    dattn = dpre.astype(BF)
    do = mm_nt(dattn[:, :cols], wo_ref[0, 0].reshape(D, cols))
    for b in range(1, n_b):
        do = do + mm_nt(dattn[:, b * cols : (b + 1) * cols], wo_ref[b, 0].reshape(D, cols))
    for h, t in enumerate(rows_to_heads(do[:tokens], do[tokens:])):
        dotile_ref[h] = t.astype(BF)
    moved = to_heads(dotile_ref, do_ref)
    written[0].start()
    do_ref[place.h] = dotile_ref[place.h]
    sum_ref[...] = dpre + dr

    g_second.to_diagonal()
    weight_grad(hb, dz_ref, dw1_ref)
    g_first.to_core()
    mixed_t = mixed.T
    for b in range(n_b):
        dwo = mm(mixed_t, dattn[:, b * cols : (b + 1) * cols]).astype(BF)
        dwo_ref[b, 0] = dwo.reshape(n_z, 2, 2, r, cols)
    g_out.to_core()
    for k in range(H):
        for j in range(1, parts):
            shared_kv(k, j).wait_send()
        if k:
            moved_kv(k).wait_send()
    wire.drain()

    g_first.to_diagonal()
    g_out.to_diagonal()
    add_small(frames_ref, ROW_G2, column_sum(c * normed2))
    add_small(frames_ref, ROW_S2, column_sum(c))
    add_small(frames_ref, ROW_B2, column_sum(df.astype(F32)))
    for i in range(tiles):
        add_small(frames_ref, ROW_B1 + i * wide // LANES, column_sum(dz_ref[i].astype(F32)))
    add_small(frames_ref, ROW_G1, column_sum(dh * normed1))
    add_small(frames_ref, ROW_S1, column_sum(dh))
    add_small(frames_ref, ROW_BO, column_sum(dattn.astype(F32)))
    received(moved)
    masked_rows(do_ref, dom_ref)
    g_second.to_plane()
    for g in range(groups):
        product = do_ref[g * GROUP : (g + 1) * GROUP].reshape(width, LANES).astype(F32).T * ot_ref[g]
        for m in range(rows):
            delta_ref[g * rows + m] = column_sum(product[m * HD : (m + 1) * HD])

    near_sems = wire.reserve(H * (parts - 1))
    back_sems = wire.reserve(H)

    def target(k):
        far = far_first(k) if isinstance(k, int) else jnp.where(k == H, H, far_first(k))
        return place.head_ahead(far)

    def near_kv(k, j):
        h = target(k)
        return wire.make(
            near_sems + (k - 1) * (parts - 1) + j - 1,
            part_ref.at[h, place.part_ahead(j)],
            near_ref.at[j - 1, h],
            place.across_parts(j),
        )

    def back_kv(k):
        h = target(k)
        return wire.make(back_sems + k - 1, dkv_sum.at[h], dkv_back.at[place.h], (h * parts + place.g, place.b))

    def fold(k):
        h = target(k)
        total = part_ref[h, place.g].astype(F32)
        for j in range(1, parts):
            near_kv(k, j).wait_recv()
            total = total + near_ref[j - 1, h].astype(F32)
        return total.astype(BF)

    def key_step(k):
        h = target(k)
        key, value = pair(h)
        key_t = key.T
        ids = [key_ids(h, m) for m in range(rows)]
        dk = jnp.zeros((keys, LANES), F32)
        dv = jnp.zeros((keys, LANES), F32)
        for g in range(groups):
            for m in range(rows):
                i = g * rows + m
                p = jnp.exp2(mm_nt(key, qm_ref[m, g]) * scale2 - lse_ref[i])
                p = jnp.where(ids[m] == idq_ref[m, g], p, 0.0)
                ds = (p * (mm_nt(value, dom_ref[m, g]) - delta_ref[i])).astype(BF)
                dv = dv + mm(p.astype(BF), dom_ref[m, g])
                dk = dk + mm(ds, qm_ref[m, g])
                dqt_ref[g, m * HD : (m + 1) * HD] += mm(key_t[m * HD : (m + 1) * HD], ds)
        part_ref[h, :, 0] = (dk * SCALE).astype(BF).reshape(parts, tokens, LANES)
        part_ref[h, :, 1] = dv.astype(BF).reshape(parts, tokens, LANES)
        for j in range(1, parts):
            near_kv(k, j).start()

    def backward_step(k, carry):
        key_step(k)
        dkv_sum[target(k - 1)] = fold(k - 1)
        back_kv(k - 1).start()
        meanwhile(
            k,
            (6, g_first.to_plane),
            (6, g_out.to_plane),
        )
        return carry

    token_pieces = (g_second, g_first, g_out)
    key_step(1)
    lax.fori_loop(2, H + 1, backward_step, 0)
    for g in range(groups):
        dq_ref[g * GROUP : (g + 1) * GROUP] = (dqt_ref[g] * SCALE).T.astype(BF).reshape(GROUP, tokens, LANES)
    moved = to_heads(dq_ref, dq_back)
    dq_back[place.h] = dq_ref[place.h]
    dkv_back[place.h] = fold(H)
    g_second.to_owner()

    def to_rows(parts_of):
        return jnp.concatenate(heads_to_rows([t.astype(F32) for t in parts_of]), axis=0).astype(BF)

    def grad_of(left, right, b):
        return mm(left, right[:, b * cols : (b + 1) * cols]).astype(BF).reshape(n_z, 2, 2, r, cols)

    def back_through(total, right, j):
        for b in range(n_b):
            total = total + mm_nt(right[:, b * cols : (b + 1) * cols], w_qkv(b, j))
        return total

    for k in range(1, H):
        back_kv(k).wait_recv()
    a_t = inputs().astype(BF).T
    dk = to_rows([dkv_back[h, 0] for h in range(H)])
    dv = to_rows([dkv_back[h, 1] for h in range(H)])
    for b in range(n_b):
        dkv_w_ref[b, 0] = grad_of(a_t, dk, b)
        dkv_w_ref[b, 1] = grad_of(a_t, dv, b)
    g_kv.to_core()
    add_small(frames_ref, ROW_BV, column_sum(dv.astype(F32)))
    du = back_through(back_through(sum_ref[...], dk, 1), dv, 2)
    g_kv.to_diagonal()
    g_second.to_far()
    g_first.to_owner()
    g_out.to_owner()
    received(moved)
    dq = to_rows([dq_back[h] for h in range(H)])
    for b in range(n_b):
        dq_w_ref[b, 0] = grad_of(a_t, dq, b)
    g_q.to_core()
    du = back_through(du, dq, 0)
    add_small(frames_ref, ROW_BQ, column_sum(dq.astype(F32)))
    sums = [column_sum(du[m * tokens : (m + 1) * tokens]) for m in range(rows)]
    for e in range(GROUPS):
        total = jnp.zeros_like(sums[0])
        for m in range(rows):
            total = total + jnp.where(groups_ref[m] == e, sums[m], 0.0)
        add_small(frames_ref, ROW_E + 4 * e, total)
    for s in range(place.n_s):
        for b in range(n_b):
            dsmall_ref[b, 0, s // 4, s // 2 % 2, s % 2] = frames_ref[(s * n_b + b) // frame]
    g_small.to_core()
    g_q.to_plane()
    g_kv.to_plane()
    g_small.to_plane()
    g_first.to_far()
    g_out.to_far()
    du_ref[...] = du.astype(BF)
    written[1].start()
    g_kv.to_owner()

    weights = [attn_ref.at[j] for j in range(4)] + [ffn_ref.at[j] for j in range(2)]
    outs = [agrad_ref.at[j] for j in range(4)] + [fgrad_ref.at[j] for j in range(2)]
    updates = [update_a.at[j] for j in range(4)] + [update_f.at[j] for j in range(2)]
    old_cols = [acols_ref[j : j + 1] for j in range(4)] + [fcols_ref[j : j + 1] for j in range(2)]
    owners = [(g_q, 0), (g_kv, 0), (g_kv, 1), (g_out, 0), (g_first, 0), (g_second, 0)]
    spans = [cols] * 4 + [cols_f] * 2
    places, used = [], 0
    for span in spans:
        places.append(used)
        used += -(-span // LANES)
    pad = cols_plane.shape[1]
    late = 3
    mine = cols_plane.at[place.xc]
    mine_rows = rows_plane.at[place.b, place.xc]
    mine_late = late_cols.at[place.s]
    mine_late_rows = late_rows.at[place.b]
    mine_sums = late_sums.at[place.b, place.s]
    mine[...] = jnp.zeros((pad, LANES), F32)
    mine_late[...] = jnp.zeros((8, LANES), F32)
    lane = lax.broadcasted_iota(jnp.int32, (r, LANES), 1)
    square_sums = [None] * SLABS
    old_rows = jnp.concatenate([arows_ref[...], frows_ref[...], jnp.zeros((2, r), F32)], axis=0).T
    old_rows = [old_rows[:, j : j + 1] for j in range(SLABS)]
    row_sums_old = [sum_all(x) for x in old_rows]
    weight_squares = [sum_all(w[...] * w[...]) for w in weights]
    own = own_ref[...]
    entry = lax.broadcasted_iota(jnp.int32, (8, LANES), 0) * LANES + lax.broadcasted_iota(jnp.int32, (8, LANES), 1)
    own_mask = jnp.where((entry >= own_at) & (entry < own_at + chunk), 1.0, 0.0)
    weight_squares.append(sum_all(own * own))
    rows_tiles = []

    def gradient(j):
        owner, slab = owners[j]
        grad = owner.total(slab)
        outs[j][...] = grad
        square = grad * grad + EPS_ONE
        row_sum = jnp.sum(square, axis=1, keepdims=True)
        col_sum = column_sum(square)
        ref = mine_late if j < late else mine
        for k in range(0, spans[j], LANES):
            span = min(LANES, spans[j] - k)
            ref[pl.ds(places[j] + k // LANES, 1), pl.ds(0, span)] = col_sum[:, k : k + span]
        square_sums[j] = sum_all(row_sum)
        return jnp.where(lane == j, row_sum, 0.0)

    def renewed(j, row_total, sums, square_total, old_total):
        length = D if j < 4 else FF
        new_rows = DECAY * old_rows[j] + (1.0 - DECAY) * row_total[:, j : j + 1] * (1.0 / length)
        rows_tiles.append(jnp.where(lane == j, new_rows, 0.0))
        mean_rows = (DECAY / n_b * old_total + (1.0 - DECAY) * (1.0 / length) * square_total) * (1.0 / D)
        pieces = [
            sums[places[j] + k // LANES : places[j] + k // LANES + 1, : min(LANES, spans[j] - k)]
            for k in range(0, spans[j], LANES)
        ]
        col_sum = pieces[0] if len(pieces) == 1 else jnp.concatenate(pieces, axis=1)
        new = DECAY * old_cols[j] + (1.0 - DECAY) * (1.0 / D) * col_sum
        if j < 4:
            acols_new_ref[j : j + 1, :] = new
        else:
            fcols_new_ref[j - 4 : j - 3, :] = new
        update = outs[j][...] * lax.rsqrt((new_rows / mean_rows) * new)
        updates[j][...] = update
        return sum_all(update * update)

    def pick(tile, j):
        return tile[0:1, j : j + 1]

    def fan(i, ref, offsets):
        for db in offsets:
            b = place.batch_ahead(db)

            def one(k, carry=0, b=b):
                wire.make(i, ref, ref, (wrap(place.s + k, place.n_s), b)).start()
                return carry

            if place.n_s > 16:
                lax.fori_loop(0 if db else 1, place.n_s, one, 0)
            else:
                for k in outwards(place.n_s) + [0] * (db > 0):
                    one(k)

    near, others = [0], list(range(1, n_b))
    one_peer = place.along_z(1)

    g_second.finish()
    row_tile = gradient(5)
    g_q.to_owner()
    g_small.to_owner()
    g_first.finish()
    g_out.finish()
    mine_rows[pl.ds(0, r), :] = row_tile + gradient(4) + gradient(3)
    tail = pl.ds(r, 8)
    mine_rows[tail, :] = lanes_of(square_sums + row_sums_old + weight_squares)
    moved = []
    for dx, db in plane:
        peer = plane_peer(dx, db)
        if db == 0:
            moved.append(wire.send(lambda peer=peer: (mine, mine, peer)))
        if dx == 0:
            moved.append(wire.send(lambda peer=peer: (mine_rows, mine_rows, peer)))
        else:
            moved.append(wire.send(lambda peer=peer: (mine_rows.at[tail], mine_rows.at[tail], peer)))
    g_kv.finish()
    row_tile = gradient(1) + gradient(2)
    received(moved)
    mine_z = all_z.at[place.z]
    mine_z[pl.ds(0, pad), :] = cols_plane[0] + cols_plane[1] + cols_plane[2] + cols_plane[3]
    scalars = jnp.zeros((8, LANES), F32)
    row_total = jnp.zeros((r, LANES), F32)
    for b in range(n_b):
        for xc in range(4):
            scalars = scalars + rows_plane[b, xc, tail, :]
        row_total = row_total + rows_plane[b, place.xc, pl.ds(0, r), :]
    mine_z[pl.ds(pad, 8), :] = scalars
    moved = [wire.send(lambda peer=peer: (mine_z, mine_z, peer)) for peer in along]

    g_q.finish()
    mine_late_rows[...] = row_tile + gradient(0)
    written[2].start()
    written[3].start()
    sums = lanes_of(square_sums[:late])[0:1]
    mine_late[7:8, :] = sums
    late_sums[place.b] = jnp.zeros((place.n_s, 1, LANES), F32)
    mine_sums[...] = sums
    late_i, sums_i, all_i = wire.reserve(1), wire.reserve(1), wire.reserve(1)
    moved_rows = [
        wire.send(lambda k=k: (mine_late_rows, mine_late_rows, place.across_batch(k))) for k in range(1, n_b)
    ]
    fan(late_i, mine_late, near)
    fan(sums_i, mine_sums, others)

    received(moved)
    reduced = all_z[0]
    for z in range(1, n_z):
        reduced = reduced + all_z[z]
    tile = reduced[pad:]

    def scalar(j):
        return pick(tile, j)

    update_squares = [None] * SLABS
    for j in range(late, SLABS):
        update_squares[j] = renewed(j, row_total, reduced, scalar(j), scalar(SLABS + j))
    g_small.finish()
    own_grad = g_small.total(0) * own_mask
    own_sq = DECAY * to_frame(sq_ref[...].reshape(1, chunk), own_at) + (1.0 - DECAY) * (own_grad * own_grad + EPS_ONE)
    own_update = own_grad * lax.rsqrt(own_sq)
    update_squares.append(sum_all(own_update * own_update))
    for k in range(1, H + 1):
        for j in range(1, parts):
            near_kv(k, j).wait_send()
        if k < H:
            back_kv(k).wait_send()
    wire.drain()

    late_part = late_cols.at[pl.ds(0, place.n_s - 1)]
    sums_part = late_sums.at[pl.ds(0, n_b - 1)]
    wire.make(late_i, late_part, late_part, one_peer).wait_recv()
    wire.make(sums_i, sums_part, sums_part, one_peer).wait_recv()
    received(moved_rows)
    sums = late_cols[0]
    for s in range(1, place.n_s):
        sums = sums + late_cols[s]
    totals = jnp.zeros((1, LANES), F32)
    row_total = jnp.zeros((r, LANES), F32)
    for b in range(n_b):
        other = late_sums[b, 0]
        for s in range(1, place.n_s):
            other = other + late_sums[b, s]
        totals = totals + jnp.where(place.b == b, sums[7:8], other)
        row_total = row_total + late_rows[b]
    for j in range(late):
        update_squares[j] = renewed(j, row_total, sums, pick(totals, j), scalar(SLABS + j))
    written[4].start()
    written[5].start()
    rows_new_ref[...] = sum(rows_tiles[1:], rows_tiles[0])
    mine_u = all_sums.at[place.b * place.n_s + place.s]
    mine_u[...] = lanes_of(update_squares)[0:1]
    fan(all_i, mine_u, near + others)
    wire.make(late_i, late_part, late_part, one_peer).wait_send()
    wire.make(sums_i, sums_part, sums_part, one_peer).wait_send()
    all_part = all_sums.at[pl.ds(0, place.n_s * n_b - 1)]
    copy = wire.make(all_i, all_part, all_part, one_peer)
    copy.wait_send()
    copy.wait_recv()
    update_tile = jnp.zeros((1, LANES), F32)
    for i in range(place.n_s * n_b):
        update_tile = update_tile + all_sums[i]
    sizes = [D * D] * 4 + [D * FF] * 2 + [NVEC]

    def scale(j):
        weight = jnp.sqrt(scalar(2 * SLABS + j) * (1.0 / sizes[j]))
        return LEARN * weight / jnp.maximum(1.0, jnp.sqrt(update_tile[0:1, j : j + 1] * (1.0 / sizes[j])))

    scales_ref[...] = lanes_of([scale(j) for j in range(SLABS)])
    own_new_ref[0] = own_grad
    own_new_ref[1] = own - scale(SLABS) * own_update
    own_new_ref[2] = own_sq
    for copy in written:
        copy.wait()
    wire.drain()


def layer_part(groups, lengths, tok, cot, attn, ffn, params, arows, acols, frows, fcols, sq):
    n_s, n_b = lax.axis_size("seq"), lax.axis_size("batch")
    n_z, parts = n_s // 4, n_s // H
    count = tok.shape[0]
    tokens = count // 2
    rows = 2
    _, r, cols = attn.shape
    cols_f = ffn.shape[2]
    groups_q = H // GROUP
    width = GROUP * tokens
    length = tokens * n_s
    wide = min(512, cols_f)
    tiles = FF // wide
    pad = 4 * -(-cols // LANES) + 2 * (cols_f // LANES)
    pad = -(-pad // 8) * 8
    gather = (n_z - 1) + (1 + n_b) + 2 * (n_b - 1) + 1 + (n_b - 1) + 2 * (n_b - 1)
    copies = 5 * gather + 7 * (H - 1) + 2 * H + 2 * H * (parts - 1)
    copies += 6 * (1 + 2 * (n_b - 1) + n_b + n_z - 1)
    copies += 6 + 4 * n_b + (n_z - 1) + (n_b - 1) + 3

    def shape(dims, kind):
        return jax.ShapeDtypeStruct(dims, kind)

    out = (
        shape(tok.shape, BF),
        shape(tok.shape, BF),
        shape(attn.shape, F32),
        shape(ffn.shape, F32),
        shape(attn.shape, F32),
        shape(ffn.shape, F32),
        shape((8, LANES), F32),
        shape((r, LANES), F32),
        shape(acols.shape, F32),
        shape(fcols.shape, F32),
        shape((3, 8, LANES), F32),
    )
    vmem = pltpu.VMEM
    heads = (H, tokens, LANES)
    scratch = [
        vmem((1, r + 16, cols), BF),
        vmem((2, r, cols), BF),
        vmem((1, r, cols), BF),
        vmem(ffn.shape, BF),
        vmem((8, LANES), F32),
        vmem((FRAMES, 8, LANES), F32),
        vmem((n_b, 1, n_z, 4, r + 16, cols), BF),
        vmem((n_b, 2, n_z, 4, r, cols), BF),
        vmem((n_b, 1, n_z, 4, r, cols), BF),
        vmem((n_b, 1, n_z, 4, r, cols_f), BF),
        vmem((n_b, 1, n_z, 4, r, cols_f), BF),
        vmem((rows, length, LANES), F32),
        vmem((rows, groups_q, 1, width), F32),
        vmem(heads, BF),
        vmem((n_s, 2, tokens, LANES), BF),
        vmem(heads, BF),
        vmem((H, 2, tokens, LANES), BF),
        vmem((rows, groups_q, width, LANES), BF),
        vmem((rows, groups_q, width, LANES), BF),
        vmem((rows * groups_q, 1, width), F32),
        vmem((rows * groups_q, HD + 16, width), F32),
        vmem((groups_q, LANES, width), F32),
        vmem((rows * groups_q, 1, width), F32),
        vmem((rows * groups_q, 1, width), F32),
        vmem(heads, BF),
        vmem(heads, BF),
        vmem(heads, BF),
        vmem(heads, BF),
        vmem((tiles, count, wide), BF),
        vmem((tiles, count, wide), F32),
        vmem((tiles, count, wide), BF),
        vmem((count, D), F32),
        vmem((FRAMES, 8, LANES), F32),
        vmem((groups_q, LANES, width), F32),
        vmem((H, parts, 2, tokens, LANES), BF),
        vmem((parts - 1, H, 2, tokens, LANES), BF),
        vmem((H, 2, tokens, LANES), BF),
        vmem(heads, BF),
        vmem(heads, BF),
        vmem((H, 2, tokens, LANES), BF),
        vmem((n_b, 1, n_z, 2, 2, r, cols), BF),
        vmem((n_b, 1, n_z, 2, 2, r, cols_f), BF),
        vmem((n_b, 1, n_z, 2, 2, r, cols_f), BF),
        vmem((n_b, 2, n_z, 2, 2, r, cols), BF),
        vmem((n_b, 1, n_z, 2, 2, r, cols), BF),
        vmem((n_b, 1, n_z, 2, 2, 8, LANES), F32),
        vmem((4, pad, LANES), F32),
        vmem((n_b, 4, r + 8, LANES), F32),
        vmem((n_z, pad + 8, LANES), F32),
        vmem((n_s, 8, LANES), F32),
        vmem((n_b, r, LANES), F32),
        vmem((n_b, n_s, 1, LANES), F32),
        vmem((n_b * n_s, 1, LANES), F32),
        vmem(tok.shape, BF),
        vmem(tok.shape, BF),
        vmem(attn.shape, F32),
        vmem(ffn.shape, F32),
        vmem(attn.shape, F32),
        vmem(ffn.shape, F32),
    ]
    scratch += scatter_scratch(n_b, 1, n_z, r, cols_f, BF) * 2
    scratch += scatter_scratch(n_b, 1, n_z, r, cols, BF)
    scratch += scatter_scratch(n_b, 2, n_z, r, cols, BF)
    scratch += short_scratch(n_b, 1, n_z, r, cols, BF)
    scratch += short_scratch(n_b, 1, n_z, 8, LANES, F32)
    dma = pltpu.SemaphoreType.DMA
    scratch += [dma((copies,)), dma((copies,)), dma((11,))]
    return pl.pallas_call(
        layer_kernel,
        out_shape=out,
        in_specs=[SMEM_SPEC] + [VMEM_SPEC] * 11,
        out_specs=(pl.BlockSpec(memory_space=pl.ANY),) * 6 + (VMEM_SPEC,) * 5,
        scratch_shapes=scratch,
        compiler_params=pltpu.CompilerParams(
            vmem_limit_bytes=63 * 2**20, collective_id=0, has_side_effects=True
        ),
    )(groups, lengths, tok, cot, attn, ffn, params, arows, acols, frows, fcols, sq)


def result_kernel(
    out_in, du_in, agrad_in, fgrad_in, update_a, update_f, scales_ref, rows_ref, acols_in, fcols_in, own_ref,
    attn_ref, ffn_ref,
    out_ref, du_ref, agrad_ref, fgrad_ref, grad_ref, anew_ref, fnew_ref, new_ref, acopy_ref, fcopy_ref, copy_ref,
    arows_ref, acols_ref, frows_ref, fcols_ref, sq_ref,
):
    for src, dst in ((out_in, out_ref), (du_in, du_ref), (agrad_in, agrad_ref), (fgrad_in, fgrad_ref)):
        dst[...] = src[...]
    for j in range(4):
        new = attn_ref[j] - scales_ref[0:1, j : j + 1] * update_a[j]
        anew_ref[j] = new
        acopy_ref[j] = new.astype(BF)
    for j in range(2):
        new = ffn_ref[j] - scales_ref[0:1, 4 + j : 5 + j] * update_f[j]
        fnew_ref[j] = new
        fcopy_ref[j] = new.astype(BF)
    rows = rows_ref[...].T
    arows_ref[...] = rows[0:4]
    frows_ref[...] = rows[4:6]
    acols_ref[...] = acols_in[...]
    fcols_ref[...] = fcols_in[...]
    chunk = grad_ref.shape[0]
    at = own_place(chunk)
    grad_ref[...] = from_frame(own_ref[0], at, chunk).reshape(chunk)
    new = from_frame(own_ref[1], at, chunk)
    new_ref[...] = new.reshape(chunk)
    copy_ref[...] = new.astype(BF).reshape(chunk)
    sq_ref[...] = from_frame(own_ref[2], at, chunk).reshape(chunk)


def result_part(made, attn, ffn, chunk):
    out, _, agrad, fgrad, _, _, _, rows, acols, fcols, _ = made
    r = rows.shape[0]

    def shape(dims, kind):
        return jax.ShapeDtypeStruct(dims, kind)

    shapes = (
        shape(out.shape, BF),
        shape(out.shape, BF),
        shape(attn.shape, F32),
        shape(ffn.shape, F32),
        shape((chunk,), F32),
        shape(attn.shape, F32),
        shape(ffn.shape, F32),
        shape((chunk,), F32),
        shape(attn.shape, BF),
        shape(ffn.shape, BF),
        shape((chunk,), BF),
        shape((4, r), F32),
        shape(acols.shape, F32),
        shape((2, r), F32),
        shape(fcols.shape, F32),
        shape((chunk,), F32),
    )
    return pl.pallas_call(
        result_kernel,
        out_shape=shapes,
        in_specs=[VMEM_SPEC] * 13,
        out_specs=(VMEM_SPEC,) * 16,
        compiler_params=pltpu.CompilerParams(vmem_limit_bytes=60 * 2**20),
    )(*made, attn, ffn)


def shards(
    tokens, lengths, groups, cotangent, attn_weights, ffn_weights, small_params,
    attn_rows, attn_cols, ffn_rows, ffn_cols, small_sq,
):
    micro, rb, toks, _ = tokens.shape
    rows = micro * rb
    chunk = small_params.shape[0]
    made = layer_part(
        groups.reshape(rows),
        lengths.reshape(rows, SEGS),
        tokens.reshape(rows * toks, D),
        cotangent.reshape(rows * toks, D),
        attn_weights,
        ffn_weights,
        small_params,
        attn_rows,
        attn_cols,
        ffn_rows,
        ffn_cols,
        small_sq,
    )
    results = list(result_part(made, attn_weights, ffn_weights, chunk))
    for i in (0, 1):
        results[i] = results[i].reshape(tokens.shape)
    return tuple(results)


def solution(mesh):
    acts = P(None, "batch", "seq", None)
    weights = P(None, "seq", "batch")
    small = P(("seq", "batch"))
    rows, cols = P(None, "seq"), P(None, "batch")
    return jax.shard_map(
        shards,
        mesh=mesh,
        in_specs=(acts, P(None, "batch", None), P(None, "batch"), acts, weights, weights, small)
        + (rows, cols, rows, cols, small),
        out_specs=(acts, acts, weights, weights, small, weights, weights, small, weights, weights, small)
        + (rows, cols, rows, cols, small),
        check_vma=False,
    )
```

```python
import functools

import jax
import jax.numpy as jnp
from jax import lax
from jax.experimental import pallas as pl
from jax.experimental.pallas import tpu as pltpu
from jax.sharding import PartitionSpec as P

D = 512
H = 8
HD = 64
FF = 2048
GROUPS = 8
SEGS = 64
STEP = 10
NVEC = 10240
LANES = 128

NEG = -1e30
EPS = 1e-05
EPS_ONE = 1e-30
LEARN = 1.0
DECAY = 1.0 - STEP ** (-0.8)
SCALE = HD ** (-0.5)
LOG2E = 1.4426950408889634
FRAMES = 16
FRAME_ROWS = NVEC // FRAMES // LANES
GROUP = 4
BF = jnp.bfloat16
F32 = jnp.float32
VMEM_SPEC = pl.BlockSpec(memory_space=pltpu.VMEM)
SMEM_SPEC = pl.BlockSpec(memory_space=pltpu.SMEM)

ROW_BQ, ROW_BV, ROW_BO, ROW_B1, ROW_B2 = 0, 4, 8, 12, 28
ROW_G1, ROW_S1, ROW_G2, ROW_S2, ROW_E = 32, 36, 40, 44, 48


def mm(a, b):
    return lax.dot_general(a, b, (((1,), (0,)), ((), ())), preferred_element_type=F32)


def mm_nt(a, b):
    return lax.dot_general(a, b, (((1,), (1,)), ((), ())), preferred_element_type=F32)


def mm_tn(a, b):
    return lax.dot_general(a, b, (((0,), (0,)), ((), ())), preferred_element_type=F32)


def small_piece(small_ref, row, count):
    parts = [small_ref[r // FRAME_ROWS, pl.ds(r % FRAME_ROWS, 1), :] for r in range(row, row + count)]
    return jnp.concatenate(parts, axis=1)


def add_small(ref, row, values):
    for k in range(values.shape[1] // LANES):
        r = row + k
        ref[r // FRAME_ROWS, pl.ds(r % FRAME_ROWS, 1), :] += values[:, k * LANES : (k + 1) * LANES]


def low_half():
    return lax.broadcasted_iota(jnp.int32, (1, LANES), 1) < HD


def swap_halves(x):
    return pltpu.roll(x, HD, 1)


def heads_to_rows(tiles):
    low = low_half()
    first, second = [], []
    for j in range(H // 2):
        a, b = tiles[2 * j], tiles[2 * j + 1]
        first.append(jnp.where(low, a, swap_halves(b)))
        second.append(jnp.where(low, swap_halves(a), b))
    return jnp.concatenate(first, axis=1), jnp.concatenate(second, axis=1)


def rows_to_heads(first, second):
    low = low_half()
    tiles = []
    for j in range(H // 2):
        a = first[:, j * LANES : (j + 1) * LANES]
        b = second[:, j * LANES : (j + 1) * LANES]
        tiles.append(jnp.where(low, a, swap_halves(b)))
        tiles.append(jnp.where(low, swap_halves(a), b))
    return tiles


def wrap(value, count):
    return value - jnp.where(value >= count, count, 0)


def outwards(count):
    return sorted(range(1, count), key=lambda k: (abs(2 * k - count), k))


class Place:
    def __init__(self):
        self.n_s, self.n_b = lax.axis_size("seq"), lax.axis_size("batch")
        self.s, self.b = lax.axis_index("seq"), lax.axis_index("batch")
        self.n_z, self.parts = self.n_s // 4, self.n_s // H
        self.z, self.xc = self.s // 4, self.s % 4
        self.x, self.c = self.xc // 2, self.xc % 2
        self.other_x = (1 - self.x) * 2 + self.c
        self.other_c = self.x * 2 + 1 - self.c
        self.h, self.g = self.s // self.parts, self.s % self.parts
        self.z_ahead = [wrap(self.z + k, self.n_z) for k in range(self.n_z)]
        self.b_ahead = [wrap(self.b + k, self.n_b) for k in range(self.n_b)]
        self.xc_ahead = [wrap(self.xc + k, 4) for k in range(4)]
        self.h_ahead = [wrap(self.h + k, H) for k in range(H)]
        self.g_ahead = [wrap(self.g + k, self.parts) for k in range(self.parts)]
        self.z_pair = self.z + 1 - self.z % 2 * 2
        self.z_pair_ahead = [wrap(self.z_pair + k, self.n_z) for k in range(self.n_z)]
        self.at_z = [z * 4 + self.xc for z in self.z_ahead]
        self.at_x, self.at_core = self.z * 4 + self.other_x, self.z * 4 + self.other_c
        self.at_head = [h * self.parts + self.g for h in self.h_ahead]
        self.at_part = [self.h * self.parts + g for g in self.g_ahead]

    def along_z(self, k):
        return (self.at_z[k], self.b)

    def across_z(self):
        return (self.z_pair * 4 + self.xc, self.b)

    def across_x(self):
        return (self.at_x, self.b)

    def across_core(self):
        return (self.at_core, self.b)

    def batch_ahead(self, k):
        return self.b_ahead[k]

    def batch_behind(self, k):
        return self.b_ahead[(self.n_b - k) % self.n_b]

    def across_batch(self, k):
        return (self.s, self.b_ahead[k])

    def head_ahead(self, k):
        return self.h_ahead[k % H] if isinstance(k, int) else wrap(self.h + k, H)

    def head_behind(self, k):
        return self.h_ahead[(H - k) % H] if isinstance(k, int) else wrap(self.h + H - k, H)

    def across_heads(self, k):
        return (self.at_head[k] if isinstance(k, int) else self.head_ahead(k) * self.parts + self.g, self.b)

    def part_ahead(self, k):
        return self.g_ahead[k]

    def across_parts(self, k):
        return (self.at_part[k], self.b)


def greet(peers):
    barrier = pltpu.get_barrier_semaphore()
    for peer in peers:
        pl.semaphore_signal(barrier, inc=1, device_id=peer, device_id_type=pl.DeviceIdType.MESH)
    pl.semaphore_wait(barrier, len(peers))


def greet_all(place):
    barrier = pltpu.get_barrier_semaphore()

    def hello(b, i, carry):
        peer = (wrap(place.s + i, place.n_s), b)
        pl.semaphore_signal(barrier, inc=1, device_id=peer, device_id_type=pl.DeviceIdType.MESH)
        return carry

    for k, b in enumerate(place.b_ahead):
        lax.fori_loop(0 if k else 1, place.n_s, functools.partial(hello, b), 0)
    return lambda: pl.semaphore_wait(barrier, place.n_s * place.n_b - 1)


def far_first(i):
    if isinstance(i, int) and i in (0, H):
        return i
    return H // 2 + i // 2 * (1 - i % 2 * 2)


class Copy:
    def __init__(self, wire, i, build):
        self.wire, self.i, self.build = wire, i, build

    def made(self):
        return self.wire.make(self.i, *self.build())

    def start(self):
        self.made().start()

    def wait_recv(self):
        self.made().wait_recv()

    def wait_send(self):
        self.made().wait_send()


class Wire:
    def __init__(self, send_sems, recv_sems):
        self.send_sems, self.recv_sems, self.copies, self.used = send_sems, recv_sems, [], 0

    def reserve(self, count):
        self.used += count
        return self.used - count

    def make(self, i, src, dst, peer):
        return pltpu.make_async_remote_copy(
            src_ref=src,
            dst_ref=dst,
            send_sem=self.send_sems.at[i],
            recv_sem=self.recv_sems.at[i],
            device_id=peer,
            device_id_type=pl.DeviceIdType.MESH,
        )

    def plan(self, build):
        return Copy(self, self.reserve(1), build)

    def send(self, build):
        copy = self.plan(build)
        copy.start()
        self.copies.append(copy)
        return copy

    def drain(self):
        for copy in self.copies:
            copy.wait_send()
        self.copies = []


def received(copies):
    for copy in copies:
        copy.wait_recv()


class Gather:
    def __init__(self, place, wire, src, dst, own_sem, cut):
        self.place, self.wire, self.src, self.dst, self.cut, self.own_sem = place, wire, src, dst, cut, own_sem
        self.own().start()
        self.begin()

    def begin(self):
        p = self.place
        self.along = [self.wire.send(lambda k=k: (self.src, self.slot(p.z), p.along_z(k))) for k in range(1, p.n_z)]

    def slot(self, z):
        return self.dst.at[self.place.b, :, z, self.place.xc]

    def own(self):
        return pltpu.make_async_copy(self.src, self.slot(self.place.z), self.own_sem)

    def forward(self, part, *peers):
        return [self.wire.send(lambda peer=peer: (part(), part(), peer())) for peer in peers]

    def column(self, b, xc):
        return lambda: self.dst.at[b(), :, :, xc]

    def half(self, b, xc, second):
        span = pl.ds(self.cut, self.place.n_z - self.cut) if second else pl.ds(0, self.cut)
        return lambda: self.dst.at[b(), :, span, xc]

    def batch_peers(self):
        return [lambda k=k: self.place.across_batch(k) for k in range(1, self.place.n_b)]

    def to_plane(self):
        p = self.place
        self.own().wait()
        received(self.along)
        peers = [p.across_x, p.across_core] + self.batch_peers()
        self.plane = self.forward(self.column(lambda: p.b, p.xc), *peers)

    def to_diagonal(self):
        p = self.place
        self.plane[0].wait_recv()
        self.diagonal = self.forward(self.half(lambda: p.b, p.other_x, 0), *self.batch_peers())
        self.cores = [self.plane[1]] + self.forward(self.column(lambda: p.b, p.other_x), p.across_core)
        for k in range(1, p.n_b):
            b = lambda k=k: p.batch_behind(k)
            self.plane[1 + k].wait_recv()
            self.diagonal += self.forward(self.half(b, p.xc, 1), p.across_x)
            self.cores += self.forward(self.column(b, p.xc), p.across_core)

    def to_cores(self):
        p = self.place
        for k in range(1, p.n_b):
            for second in range(2):
                self.diagonal[(p.n_b - 1) * second + k - 1].wait_recv()
                part = self.half(lambda k=k: p.batch_behind(k), p.other_x, second)
                self.cores += self.forward(part, p.across_core)

    def finish(self):
        received(self.cores)


class PairGather(Gather):

    def begin(self):
        p, self.far = self.place, range(2, self.place.n_z, 2)
        self.along = [self.wire.send(lambda: (self.src, self.slot(p.z), p.across_z()))]
        self.arriving = [self.wire.send(lambda k=k: (self.src, self.slot(p.z), p.along_z(k))) for k in self.far]

    def to_pair(self):
        p = self.place
        for copy, k in zip(self.arriving, self.far):
            copy.wait_recv()
            z = p.z_ahead[p.n_z - k]
            self.along.append(self.wire.send(lambda z=z: (self.slot(z), self.slot(z), p.across_z())))


class ShortGather(Gather):
    def to_plane(self):
        p = self.place
        self.own().wait()
        received(self.along)
        diagonal = [
            lambda k=k: (p.z * 4 + p.other_x, p.batch_ahead(k)) for k in range(1, p.n_b)
        ]
        peers = [p.across_core, p.across_x] + self.batch_peers() + diagonal
        self.plane = self.forward(self.column(lambda: p.b, p.xc), *peers)

    def to_cores(self):
        p = self.place
        behind = [lambda k=k: p.batch_behind(k) for k in range(1, p.n_b)]
        columns = [(lambda: p.b, p.other_x)] + [(b, p.xc) for b in behind] + [(b, p.other_x) for b in behind]
        self.cores = [self.plane[0]]
        for copy, (b, xc) in zip(self.plane[1:], columns):
            copy.wait_recv()
            self.cores += self.forward(self.column(b, xc), p.across_core)


def normed_of(values):
    center = values - jnp.mean(values, axis=-1, keepdims=True)
    inverse = lax.rsqrt(jnp.mean(center * center, axis=-1, keepdims=True) + EPS)
    return center * inverse, inverse


def norm_back(grad_norm, normed, inverse):
    return inverse * (
        grad_norm
        - jnp.mean(grad_norm, axis=-1, keepdims=True)
        - normed * jnp.mean(grad_norm * normed, axis=-1, keepdims=True)
    )


def gelu_pair(z):
    c = 0.7978845608028654
    z2 = z * z
    t = jnp.tanh(c * z * (1.0 + 0.044715 * z2))
    half = 0.5 * (1.0 + t)
    slope = half + 0.5 * z * (1.0 - t * t) * (c * (1.0 + 3 * 0.044715 * z2))
    return z * half, slope


def language_rows(groups_ref, small_ref, rows):
    table = [small_piece(small_ref, ROW_E + 4 * e, 4) for e in range(GROUPS)]
    out = []
    for m in range(rows):
        acc = jnp.zeros_like(table[0])
        for e in range(GROUPS):
            acc = acc + jnp.where(groups_ref[m] == e, table[e], 0.0)
        out.append(acc)
    return out


def column_sum(x):
    return jnp.sum(x, axis=0, keepdims=True)


class Scatter:
    def __init__(self, place, wire, part, core, acc, far, near, plane_x, plane_b, column):
        self.begin(place, wire, part, core, acc, column)
        self.far, self.near, self.plane_x, self.plane_b = far, near, plane_x, plane_b
        self.cut = far.shape[2]

    def begin(self, place, wire, part, core, acc, column):
        self.place, self.wire = place, wire
        self.part, self.core, self.acc, self.column = part, core, acc, column
        self.kind = part.dtype
        self.x, self.c = place.x, place.c
        self.slabs = part.shape[1]

    def add(self, target, *others):
        total = target[...].astype(F32)
        for other in others:
            total = total + other[...].astype(F32)
        target[...] = total.astype(self.kind)

    def each(self, body, first=0, last=None):
        for j in range(self.slabs):

            def step(z, carry, j=j):
                body(j, z)
                return carry

            lax.fori_loop(first, self.place.n_z if last is None else last, step, 0)

    def to_core(self):
        p = self.place
        self.moved = [self.wire.send(lambda: (self.part.at[:, :, :, :, 1 - self.c], self.core, p.across_core()))]

    def join(self):
        p = self.place
        received(self.moved)
        for j in range(self.slabs):

            def body(b, carry, j=j):
                def at_z(z, carry):
                    for x in range(2):
                        total = self.part[b, j, z, x, self.c].astype(F32) + self.core[b, j, z, x].astype(F32)
                        self.acc[b, j, z, x] = total.astype(self.kind)
                    return carry

                return lax.fori_loop(0, p.n_z, at_z, carry)

            lax.fori_loop(0, p.n_b, body, 0)

    def to_diagonal(self):
        p = self.place
        self.join()
        cut, rest = pl.ds(0, self.cut), pl.ds(self.cut, p.n_z - self.cut)
        self.moved_far, self.moved_near = [], []
        for k in range(1, p.n_b):
            diagonal = lambda k=k: self.acc.at[p.batch_ahead(k), :, :, 1 - self.x]
            self.moved_far.append(
                self.wire.send(
                    lambda k=k, part=diagonal: (part().at[:, cut], self.far.at[k - 1], p.across_batch(k))
                )
            )
            self.moved_near.append(
                self.wire.send(lambda k=k, part=diagonal: (part().at[:, rest], self.near.at[k - 1], p.across_x()))
            )

    def to_plane(self):
        p = self.place
        for k in range(1, p.n_b):
            self.moved_near[k - 1].wait_recv()
            self.each(
                lambda j, z, k=k: self.add(
                    self.acc.at[p.batch_ahead(k), j, z, self.x], self.near.at[k - 1, j, z - self.cut]
                ),
                self.cut,
            )
        received(self.moved_far)
        self.each(
            lambda j, z: self.add(
                self.acc.at[p.b, j, z, 1 - self.x], *[self.far.at[k - 1, j, z] for k in range(1, p.n_b)]
            ),
            0,
            self.cut,
        )
        self.moved = [self.wire.send(lambda: (self.acc.at[p.b, :, :, 1 - self.x], self.plane_x, p.across_x()))]
        self.moved += [
            self.wire.send(
                lambda k=k: (
                    self.acc.at[p.batch_ahead(k), :, :, self.x],
                    self.plane_b.at[k - 1],
                    p.across_batch(k),
                )
            )
            for k in range(1, p.n_b)
        ]

    def others(self, j, z):
        return [self.plane_x.at[j, z]] + [self.plane_b.at[k - 1, j, z] for k in range(1, self.place.n_b)]

    def to_owner(self):
        p = self.place
        received(self.moved)
        self.each(lambda j, z: self.add(self.acc.at[p.b, j, z, self.x], *self.others(j, z)))
        self.moved = [
            self.wire.send(
                lambda k=k: (
                    self.acc.at[p.b, :, p.z_ahead[k], self.x],
                    self.column.at[k - 1],
                    p.along_z(k),
                )
            )
            for k in range(1, p.n_z)
        ]

    def total(self, j):
        p = self.place
        out = self.acc[p.b, j, p.z, self.x].astype(F32)
        for k in range(1, p.n_z):
            out = out + self.column[k - 1, j].astype(F32)
        return out

    def finish(self):
        received(self.moved)


class PairScatter(Scatter):

    def to_owner(self):
        p = self.place
        received(self.moved)
        self.each(lambda j, z: self.add(self.acc.at[p.b, j, z, self.x], *self.others(j, z)))
        self.moved = [
            self.wire.send(
                lambda i=i: (
                    self.acc.at[p.b, :, p.z_pair_ahead[2 * i], self.x],
                    self.column.at[i],
                    p.across_z(),
                )
            )
            for i in range(p.n_z // 2)
        ]

    def to_far(self):
        p = self.place
        half = p.n_z // 2
        received(self.moved)
        for i in range(half):
            for j in range(self.slabs):
                self.add(self.acc.at[p.b, j, p.z_ahead[2 * i], self.x], self.column.at[i, j])
        self.moved = [
            self.wire.send(
                lambda i=i: (
                    self.acc.at[p.b, :, p.z_ahead[2 * i], self.x],
                    self.column.at[half + i - 1],
                    p.along_z(2 * i),
                )
            )
            for i in range(1, half)
        ]

    def total(self, j):
        p = self.place
        out = self.acc[p.b, j, p.z, self.x].astype(F32)
        for k in range(p.n_z // 2, p.n_z - 1):
            out = out + self.column[k, j].astype(F32)
        return out


class ShortScatter(Scatter):
    def __init__(self, place, wire, part, core, acc, plane, column):
        self.begin(place, wire, part, core, acc, column)
        self.plane = plane

    def to_plane(self):
        p = self.place
        self.join()
        self.moved = []
        for k in range(p.n_b):
            for dx in range(2):
                if k or dx:

                    def build(k=k, dx=dx, slot=len(self.moved)):
                        x = self.x if dx == 0 else 1 - self.x
                        to = p.z * 4 + (p.other_x if dx else p.xc)
                        b = p.batch_ahead(k)
                        return (self.acc.at[b, :, :, x], self.plane.at[slot], (to, b))

                    self.moved.append(self.wire.send(build))

    def others(self, j, z):
        return [self.plane.at[k, j, z] for k in range(2 * self.place.n_b - 1)]


def short_scratch(n_b, slabs, n_z, r, cols, kind):
    return [
        pltpu.VMEM((n_b, slabs, n_z, 2, r, cols), kind),
        pltpu.VMEM((n_b, slabs, n_z, 2, r, cols), kind),
        pltpu.VMEM((2 * n_b - 1, slabs, n_z, r, cols), kind),
        pltpu.VMEM((n_z - 1, slabs, r, cols), kind),
    ]


def scatter_scratch(n_b, slabs, n_z, r, cols, kind):
    return [
        pltpu.VMEM((n_b, slabs, n_z, 2, r, cols), kind),
        pltpu.VMEM((n_b, slabs, n_z, 2, r, cols), kind),
        pltpu.VMEM((n_b - 1, slabs, n_z - n_z // 4, r, cols), kind),
        pltpu.VMEM((n_b - 1, slabs, n_z // 4, r, cols), kind),
        pltpu.VMEM((slabs, n_z, r, cols), kind),
        pltpu.VMEM((n_b - 1, slabs, n_z, r, cols), kind),
        pltpu.VMEM((n_z - 1, slabs, r, cols), kind),
    ]


SCATTER_SCRATCH, SHORT_SCRATCH = 7, 4
SLABS = 6


def lanes_of(values):
    lane = lax.broadcasted_iota(jnp.int32, (8, LANES), 1)
    row = lax.broadcasted_iota(jnp.int32, (8, LANES), 0)
    tile = jnp.zeros((8, LANES), F32)
    for j, value in enumerate(values):
        if value is not None:
            tile = tile + jnp.where((lane == j) & (row == 0), value, 0.0)
    return tile


def sum_all(x):
    return jnp.sum(jnp.sum(x, axis=1, keepdims=True), axis=0, keepdims=True)


def to_frame(values, at):
    wide = jnp.concatenate([values, jnp.zeros((1, 8 * LANES - values.shape[1]), F32)], axis=1)
    wide = pltpu.roll(wide, at, 1)
    return jnp.concatenate([wide[:, k * LANES : (k + 1) * LANES] for k in range(8)], axis=0)


def from_frame(tile, at, chunk):
    wide = jnp.concatenate([tile[k : k + 1] for k in range(8)], axis=1)
    return pltpu.roll(wide, 8 * LANES - at, 1)[:, :chunk]


def own_place(chunk):
    index = lax.axis_index("seq") * lax.axis_size("batch") + lax.axis_index("batch")
    return lax.rem(index * chunk, FRAME_ROWS * LANES)


def segment_ids(lengths, idk_ref, idq_ref, place, tokens):
    rows, length = idk_ref.shape[0], idk_ref.shape[1]
    upto = lax.broadcasted_iota(jnp.int32, (SEGS, LANES), 0) <= lax.broadcasted_iota(jnp.int32, (SEGS, LANES), 1)
    upto = jnp.where(upto, 1.0, 0.0).astype(BF)
    values = lengths.astype(F32)
    high = jnp.floor(values * (1.0 / 64))
    low = (values - 64.0 * high).astype(BF)
    high = high.astype(BF)
    ends = mm(high, upto) * 64.0 + mm(low, upto)
    ends = jnp.where(lax.broadcasted_iota(jnp.int32, (rows, LANES), 1) < SEGS, ends, 1e9)
    upto = upto[:, :SEGS]
    ends_down = lax.dot_general(upto, high, (((0,), (1,)), ((), ())), preferred_element_type=F32) * 64.0
    ends_down = ends_down + lax.dot_general(upto, low, (((0,), (1,)), ((), ())), preferred_element_type=F32)
    ones = jnp.ones((LANES, LANES), BF)
    span = 256
    for m in range(rows):

        def fill(i, carry, m=m):
            at = pl.multiple_of(i * span, span)
            places = (at + lax.broadcasted_iota(jnp.int32, (span, LANES), 0)).astype(F32)
            passed = jnp.where(ends[m : m + 1] <= places, 1.0, 0.0).astype(BF)
            seg = mm(passed, ones)
            idk_ref[m, pl.ds(at, span), :] = jnp.where(seg < SEGS, seg, SEGS + places)
            return carry

        lax.fori_loop(0, length // span, fill, 0)
        for h in range(H):
            first = ((h * place.parts + place.g) * tokens + lax.broadcasted_iota(jnp.int32, (1, tokens), 1)).astype(F32)
            seg = column_sum(jnp.where(ends_down[:, m : m + 1] <= first, 1.0, 0.0))
            group, k = h // GROUP, h % GROUP
            idq_ref[m, group, :, k * tokens : (k + 1) * tokens] = jnp.where(seg < SEGS, seg, SEGS + first)


def layer_kernel(
    groups_ref, lengths_ref, tok_ref, cot_ref, attn_ref, ffn_ref, params_ref, arows_ref, acols_ref, frows_ref,
    fcols_ref, sq_ref,
    out_hbm, du_hbm, agrad_hbm, fgrad_hbm, update_a_hbm, update_f_hbm, scales_ref, rows_new_ref, acols_new_ref,
    fcols_new_ref, own_new_ref,
    *scratch,
):
    place = Place()
    scratch = list(scratch)
    own_sems, recv_sems, send_sems = scratch.pop(), scratch.pop(), scratch.pop()
    wire = Wire(send_sems, recv_sems)

    def take(count):
        taken = scratch[:count]
        del scratch[:count]
        return taken

    pack_low, kv_low, wo_low, ffn_low, own_ref, small_ref, pack_ref, wkv_ref, wo_ref, w1_ref, w2_ref = take(11)
    idk_ref, idq_ref, q_ref, kv_ref, qsend_ref, kvsend_ref, qm_ref, dom_ref = take(8)
    peak_ref, acc_ref, ot_ref, lse_ref, delta_ref, o_ref, otile_ref, dotile_ref, do_ref = take(9)
    act_ref, slope_ref, dz_ref, sum_ref, frames_ref = take(5)
    dqt_ref, part_ref, near_ref, dkv_sum, dq_ref, dq_back, dkv_back = take(7)
    dwo_ref, dw1_ref, dw2_ref, dkv_w_ref, dq_w_ref, dsmall_ref = take(6)
    cols_plane, rows_plane, all_z, late_cols, late_rows, late_sums, all_sums = take(7)
    out_ref, du_ref, agrad_ref, fgrad_ref, update_a, update_f = take(6)
    written = [
        pltpu.make_async_copy(src, dst, own_sems.at[5 + i])
        for i, (src, dst) in enumerate(
            (
                (out_ref, out_hbm),
                (du_ref, du_hbm),
                (agrad_ref, agrad_hbm),
                (fgrad_ref, fgrad_hbm),
                (update_a, update_a_hbm),
                (update_f, update_f_hbm),
            )
        )
    ]
    n_z, n_b, parts = place.n_z, place.n_b, place.parts
    rows = 2
    count = tok_ref.shape[0]
    tokens = count // rows
    r, cols = attn_ref.shape[1:]
    cols_f = ffn_ref.shape[2]
    groups = H // GROUP
    width = GROUP * tokens
    keys = parts * tokens
    scale2 = SCALE * LOG2E
    low = low_half()

    plane = [(dx, db) for db in range(n_b) for dx in range(4) if dx or db]

    def plane_peer(dx, db):
        return (place.z * 4 + place.xc_ahead[dx], place.batch_ahead(db))

    along = [place.along_z(k) for k in range(1, n_z)]
    all_here = greet_all(place)

    chunk = params_ref.shape[0]
    own_at = own_place(chunk)
    own = to_frame(params_ref[...].reshape(1, chunk), own_at)
    own_ref[...] = own
    pack_low[0, :r] = attn_ref[0].astype(BF)
    tile = jnp.concatenate([own, jnp.zeros((8, LANES), F32)], axis=0)
    if cols < LANES:
        tile = jnp.concatenate([own[:, :cols], own[:, cols:]], axis=0)
    if cols > LANES:
        tile = jnp.concatenate([tile, jnp.zeros((16, cols - LANES), F32)], axis=1)
    pack_low[0, r:] = tile.astype(BF)
    kv_low[...] = attn_ref[1:3].astype(BF)
    all_here()
    pack = ShortGather(place, wire, pack_low, pack_ref, own_sems.at[0], n_z)
    kv_w = ShortGather(place, wire, kv_low, wkv_ref, own_sems.at[4], n_z)
    wo_low[0] = attn_ref[3].astype(BF)
    ffn_low[...] = ffn_ref[...].astype(BF)
    segment_ids(lengths_ref[...], idk_ref, idq_ref, place, tokens)
    for i in range(rows * groups):
        peak_ref[i] = jnp.full((1, width), NEG, F32)
        acc_ref[i] = jnp.zeros((HD + 16, width), F32)
    frames_ref[...] = jnp.zeros_like(frames_ref)
    dqt_ref[...] = jnp.zeros_like(dqt_ref)
    pack.to_plane()
    kv_w.to_plane()
    most = n_z - n_z // 4
    first = PairGather(place, wire, ffn_low.at[pl.ds(0, 1)], w1_ref, own_sems.at[1], most)
    out_w = PairGather(place, wire, wo_low, wo_ref, own_sems.at[2], most)
    second = PairGather(place, wire, ffn_low.at[pl.ds(1, 1)], w2_ref, own_sems.at[3], most)
    pack.to_cores()
    pack.finish()
    frame = place.n_s * n_b // FRAMES
    for f in range(FRAMES):
        total = None
        for i in range(f * frame, (f + 1) * frame):
            s, b = i // n_b, i % n_b
            tile = pack_ref[b, 0, s // 4, s % 4, r:].astype(F32)
            if cols < LANES:
                tile = jnp.concatenate([tile[:8], tile[8:]], axis=1)
            tile = tile[:8, :LANES]
            total = tile if total is None else total + tile
        small_ref[f] = total
    lang = language_rows(groups_ref, small_ref, rows)
    first.to_pair()
    out_w.to_pair()

    def inputs():
        return jnp.concatenate(
            [tok_ref[m * tokens : (m + 1) * tokens].astype(F32) + lang[m] for m in range(rows)], axis=0
        )

    def w_qkv(b, j):
        w = wkv_ref[b, j - 1] if j else pack_ref[b, 0, :, :, :r]
        return w.reshape(D, cols)

    a = inputs().astype(BF)

    def project(j, bias):
        out = jnp.concatenate([mm(a, w_qkv(b, j)) for b in range(n_b)], axis=1)
        if bias is not None:
            out = out + small_piece(small_ref, bias, 4)
        return [t.astype(BF) for t in rows_to_heads(out[:tokens], out[tokens:])]

    for h, t in enumerate(project(0, ROW_BQ)):
        qsend_ref[h] = t
    q_ref[place.h] = qsend_ref[place.h]
    def to_heads(src, dst):
        return [
            wire.send(lambda k=k: (src.at[place.head_ahead(k)], dst.at[place.h], place.across_heads(k)))
            for k in outwards(H)
        ]

    moved_q = to_heads(qsend_ref, q_ref)
    second.to_pair()
    kv_w.to_cores()
    first.to_plane()
    out_w.to_plane()
    kv_w.finish()
    for j, bias in ((0, None), (1, ROW_BV)):
        for h, t in enumerate(project(1 + j, bias)):
            kvsend_ref[h, j] = t
    kv_ref[place.s] = kvsend_ref[place.h]
    kv_sems = wire.reserve(H)
    share_sems = wire.reserve(H * (parts - 1))

    def moved_kv(i):
        k = far_first(i)
        return wire.make(
            kv_sems + i, kvsend_ref.at[place.head_ahead(k)], kv_ref.at[place.s], place.across_heads(k)
        )

    def ordered(i):
        return far_first(i) if isinstance(i, int) else jnp.where(i == 0, 0, far_first(i))

    def shared_kv(i, j):
        slot = kv_ref.at[place.head_behind(ordered(i)) * parts + place.g]
        return wire.make(share_sems + i * (parts - 1) + j - 1, slot, slot, place.across_parts(j))

    for j in range(1, parts):
        shared_kv(0, j).start()
    for k in range(1, H):
        moved_kv(k).start()
    second.to_plane()

    def masked_rows(src_ref, dst_ref):
        for g in range(groups):
            both = src_ref[g * GROUP : (g + 1) * GROUP].reshape(width, LANES)
            zero = jnp.zeros_like(both)
            dst_ref[0, g] = jnp.where(low, both, zero)
            dst_ref[1, g] = jnp.where(low, zero, both)

    received(moved_q)
    masked_rows(q_ref, qm_ref)

    def pair(h):
        kv = kv_ref[pl.ds(h * parts, parts)]
        return kv[:, 0].reshape(keys, LANES), kv[:, 1].reshape(keys, LANES)

    def key_ids(h, m):
        ids = idk_ref[m, pl.ds(pl.multiple_of(h * keys, keys), keys), :]
        return jnp.concatenate([ids] * (width // LANES), axis=1)

    def attend(k):
        h = place.head_behind(ordered(k))
        ids = [key_ids(h, m) for m in range(rows)]
        for j in range(1, parts):
            shared_kv(k, j).wait_recv()
        key, value = pair(h)
        value_t = value.T
        ones = jnp.ones((16, keys), BF)
        for g in range(groups):
            for m in range(rows):
                i = g * rows + m
                s = jnp.where(ids[m] == idq_ref[m, g], mm_nt(key, qm_ref[m, g]) * scale2, NEG)
                new = jnp.maximum(peak_ref[i], jnp.max(s, axis=0, keepdims=True))
                p = jnp.exp2(s - new).astype(BF)
                alpha = jnp.exp2(peak_ref[i] - new)
                left = jnp.concatenate([value_t[m * HD : (m + 1) * HD], ones], axis=0)
                acc_ref[i] = acc_ref[i] * alpha + mm(left, p)
                peak_ref[i] = new

    def meanwhile(k, *stages):
        for at, stage in stages:
            pl.when(k == at)(stage)

    def forward_step(k, carry):
        moved_kv(k).wait_recv()
        for j in range(1, parts):
            shared_kv(k, j).start()
        attend(k - 1)
        meanwhile(
            k,
            (2, first.to_diagonal),
            (2, out_w.to_diagonal),
            (6, second.to_diagonal),
        )
        return carry

    lax.fori_loop(1, H, forward_step, 0)
    attend(H - 1)
    for g in range(groups):
        for m in range(rows):
            i = g * rows + m
            total = acc_ref[i, HD : HD + 1]
            ot_ref[g, m * HD : (m + 1) * HD] = acc_ref[i, :HD] * (1.0 / total)
            lse_ref[i] = peak_ref[i] + jnp.log2(total)
        o_ref[g * GROUP : (g + 1) * GROUP] = ot_ref[g].T.astype(BF).reshape(GROUP, tokens, LANES)
    moved = to_heads(o_ref, otile_ref)
    otile_ref[place.h] = o_ref[place.h]
    for piece in (out_w, first, second):
        piece.to_cores()

    tiles, wide = act_ref.shape[0], act_ref.shape[2]
    per_b = cols_f // wide
    bias_1 = [small_piece(small_ref, ROW_B1 + i * wide // LANES, wide // LANES) for i in range(tiles)]
    gain1, shift1 = small_piece(small_ref, ROW_G1, 4), small_piece(small_ref, ROW_S1, 4)
    gain2, shift2 = small_piece(small_ref, ROW_G2, 4), small_piece(small_ref, ROW_S2, 4)
    bias_o, bias_2 = small_piece(small_ref, ROW_BO, 4), small_piece(small_ref, ROW_B2, 4)

    def block(ref, i):
        at = i % per_b * wide
        return ref[i // per_b, 0, :, :, :, at : at + wide].reshape(D, wide)

    def joined(ref, b):
        return jnp.concatenate([ref[b * per_b + i] for i in range(per_b)], axis=1)

    live = jnp.concatenate(
        [idk_ref[m, pl.ds(pl.multiple_of(place.s * tokens, tokens), tokens), :] for m in range(rows)], axis=0
    )
    live = jnp.where(live < SEGS, 1.0, 0.0)
    u = inputs()
    out_w.finish()
    first.finish()
    received(moved)
    mixed = jnp.concatenate(heads_to_rows([otile_ref[h].astype(F32) for h in range(H)]), axis=0).astype(BF)
    attn_out = jnp.concatenate([mm(mixed, wo_ref[b, 0].reshape(D, cols)) for b in range(n_b)], axis=1)
    normed1, inverse1 = normed_of(u + (attn_out + bias_o))
    hidden = normed1 * gain1 + shift1
    hb = hidden.astype(BF)
    for i in range(tiles):
        act, slope = gelu_pair(mm(hb, block(w1_ref, i)) + bias_1[i])
        slope_ref[i] = slope
        act_ref[i] = act.astype(BF)
    second.finish()
    total = hidden + u + bias_2
    for b in range(n_b):
        total = total + mm_nt(joined(act_ref, b), w2_ref[b, 0].reshape(D, cols_f))

    normed2, inverse2 = normed_of(total)
    out_ref[...] = (normed2 * gain2 + shift2).astype(BF)
    c = cot_ref[...].astype(F32) * jnp.concatenate([live] * (D // LANES), axis=1)
    dr = norm_back(c * gain2, normed2, inverse2)
    df = dr.astype(BF)

    def scatter(part):
        return PairScatter(place, wire, part, *take(SCATTER_SCRATCH))

    g_first, g_second, g_out = scatter(dw1_ref), scatter(dw2_ref), scatter(dwo_ref)
    g_kv = Scatter(place, wire, dkv_w_ref, *take(SCATTER_SCRATCH))
    g_q = ShortScatter(place, wire, dq_w_ref, *take(SHORT_SCRATCH))
    g_small = ShortScatter(place, wire, dsmall_ref, *take(SHORT_SCRATCH))

    def weight_grad(left, right_ref, dst_ref):
        left = left.T
        for i in range(tiles):
            at = i % per_b * wide
            grad = mm(left, right_ref[i]).astype(BF).reshape(n_z, 2, 2, r, wide)
            dst_ref[i // per_b, 0, :, :, :, :, at : at + wide] = grad

    weight_grad(df, act_ref, dw2_ref)
    g_second.to_core()
    dh = dr
    for i in range(tiles):
        dz = (mm(df, block(w2_ref, i)) * slope_ref[i]).astype(BF)
        dz_ref[i] = dz
    for b in range(n_b):
        dh = dh + mm_nt(joined(dz_ref, b), w1_ref[b, 0].reshape(D, cols_f))
    dpre = norm_back(dh * gain1, normed1, inverse1)
    dattn = dpre.astype(BF)
    do = mm_nt(dattn[:, :cols], wo_ref[0, 0].reshape(D, cols))
    for b in range(1, n_b):
        do = do + mm_nt(dattn[:, b * cols : (b + 1) * cols], wo_ref[b, 0].reshape(D, cols))
    for h, t in enumerate(rows_to_heads(do[:tokens], do[tokens:])):
        dotile_ref[h] = t.astype(BF)
    moved = to_heads(dotile_ref, do_ref)
    written[0].start()
    do_ref[place.h] = dotile_ref[place.h]
    sum_ref[...] = dpre + dr

    g_second.to_diagonal()
    weight_grad(hb, dz_ref, dw1_ref)
    g_first.to_core()
    mixed_t = mixed.T
    for b in range(n_b):
        dwo = mm(mixed_t, dattn[:, b * cols : (b + 1) * cols]).astype(BF)
        dwo_ref[b, 0] = dwo.reshape(n_z, 2, 2, r, cols)
    g_out.to_core()
    for k in range(H):
        for j in range(1, parts):
            shared_kv(k, j).wait_send()
        if k:
            moved_kv(k).wait_send()
    wire.drain()

    g_first.to_diagonal()
    g_out.to_diagonal()
    add_small(frames_ref, ROW_G2, column_sum(c * normed2))
    add_small(frames_ref, ROW_S2, column_sum(c))
    add_small(frames_ref, ROW_B2, column_sum(df.astype(F32)))
    for i in range(tiles):
        add_small(frames_ref, ROW_B1 + i * wide // LANES, column_sum(dz_ref[i].astype(F32)))
    add_small(frames_ref, ROW_G1, column_sum(dh * normed1))
    add_small(frames_ref, ROW_S1, column_sum(dh))
    add_small(frames_ref, ROW_BO, column_sum(dattn.astype(F32)))
    received(moved)
    masked_rows(do_ref, dom_ref)
    g_second.to_plane()
    for g in range(groups):
        product = do_ref[g * GROUP : (g + 1) * GROUP].reshape(width, LANES).astype(F32).T * ot_ref[g]
        for m in range(rows):
            delta_ref[g * rows + m] = column_sum(product[m * HD : (m + 1) * HD])

    near_sems = wire.reserve(H * (parts - 1))
    back_sems = wire.reserve(H)

    def target(k):
        far = far_first(k) if isinstance(k, int) else jnp.where(k == H, H, far_first(k))
        return place.head_ahead(far)

    def near_kv(k, j):
        h = target(k)
        return wire.make(
            near_sems + (k - 1) * (parts - 1) + j - 1,
            part_ref.at[h, place.part_ahead(j)],
            near_ref.at[j - 1, h],
            place.across_parts(j),
        )

    def back_kv(k):
        h = target(k)
        return wire.make(back_sems + k - 1, dkv_sum.at[h], dkv_back.at[place.h], (h * parts + place.g, place.b))

    def fold(k):
        h = target(k)
        total = part_ref[h, place.g].astype(F32)
        for j in range(1, parts):
            near_kv(k, j).wait_recv()
            total = total + near_ref[j - 1, h].astype(F32)
        return total.astype(BF)

    def key_step(k):
        h = target(k)
        key, value = pair(h)
        key_t = key.T
        ids = [key_ids(h, m) for m in range(rows)]
        dk = jnp.zeros((keys, LANES), F32)
        dv = jnp.zeros((keys, LANES), F32)
        for g in range(groups):
            for m in range(rows):
                i = g * rows + m
                p = jnp.exp2(mm_nt(key, qm_ref[m, g]) * scale2 - lse_ref[i])
                p = jnp.where(ids[m] == idq_ref[m, g], p, 0.0)
                ds = (p * (mm_nt(value, dom_ref[m, g]) - delta_ref[i])).astype(BF)
                dv = dv + mm(p.astype(BF), dom_ref[m, g])
                dk = dk + mm(ds, qm_ref[m, g])
                dqt_ref[g, m * HD : (m + 1) * HD] += mm(key_t[m * HD : (m + 1) * HD], ds)
        part_ref[h, :, 0] = (dk * SCALE).astype(BF).reshape(parts, tokens, LANES)
        part_ref[h, :, 1] = dv.astype(BF).reshape(parts, tokens, LANES)
        for j in range(1, parts):
            near_kv(k, j).start()

    def backward_step(k, carry):
        key_step(k)
        dkv_sum[target(k - 1)] = fold(k - 1)
        back_kv(k - 1).start()
        meanwhile(
            k,
            (6, g_first.to_plane),
            (6, g_out.to_plane),
        )
        return carry

    token_pieces = (g_second, g_first, g_out)
    key_step(1)
    lax.fori_loop(2, H + 1, backward_step, 0)
    for g in range(groups):
        dq_ref[g * GROUP : (g + 1) * GROUP] = (dqt_ref[g] * SCALE).T.astype(BF).reshape(GROUP, tokens, LANES)
    moved = to_heads(dq_ref, dq_back)
    dq_back[place.h] = dq_ref[place.h]
    dkv_back[place.h] = fold(H)
    g_second.to_owner()

    def to_rows(parts_of):
        return jnp.concatenate(heads_to_rows([t.astype(F32) for t in parts_of]), axis=0).astype(BF)

    def grad_of(left, right, b):
        return mm(left, right[:, b * cols : (b + 1) * cols]).astype(BF).reshape(n_z, 2, 2, r, cols)

    def back_through(total, right, j):
        for b in range(n_b):
            total = total + mm_nt(right[:, b * cols : (b + 1) * cols], w_qkv(b, j))
        return total

    for k in range(1, H):
        back_kv(k).wait_recv()
    a_t = inputs().astype(BF).T
    dk = to_rows([dkv_back[h, 0] for h in range(H)])
    dv = to_rows([dkv_back[h, 1] for h in range(H)])
    for b in range(n_b):
        dkv_w_ref[b, 0] = grad_of(a_t, dk, b)
        dkv_w_ref[b, 1] = grad_of(a_t, dv, b)
    g_kv.to_core()
    add_small(frames_ref, ROW_BV, column_sum(dv.astype(F32)))
    du = back_through(back_through(sum_ref[...], dk, 1), dv, 2)
    g_kv.to_diagonal()
    g_second.to_far()
    g_first.to_owner()
    g_out.to_owner()
    received(moved)
    dq = to_rows([dq_back[h] for h in range(H)])
    for b in range(n_b):
        dq_w_ref[b, 0] = grad_of(a_t, dq, b)
    g_q.to_core()
    du = back_through(du, dq, 0)
    add_small(frames_ref, ROW_BQ, column_sum(dq.astype(F32)))
    sums = [column_sum(du[m * tokens : (m + 1) * tokens]) for m in range(rows)]
    for e in range(GROUPS):
        total = jnp.zeros_like(sums[0])
        for m in range(rows):
            total = total + jnp.where(groups_ref[m] == e, sums[m], 0.0)
        add_small(frames_ref, ROW_E + 4 * e, total)
    for s in range(place.n_s):
        for b in range(n_b):
            dsmall_ref[b, 0, s // 4, s // 2 % 2, s % 2] = frames_ref[(s * n_b + b) // frame]
    g_small.to_core()
    g_q.to_plane()
    g_kv.to_plane()
    g_small.to_plane()
    g_first.to_far()
    g_out.to_far()
    du_ref[...] = du.astype(BF)
    written[1].start()
    g_kv.to_owner()

    weights = [attn_ref.at[j] for j in range(4)] + [ffn_ref.at[j] for j in range(2)]
    outs = [agrad_ref.at[j] for j in range(4)] + [fgrad_ref.at[j] for j in range(2)]
    updates = [update_a.at[j] for j in range(4)] + [update_f.at[j] for j in range(2)]
    old_cols = [acols_ref[j : j + 1] for j in range(4)] + [fcols_ref[j : j + 1] for j in range(2)]
    owners = [(g_q, 0), (g_kv, 0), (g_kv, 1), (g_out, 0), (g_first, 0), (g_second, 0)]
    spans = [cols] * 4 + [cols_f] * 2
    places, used = [], 0
    for span in spans:
        places.append(used)
        used += -(-span // LANES)
    pad = cols_plane.shape[1]
    late = 3
    mine = cols_plane.at[place.xc]
    mine_rows = rows_plane.at[place.b, place.xc]
    mine_late = late_cols.at[place.s]
    mine_late_rows = late_rows.at[place.b]
    mine_sums = late_sums.at[place.b, place.s]
    mine[...] = jnp.zeros((pad, LANES), F32)
    mine_late[...] = jnp.zeros((8, LANES), F32)
    lane = lax.broadcasted_iota(jnp.int32, (r, LANES), 1)
    square_sums = [None] * SLABS
    old_rows = jnp.concatenate([arows_ref[...], frows_ref[...], jnp.zeros((2, r), F32)], axis=0).T
    old_rows = [old_rows[:, j : j + 1] for j in range(SLABS)]
    row_sums_old = [sum_all(x) for x in old_rows]
    weight_squares = [sum_all(w[...] * w[...]) for w in weights]
    own = own_ref[...]
    entry = lax.broadcasted_iota(jnp.int32, (8, LANES), 0) * LANES + lax.broadcasted_iota(jnp.int32, (8, LANES), 1)
    own_mask = jnp.where((entry >= own_at) & (entry < own_at + chunk), 1.0, 0.0)
    weight_squares.append(sum_all(own * own))
    rows_tiles = []

    def gradient(j):
        owner, slab = owners[j]
        grad = owner.total(slab)
        outs[j][...] = grad
        square = grad * grad + EPS_ONE
        row_sum = jnp.sum(square, axis=1, keepdims=True)
        col_sum = column_sum(square)
        ref = mine_late if j < late else mine
        for k in range(0, spans[j], LANES):
            span = min(LANES, spans[j] - k)
            ref[pl.ds(places[j] + k // LANES, 1), pl.ds(0, span)] = col_sum[:, k : k + span]
        square_sums[j] = sum_all(row_sum)
        return jnp.where(lane == j, row_sum, 0.0)

    def renewed(j, row_total, sums, square_total, old_total):
        length = D if j < 4 else FF
        new_rows = DECAY * old_rows[j] + (1.0 - DECAY) * row_total[:, j : j + 1] * (1.0 / length)
        rows_tiles.append(jnp.where(lane == j, new_rows, 0.0))
        mean_rows = (DECAY / n_b * old_total + (1.0 - DECAY) * (1.0 / length) * square_total) * (1.0 / D)
        pieces = [
            sums[places[j] + k // LANES : places[j] + k // LANES + 1, : min(LANES, spans[j] - k)]
            for k in range(0, spans[j], LANES)
        ]
        col_sum = pieces[0] if len(pieces) == 1 else jnp.concatenate(pieces, axis=1)
        new = DECAY * old_cols[j] + (1.0 - DECAY) * (1.0 / D) * col_sum
        if j < 4:
            acols_new_ref[j : j + 1, :] = new
        else:
            fcols_new_ref[j - 4 : j - 3, :] = new
        update = outs[j][...] * lax.rsqrt((new_rows / mean_rows) * new)
        updates[j][...] = update
        return sum_all(update * update)

    def pick(tile, j):
        return tile[0:1, j : j + 1]

    def fan(i, ref, offsets):
        for db in offsets:
            b = place.batch_ahead(db)

            def one(k, carry=0, b=b):
                wire.make(i, ref, ref, (wrap(place.s + k, place.n_s), b)).start()
                return carry

            if place.n_s > 16:
                lax.fori_loop(0 if db else 1, place.n_s, one, 0)
            else:
                for k in outwards(place.n_s) + [0] * (db > 0):
                    one(k)

    near, others = [0], list(range(1, n_b))
    one_peer = place.along_z(1)

    g_second.finish()
    row_tile = gradient(5)
    g_q.to_owner()
    g_small.to_owner()
    g_first.finish()
    g_out.finish()
    mine_rows[pl.ds(0, r), :] = row_tile + gradient(4) + gradient(3)
    tail = pl.ds(r, 8)
    mine_rows[tail, :] = lanes_of(square_sums + row_sums_old + weight_squares)
    moved = []
    for dx, db in plane:
        peer = plane_peer(dx, db)
        if db == 0:
            moved.append(wire.send(lambda peer=peer: (mine, mine, peer)))
        if dx == 0:
            moved.append(wire.send(lambda peer=peer: (mine_rows, mine_rows, peer)))
        else:
            moved.append(wire.send(lambda peer=peer: (mine_rows.at[tail], mine_rows.at[tail], peer)))
    g_kv.finish()
    row_tile = gradient(1) + gradient(2)
    received(moved)
    mine_z = all_z.at[place.z]
    mine_z[pl.ds(0, pad), :] = cols_plane[0] + cols_plane[1] + cols_plane[2] + cols_plane[3]
    scalars = jnp.zeros((8, LANES), F32)
    row_total = jnp.zeros((r, LANES), F32)
    for b in range(n_b):
        for xc in range(4):
            scalars = scalars + rows_plane[b, xc, tail, :]
        row_total = row_total + rows_plane[b, place.xc, pl.ds(0, r), :]
    mine_z[pl.ds(pad, 8), :] = scalars
    moved = [wire.send(lambda peer=peer: (mine_z, mine_z, peer)) for peer in along]

    g_q.finish()
    mine_late_rows[...] = row_tile + gradient(0)
    written[2].start()
    written[3].start()
    sums = lanes_of(square_sums[:late])[0:1]
    mine_late[7:8, :] = sums
    late_sums[place.b] = jnp.zeros((place.n_s, 1, LANES), F32)
    mine_sums[...] = sums
    late_i, sums_i, all_i = wire.reserve(1), wire.reserve(1), wire.reserve(1)
    moved_rows = [
        wire.send(lambda k=k: (mine_late_rows, mine_late_rows, place.across_batch(k))) for k in range(1, n_b)
    ]
    fan(late_i, mine_late, near)
    fan(sums_i, mine_sums, others)

    received(moved)
    reduced = all_z[0]
    for z in range(1, n_z):
        reduced = reduced + all_z[z]
    tile = reduced[pad:]

    def scalar(j):
        return pick(tile, j)

    update_squares = [None] * SLABS
    for j in range(late, SLABS):
        update_squares[j] = renewed(j, row_total, reduced, scalar(j), scalar(SLABS + j))
    g_small.finish()
    own_grad = g_small.total(0) * own_mask
    own_sq = DECAY * to_frame(sq_ref[...].reshape(1, chunk), own_at) + (1.0 - DECAY) * (own_grad * own_grad + EPS_ONE)
    own_update = own_grad * lax.rsqrt(own_sq)
    update_squares.append(sum_all(own_update * own_update))
    for k in range(1, H + 1):
        for j in range(1, parts):
            near_kv(k, j).wait_send()
        if k < H:
            back_kv(k).wait_send()
    wire.drain()

    late_part = late_cols.at[pl.ds(0, place.n_s - 1)]
    sums_part = late_sums.at[pl.ds(0, n_b - 1)]
    wire.make(late_i, late_part, late_part, one_peer).wait_recv()
    wire.make(sums_i, sums_part, sums_part, one_peer).wait_recv()
    received(moved_rows)
    sums = late_cols[0]
    for s in range(1, place.n_s):
        sums = sums + late_cols[s]
    totals = jnp.zeros((1, LANES), F32)
    row_total = jnp.zeros((r, LANES), F32)
    for b in range(n_b):
        other = late_sums[b, 0]
        for s in range(1, place.n_s):
            other = other + late_sums[b, s]
        totals = totals + jnp.where(place.b == b, sums[7:8], other)
        row_total = row_total + late_rows[b]
    for j in range(late):
        update_squares[j] = renewed(j, row_total, sums, pick(totals, j), scalar(SLABS + j))
    written[4].start()
    written[5].start()
    rows_new_ref[...] = sum(rows_tiles[1:], rows_tiles[0])
    mine_u = all_sums.at[place.b * place.n_s + place.s]
    mine_u[...] = lanes_of(update_squares)[0:1]
    fan(all_i, mine_u, near + others)
    wire.make(late_i, late_part, late_part, one_peer).wait_send()
    wire.make(sums_i, sums_part, sums_part, one_peer).wait_send()
    all_part = all_sums.at[pl.ds(0, place.n_s * n_b - 1)]
    copy = wire.make(all_i, all_part, all_part, one_peer)
    copy.wait_send()
    copy.wait_recv()
    update_tile = jnp.zeros((1, LANES), F32)
    for i in range(place.n_s * n_b):
        update_tile = update_tile + all_sums[i]
    sizes = [D * D] * 4 + [D * FF] * 2 + [NVEC]

    def scale(j):
        weight = jnp.sqrt(scalar(2 * SLABS + j) * (1.0 / sizes[j]))
        return LEARN * weight / jnp.maximum(1.0, jnp.sqrt(update_tile[0:1, j : j + 1] * (1.0 / sizes[j])))

    scales_ref[...] = lanes_of([scale(j) for j in range(SLABS)])
    own_new_ref[0] = own_grad
    own_new_ref[1] = own - scale(SLABS) * own_update
    own_new_ref[2] = own_sq
    for copy in written:
        copy.wait()
    wire.drain()


def layer_part(groups, lengths, tok, cot, attn, ffn, params, arows, acols, frows, fcols, sq):
    n_s, n_b = lax.axis_size("seq"), lax.axis_size("batch")
    n_z, parts = n_s // 4, n_s // H
    count = tok.shape[0]
    tokens = count // 2
    rows = 2
    _, r, cols = attn.shape
    cols_f = ffn.shape[2]
    groups_q = H // GROUP
    width = GROUP * tokens
    length = tokens * n_s
    wide = min(512, cols_f)
    tiles = FF // wide
    pad = 4 * -(-cols // LANES) + 2 * (cols_f // LANES)
    pad = -(-pad // 8) * 8
    gather = (n_z - 1) + (1 + n_b) + 2 * (n_b - 1) + 1 + (n_b - 1) + 2 * (n_b - 1)
    copies = 5 * gather + 7 * (H - 1) + 2 * H + 2 * H * (parts - 1)
    copies += 6 * (1 + 2 * (n_b - 1) + n_b + n_z - 1)
    copies += 6 + 4 * n_b + (n_z - 1) + (n_b - 1) + 3

    def shape(dims, kind):
        return jax.ShapeDtypeStruct(dims, kind)

    out = (
        shape(tok.shape, BF),
        shape(tok.shape, BF),
        shape(attn.shape, F32),
        shape(ffn.shape, F32),
        shape(attn.shape, F32),
        shape(ffn.shape, F32),
        shape((8, LANES), F32),
        shape((r, LANES), F32),
        shape(acols.shape, F32),
        shape(fcols.shape, F32),
        shape((3, 8, LANES), F32),
    )
    vmem = pltpu.VMEM
    heads = (H, tokens, LANES)
    scratch = [
        vmem((1, r + 16, cols), BF),
        vmem((2, r, cols), BF),
        vmem((1, r, cols), BF),
        vmem(ffn.shape, BF),
        vmem((8, LANES), F32),
        vmem((FRAMES, 8, LANES), F32),
        vmem((n_b, 1, n_z, 4, r + 16, cols), BF),
        vmem((n_b, 2, n_z, 4, r, cols), BF),
        vmem((n_b, 1, n_z, 4, r, cols), BF),
        vmem((n_b, 1, n_z, 4, r, cols_f), BF),
        vmem((n_b, 1, n_z, 4, r, cols_f), BF),
        vmem((rows, length, LANES), F32),
        vmem((rows, groups_q, 1, width), F32),
        vmem(heads, BF),
        vmem((n_s, 2, tokens, LANES), BF),
        vmem(heads, BF),
        vmem((H, 2, tokens, LANES), BF),
        vmem((rows, groups_q, width, LANES), BF),
        vmem((rows, groups_q, width, LANES), BF),
        vmem((rows * groups_q, 1, width), F32),
        vmem((rows * groups_q, HD + 16, width), F32),
        vmem((groups_q, LANES, width), F32),
        vmem((rows * groups_q, 1, width), F32),
        vmem((rows * groups_q, 1, width), F32),
        vmem(heads, BF),
        vmem(heads, BF),
        vmem(heads, BF),
        vmem(heads, BF),
        vmem((tiles, count, wide), BF),
        vmem((tiles, count, wide), F32),
        vmem((tiles, count, wide), BF),
        vmem((count, D), F32),
        vmem((FRAMES, 8, LANES), F32),
        vmem((groups_q, LANES, width), F32),
        vmem((H, parts, 2, tokens, LANES), BF),
        vmem((parts - 1, H, 2, tokens, LANES), BF),
        vmem((H, 2, tokens, LANES), BF),
        vmem(heads, BF),
        vmem(heads, BF),
        vmem((H, 2, tokens, LANES), BF),
        vmem((n_b, 1, n_z, 2, 2, r, cols), BF),
        vmem((n_b, 1, n_z, 2, 2, r, cols_f), BF),
        vmem((n_b, 1, n_z, 2, 2, r, cols_f), BF),
        vmem((n_b, 2, n_z, 2, 2, r, cols), BF),
        vmem((n_b, 1, n_z, 2, 2, r, cols), BF),
        vmem((n_b, 1, n_z, 2, 2, 8, LANES), F32),
        vmem((4, pad, LANES), F32),
        vmem((n_b, 4, r + 8, LANES), F32),
        vmem((n_z, pad + 8, LANES), F32),
        vmem((n_s, 8, LANES), F32),
        vmem((n_b, r, LANES), F32),
        vmem((n_b, n_s, 1, LANES), F32),
        vmem((n_b * n_s, 1, LANES), F32),
        vmem(tok.shape, BF),
        vmem(tok.shape, BF),
        vmem(attn.shape, F32),
        vmem(ffn.shape, F32),
        vmem(attn.shape, F32),
        vmem(ffn.shape, F32),
    ]
    scratch += scatter_scratch(n_b, 1, n_z, r, cols_f, BF) * 2
    scratch += scatter_scratch(n_b, 1, n_z, r, cols, BF)
    scratch += scatter_scratch(n_b, 2, n_z, r, cols, BF)
    scratch += short_scratch(n_b, 1, n_z, r, cols, BF)
    scratch += short_scratch(n_b, 1, n_z, 8, LANES, F32)
    dma = pltpu.SemaphoreType.DMA
    scratch += [dma((copies,)), dma((copies,)), dma((11,))]
    return pl.pallas_call(
        layer_kernel,
        out_shape=out,
        in_specs=[SMEM_SPEC] + [VMEM_SPEC] * 11,
        out_specs=(pl.BlockSpec(memory_space=pl.ANY),) * 6 + (VMEM_SPEC,) * 5,
        scratch_shapes=scratch,
        compiler_params=pltpu.CompilerParams(
            vmem_limit_bytes=63 * 2**20, collective_id=0, has_side_effects=True
        ),
    )(groups, lengths, tok, cot, attn, ffn, params, arows, acols, frows, fcols, sq)


def result_kernel(
    out_in, du_in, agrad_in, fgrad_in, update_a, update_f, scales_ref, rows_ref, acols_in, fcols_in, own_ref,
    attn_ref, ffn_ref,
    out_ref, du_ref, agrad_ref, fgrad_ref, grad_ref, anew_ref, fnew_ref, new_ref, acopy_ref, fcopy_ref, copy_ref,
    arows_ref, acols_ref, frows_ref, fcols_ref, sq_ref,
):
    for src, dst in ((out_in, out_ref), (du_in, du_ref), (agrad_in, agrad_ref), (fgrad_in, fgrad_ref)):
        dst[...] = src[...]
    for j in range(4):
        new = attn_ref[j] - scales_ref[0:1, j : j + 1] * update_a[j]
        anew_ref[j] = new
        acopy_ref[j] = new.astype(BF)
    for j in range(2):
        new = ffn_ref[j] - scales_ref[0:1, 4 + j : 5 + j] * update_f[j]
        fnew_ref[j] = new
        fcopy_ref[j] = new.astype(BF)
    rows = rows_ref[...].T
    arows_ref[...] = rows[0:4]
    frows_ref[...] = rows[4:6]
    acols_ref[...] = acols_in[...]
    fcols_ref[...] = fcols_in[...]
    chunk = grad_ref.shape[0]
    at = own_place(chunk)
    grad_ref[...] = from_frame(own_ref[0], at, chunk).reshape(chunk)
    new = from_frame(own_ref[1], at, chunk)
    new_ref[...] = new.reshape(chunk)
    copy_ref[...] = new.astype(BF).reshape(chunk)
    sq_ref[...] = from_frame(own_ref[2], at, chunk).reshape(chunk)


def result_part(made, attn, ffn, chunk):
    out, _, agrad, fgrad, _, _, _, rows, acols, fcols, _ = made
    r = rows.shape[0]

    def shape(dims, kind):
        return jax.ShapeDtypeStruct(dims, kind)

    shapes = (
        shape(out.shape, BF),
        shape(out.shape, BF),
        shape(attn.shape, F32),
        shape(ffn.shape, F32),
        shape((chunk,), F32),
        shape(attn.shape, F32),
        shape(ffn.shape, F32),
        shape((chunk,), F32),
        shape(attn.shape, BF),
        shape(ffn.shape, BF),
        shape((chunk,), BF),
        shape((4, r), F32),
        shape(acols.shape, F32),
        shape((2, r), F32),
        shape(fcols.shape, F32),
        shape((chunk,), F32),
    )
    return pl.pallas_call(
        result_kernel,
        out_shape=shapes,
        in_specs=[VMEM_SPEC] * 13,
        out_specs=(VMEM_SPEC,) * 16,
        compiler_params=pltpu.CompilerParams(vmem_limit_bytes=60 * 2**20),
    )(*made, attn, ffn)


def shards(
    tokens, lengths, groups, cotangent, attn_weights, ffn_weights, small_params,
    attn_rows, attn_cols, ffn_rows, ffn_cols, small_sq,
):
    micro, rb, toks, _ = tokens.shape
    rows = micro * rb
    chunk = small_params.shape[0]
    made = layer_part(
        groups.reshape(rows),
        lengths.reshape(rows, SEGS),
        tokens.reshape(rows * toks, D),
        cotangent.reshape(rows * toks, D),
        attn_weights,
        ffn_weights,
        small_params,
        attn_rows,
        attn_cols,
        ffn_rows,
        ffn_cols,
        small_sq,
    )
    results = list(result_part(made, attn_weights, ffn_weights, chunk))
    for i in (0, 1):
        results[i] = results[i].reshape(tokens.shape)
    return tuple(results)


def solution(mesh):
    acts = P(None, "batch", "seq", None)
    weights = P(None, "seq", "batch")
    small = P(("seq", "batch"))
    rows, cols = P(None, "seq"), P(None, "batch")
    return jax.shard_map(
        shards,
        mesh=mesh,
        in_specs=(acts, P(None, "batch", None), P(None, "batch"), acts, weights, weights, small)
        + (rows, cols, rows, cols, small),
        out_specs=(acts, acts, weights, weights, small, weights, weights, small, weights, weights, small)
        + (rows, cols, rows, cols, small),
        check_vma=False,
    )
```

```python
import functools

import jax
import jax.numpy as jnp
from jax import lax
from jax.experimental import pallas as pl
from jax.experimental.pallas import tpu as pltpu
from jax.sharding import PartitionSpec as P

D = 512
H = 8
HD = 64
FF = 2048
GROUPS = 8
SEGS = 64
STEP = 10
NVEC = 10240
LANES = 128

NEG = -1e30
EPS = 1e-05
EPS_ONE = 1e-30
LEARN = 1.0
DECAY = 1.0 - STEP ** (-0.8)
SCALE = HD ** (-0.5)
LOG2E = 1.4426950408889634
FRAMES = 16
FRAME_ROWS = NVEC // FRAMES // LANES
GROUP = 4
BF = jnp.bfloat16
F32 = jnp.float32
VMEM_SPEC = pl.BlockSpec(memory_space=pltpu.VMEM)
SMEM_SPEC = pl.BlockSpec(memory_space=pltpu.SMEM)

ROW_BQ, ROW_BV, ROW_BO, ROW_B1, ROW_B2 = 0, 4, 8, 12, 28
ROW_G1, ROW_S1, ROW_G2, ROW_S2, ROW_E = 32, 36, 40, 44, 48


def mm(a, b):
    return lax.dot_general(a, b, (((1,), (0,)), ((), ())), preferred_element_type=F32)


def mm_nt(a, b):
    return lax.dot_general(a, b, (((1,), (1,)), ((), ())), preferred_element_type=F32)


def mm_tn(a, b):
    return lax.dot_general(a, b, (((0,), (0,)), ((), ())), preferred_element_type=F32)


def small_piece(small_ref, row, count):
    parts = [small_ref[r // FRAME_ROWS, pl.ds(r % FRAME_ROWS, 1), :] for r in range(row, row + count)]
    return jnp.concatenate(parts, axis=1)


def add_small(ref, row, values):
    for k in range(values.shape[1] // LANES):
        r = row + k
        ref[r // FRAME_ROWS, pl.ds(r % FRAME_ROWS, 1), :] += values[:, k * LANES : (k + 1) * LANES]


def low_half():
    return lax.broadcasted_iota(jnp.int32, (1, LANES), 1) < HD


def swap_halves(x):
    return pltpu.roll(x, HD, 1)


def heads_to_rows(tiles):
    low = low_half()
    first, second = [], []
    for j in range(H // 2):
        a, b = tiles[2 * j], tiles[2 * j + 1]
        first.append(jnp.where(low, a, swap_halves(b)))
        second.append(jnp.where(low, swap_halves(a), b))
    return jnp.concatenate(first, axis=1), jnp.concatenate(second, axis=1)


def rows_to_heads(first, second):
    low = low_half()
    tiles = []
    for j in range(H // 2):
        a = first[:, j * LANES : (j + 1) * LANES]
        b = second[:, j * LANES : (j + 1) * LANES]
        tiles.append(jnp.where(low, a, swap_halves(b)))
        tiles.append(jnp.where(low, swap_halves(a), b))
    return tiles


def wrap(value, count):
    return value - jnp.where(value >= count, count, 0)


def outwards(count):
    return sorted(range(1, count), key=lambda k: (abs(2 * k - count), k))


class Place:
    def __init__(self):
        self.n_s, self.n_b = lax.axis_size("seq"), lax.axis_size("batch")
        self.s, self.b = lax.axis_index("seq"), lax.axis_index("batch")
        self.n_z, self.parts = self.n_s // 4, self.n_s // H
        self.z, self.xc = self.s // 4, self.s % 4
        self.x, self.c = self.xc // 2, self.xc % 2
        self.other_x = (1 - self.x) * 2 + self.c
        self.other_c = self.x * 2 + 1 - self.c
        self.h, self.g = self.s // self.parts, self.s % self.parts
        self.z_ahead = [wrap(self.z + k, self.n_z) for k in range(self.n_z)]
        self.b_ahead = [wrap(self.b + k, self.n_b) for k in range(self.n_b)]
        self.xc_ahead = [wrap(self.xc + k, 4) for k in range(4)]
        self.h_ahead = [wrap(self.h + k, H) for k in range(H)]
        self.g_ahead = [wrap(self.g + k, self.parts) for k in range(self.parts)]
        self.z_pair = self.z + 1 - self.z % 2 * 2
        self.z_pair_ahead = [wrap(self.z_pair + k, self.n_z) for k in range(self.n_z)]
        self.at_z = [z * 4 + self.xc for z in self.z_ahead]
        self.at_x, self.at_core = self.z * 4 + self.other_x, self.z * 4 + self.other_c
        self.at_head = [h * self.parts + self.g for h in self.h_ahead]
        self.at_part = [self.h * self.parts + g for g in self.g_ahead]

    def along_z(self, k):
        return (self.at_z[k], self.b)

    def across_z(self):
        return (self.z_pair * 4 + self.xc, self.b)

    def across_x(self):
        return (self.at_x, self.b)

    def across_core(self):
        return (self.at_core, self.b)

    def batch_ahead(self, k):
        return self.b_ahead[k]

    def batch_behind(self, k):
        return self.b_ahead[(self.n_b - k) % self.n_b]

    def across_batch(self, k):
        return (self.s, self.b_ahead[k])

    def head_ahead(self, k):
        return self.h_ahead[k % H] if isinstance(k, int) else wrap(self.h + k, H)

    def head_behind(self, k):
        return self.h_ahead[(H - k) % H] if isinstance(k, int) else wrap(self.h + H - k, H)

    def across_heads(self, k):
        return (self.at_head[k] if isinstance(k, int) else self.head_ahead(k) * self.parts + self.g, self.b)

    def part_ahead(self, k):
        return self.g_ahead[k]

    def across_parts(self, k):
        return (self.at_part[k], self.b)


def greet(peers):
    barrier = pltpu.get_barrier_semaphore()
    for peer in peers:
        pl.semaphore_signal(barrier, inc=1, device_id=peer, device_id_type=pl.DeviceIdType.MESH)
    pl.semaphore_wait(barrier, len(peers))


def greet_all(place):
    barrier = pltpu.get_barrier_semaphore()

    def hello(b, i, carry):
        peer = (wrap(place.s + i, place.n_s), b)
        pl.semaphore_signal(barrier, inc=1, device_id=peer, device_id_type=pl.DeviceIdType.MESH)
        return carry

    for k, b in enumerate(place.b_ahead):
        lax.fori_loop(0 if k else 1, place.n_s, functools.partial(hello, b), 0)
    return lambda: pl.semaphore_wait(barrier, place.n_s * place.n_b - 1)


def far_first(i):
    if isinstance(i, int) and i in (0, H):
        return i
    return H // 2 + i // 2 * (1 - i % 2 * 2)


class Copy:
    def __init__(self, wire, i, build):
        self.wire, self.i, self.build = wire, i, build

    def made(self):
        return self.wire.make(self.i, *self.build())

    def start(self):
        self.made().start()

    def wait_recv(self):
        self.made().wait_recv()

    def wait_send(self):
        self.made().wait_send()


class Wire:
    def __init__(self, send_sems, recv_sems):
        self.send_sems, self.recv_sems, self.copies, self.used = send_sems, recv_sems, [], 0

    def reserve(self, count):
        self.used += count
        return self.used - count

    def make(self, i, src, dst, peer):
        return pltpu.make_async_remote_copy(
            src_ref=src,
            dst_ref=dst,
            send_sem=self.send_sems.at[i],
            recv_sem=self.recv_sems.at[i],
            device_id=peer,
            device_id_type=pl.DeviceIdType.MESH,
        )

    def plan(self, build):
        return Copy(self, self.reserve(1), build)

    def send(self, build):
        copy = self.plan(build)
        copy.start()
        self.copies.append(copy)
        return copy

    def drain(self):
        for copy in self.copies:
            copy.wait_send()
        self.copies = []


def received(copies):
    for copy in copies:
        copy.wait_recv()


class Gather:
    def __init__(self, place, wire, src, dst, own_sem, cut):
        self.place, self.wire, self.src, self.dst, self.cut, self.own_sem = place, wire, src, dst, cut, own_sem
        self.own().start()
        self.begin()

    def begin(self):
        p = self.place
        self.along = [self.wire.send(lambda k=k: (self.src, self.slot(p.z), p.along_z(k))) for k in range(1, p.n_z)]

    def slot(self, z):
        return self.dst.at[self.place.b, :, z, self.place.xc]

    def own(self):
        return pltpu.make_async_copy(self.src, self.slot(self.place.z), self.own_sem)

    def forward(self, part, *peers):
        return [self.wire.send(lambda peer=peer: (part(), part(), peer())) for peer in peers]

    def column(self, b, xc):
        return lambda: self.dst.at[b(), :, :, xc]

    def half(self, b, xc, second):
        span = pl.ds(self.cut, self.place.n_z - self.cut) if second else pl.ds(0, self.cut)
        return lambda: self.dst.at[b(), :, span, xc]

    def batch_peers(self):
        return [lambda k=k: self.place.across_batch(k) for k in range(1, self.place.n_b)]

    def to_plane(self):
        p = self.place
        self.own().wait()
        received(self.along)
        peers = [p.across_x, p.across_core] + self.batch_peers()
        self.plane = self.forward(self.column(lambda: p.b, p.xc), *peers)

    def to_diagonal(self):
        p = self.place
        self.plane[0].wait_recv()
        self.diagonal = self.forward(self.half(lambda: p.b, p.other_x, 0), *self.batch_peers())
        self.cores = [self.plane[1]] + self.forward(self.column(lambda: p.b, p.other_x), p.across_core)
        for k in range(1, p.n_b):
            b = lambda k=k: p.batch_behind(k)
            self.plane[1 + k].wait_recv()
            self.diagonal += self.forward(self.half(b, p.xc, 1), p.across_x)
            self.cores += self.forward(self.column(b, p.xc), p.across_core)

    def to_cores(self):
        p = self.place
        for k in range(1, p.n_b):
            for second in range(2):
                self.diagonal[(p.n_b - 1) * second + k - 1].wait_recv()
                part = self.half(lambda k=k: p.batch_behind(k), p.other_x, second)
                self.cores += self.forward(part, p.across_core)

    def finish(self):
        received(self.cores)


class PairGather(Gather):

    def begin(self):
        p, self.far = self.place, range(2, self.place.n_z, 2)
        self.along = [self.wire.send(lambda: (self.src, self.slot(p.z), p.across_z()))]
        self.arriving = [self.wire.send(lambda k=k: (self.src, self.slot(p.z), p.along_z(k))) for k in self.far]

    def to_pair(self):
        p = self.place
        for copy, k in zip(self.arriving, self.far):
            copy.wait_recv()
            z = p.z_ahead[p.n_z - k]
            self.along.append(self.wire.send(lambda z=z: (self.slot(z), self.slot(z), p.across_z())))


class ShortGather(Gather):
    def to_plane(self):
        p = self.place
        self.own().wait()
        received(self.along)
        diagonal = [
            lambda k=k: (p.z * 4 + p.other_x, p.batch_ahead(k)) for k in range(1, p.n_b)
        ]
        peers = [p.across_core, p.across_x] + self.batch_peers() + diagonal
        self.plane = self.forward(self.column(lambda: p.b, p.xc), *peers)

    def to_cores(self):
        p = self.place
        behind = [lambda k=k: p.batch_behind(k) for k in range(1, p.n_b)]
        columns = [(lambda: p.b, p.other_x)] + [(b, p.xc) for b in behind] + [(b, p.other_x) for b in behind]
        self.cores = [self.plane[0]]
        for copy, (b, xc) in zip(self.plane[1:], columns):
            copy.wait_recv()
            self.cores += self.forward(self.column(b, xc), p.across_core)


def normed_of(values):
    center = values - jnp.mean(values, axis=-1, keepdims=True)
    inverse = lax.rsqrt(jnp.mean(center * center, axis=-1, keepdims=True) + EPS)
    return center * inverse, inverse


def norm_back(grad_norm, normed, inverse):
    return inverse * (
        grad_norm
        - jnp.mean(grad_norm, axis=-1, keepdims=True)
        - normed * jnp.mean(grad_norm * normed, axis=-1, keepdims=True)
    )


def gelu_pair(z):
    c = 0.7978845608028654
    z2 = z * z
    t = jnp.tanh(c * z * (1.0 + 0.044715 * z2))
    half = 0.5 * (1.0 + t)
    slope = half + 0.5 * z * (1.0 - t * t) * (c * (1.0 + 3 * 0.044715 * z2))
    return z * half, slope


def language_rows(groups_ref, small_ref, rows):
    table = [small_piece(small_ref, ROW_E + 4 * e, 4) for e in range(GROUPS)]
    out = []
    for m in range(rows):
        acc = jnp.zeros_like(table[0])
        for e in range(GROUPS):
            acc = acc + jnp.where(groups_ref[m] == e, table[e], 0.0)
        out.append(acc)
    return out


def column_sum(x):
    return jnp.sum(x, axis=0, keepdims=True)


class Scatter:
    def __init__(self, place, wire, part, core, acc, far, near, plane_x, plane_b, column):
        self.begin(place, wire, part, core, acc, column)
        self.far, self.near, self.plane_x, self.plane_b = far, near, plane_x, plane_b
        self.cut = far.shape[2]

    def begin(self, place, wire, part, core, acc, column):
        self.place, self.wire = place, wire
        self.part, self.core, self.acc, self.column = part, core, acc, column
        self.kind = part.dtype
        self.x, self.c = place.x, place.c
        self.slabs = part.shape[1]

    def add(self, target, *others):
        total = target[...].astype(F32)
        for other in others:
            total = total + other[...].astype(F32)
        target[...] = total.astype(self.kind)

    def each(self, body, first=0, last=None):
        for j in range(self.slabs):

            def step(z, carry, j=j):
                body(j, z)
                return carry

            lax.fori_loop(first, self.place.n_z if last is None else last, step, 0)

    def to_core(self):
        p = self.place
        self.moved = [self.wire.send(lambda: (self.part.at[:, :, :, :, 1 - self.c], self.core, p.across_core()))]

    def join(self):
        p = self.place
        received(self.moved)
        for j in range(self.slabs):

            def body(b, carry, j=j):
                def at_z(z, carry):
                    for x in range(2):
                        total = self.part[b, j, z, x, self.c].astype(F32) + self.core[b, j, z, x].astype(F32)
                        self.acc[b, j, z, x] = total.astype(self.kind)
                    return carry

                return lax.fori_loop(0, p.n_z, at_z, carry)

            lax.fori_loop(0, p.n_b, body, 0)

    def to_diagonal(self):
        p = self.place
        self.join()
        cut, rest = pl.ds(0, self.cut), pl.ds(self.cut, p.n_z - self.cut)
        self.moved_far, self.moved_near = [], []
        for k in range(1, p.n_b):
            diagonal = lambda k=k: self.acc.at[p.batch_ahead(k), :, :, 1 - self.x]
            self.moved_far.append(
                self.wire.send(
                    lambda k=k, part=diagonal: (part().at[:, cut], self.far.at[k - 1], p.across_batch(k))
                )
            )
            self.moved_near.append(
                self.wire.send(lambda k=k, part=diagonal: (part().at[:, rest], self.near.at[k - 1], p.across_x()))
            )

    def to_plane(self):
        p = self.place
        for k in range(1, p.n_b):
            self.moved_near[k - 1].wait_recv()
            self.each(
                lambda j, z, k=k: self.add(
                    self.acc.at[p.batch_ahead(k), j, z, self.x], self.near.at[k - 1, j, z - self.cut]
                ),
                self.cut,
            )
        received(self.moved_far)
        self.each(
            lambda j, z: self.add(
                self.acc.at[p.b, j, z, 1 - self.x], *[self.far.at[k - 1, j, z] for k in range(1, p.n_b)]
            ),
            0,
            self.cut,
        )
        self.moved = [self.wire.send(lambda: (self.acc.at[p.b, :, :, 1 - self.x], self.plane_x, p.across_x()))]
        self.moved += [
            self.wire.send(
                lambda k=k: (
                    self.acc.at[p.batch_ahead(k), :, :, self.x],
                    self.plane_b.at[k - 1],
                    p.across_batch(k),
                )
            )
            for k in range(1, p.n_b)
        ]

    def others(self, j, z):
        return [self.plane_x.at[j, z]] + [self.plane_b.at[k - 1, j, z] for k in range(1, self.place.n_b)]

    def to_owner(self):
        p = self.place
        received(self.moved)
        self.each(lambda j, z: self.add(self.acc.at[p.b, j, z, self.x], *self.others(j, z)))
        self.moved = [
            self.wire.send(
                lambda k=k: (
                    self.acc.at[p.b, :, p.z_ahead[k], self.x],
                    self.column.at[k - 1],
                    p.along_z(k),
                )
            )
            for k in range(1, p.n_z)
        ]

    def total(self, j):
        p = self.place
        out = self.acc[p.b, j, p.z, self.x].astype(F32)
        for k in range(1, p.n_z):
            out = out + self.column[k - 1, j].astype(F32)
        return out

    def finish(self):
        received(self.moved)


class PairScatter(Scatter):

    def to_owner(self):
        p = self.place
        received(self.moved)
        self.each(lambda j, z: self.add(self.acc.at[p.b, j, z, self.x], *self.others(j, z)))
        self.moved = [
            self.wire.send(
                lambda i=i: (
                    self.acc.at[p.b, :, p.z_pair_ahead[2 * i], self.x],
                    self.column.at[i],
                    p.across_z(),
                )
            )
            for i in range(p.n_z // 2)
        ]

    def to_far(self):
        p = self.place
        half = p.n_z // 2
        received(self.moved)
        for i in range(half):
            for j in range(self.slabs):
                self.add(self.acc.at[p.b, j, p.z_ahead[2 * i], self.x], self.column.at[i, j])
        self.moved = [
            self.wire.send(
                lambda i=i: (
                    self.acc.at[p.b, :, p.z_ahead[2 * i], self.x],
                    self.column.at[half + i - 1],
                    p.along_z(2 * i),
                )
            )
            for i in range(1, half)
        ]

    def total(self, j):
        p = self.place
        out = self.acc[p.b, j, p.z, self.x].astype(F32)
        for k in range(p.n_z // 2, p.n_z - 1):
            out = out + self.column[k, j].astype(F32)
        return out


class ShortScatter(Scatter):
    def __init__(self, place, wire, part, core, acc, plane, column):
        self.begin(place, wire, part, core, acc, column)
        self.plane = plane

    def to_plane(self):
        p = self.place
        self.join()
        self.moved = []
        for k in range(p.n_b):
            for dx in range(2):
                if k or dx:

                    def build(k=k, dx=dx, slot=len(self.moved)):
                        x = self.x if dx == 0 else 1 - self.x
                        to = p.z * 4 + (p.other_x if dx else p.xc)
                        b = p.batch_ahead(k)
                        return (self.acc.at[b, :, :, x], self.plane.at[slot], (to, b))

                    self.moved.append(self.wire.send(build))

    def others(self, j, z):
        return [self.plane.at[k, j, z] for k in range(2 * self.place.n_b - 1)]


def short_scratch(n_b, slabs, n_z, r, cols, kind):
    return [
        pltpu.VMEM((n_b, slabs, n_z, 2, r, cols), kind),
        pltpu.VMEM((n_b, slabs, n_z, 2, r, cols), kind),
        pltpu.VMEM((2 * n_b - 1, slabs, n_z, r, cols), kind),
        pltpu.VMEM((n_z - 1, slabs, r, cols), kind),
    ]


def scatter_scratch(n_b, slabs, n_z, r, cols, kind):
    return [
        pltpu.VMEM((n_b, slabs, n_z, 2, r, cols), kind),
        pltpu.VMEM((n_b, slabs, n_z, 2, r, cols), kind),
        pltpu.VMEM((n_b - 1, slabs, n_z - n_z // 4, r, cols), kind),
        pltpu.VMEM((n_b - 1, slabs, n_z // 4, r, cols), kind),
        pltpu.VMEM((slabs, n_z, r, cols), kind),
        pltpu.VMEM((n_b - 1, slabs, n_z, r, cols), kind),
        pltpu.VMEM((n_z - 1, slabs, r, cols), kind),
    ]


SCATTER_SCRATCH, SHORT_SCRATCH = 7, 4
SLABS = 6


def lanes_of(values):
    lane = lax.broadcasted_iota(jnp.int32, (8, LANES), 1)
    row = lax.broadcasted_iota(jnp.int32, (8, LANES), 0)
    tile = jnp.zeros((8, LANES), F32)
    for j, value in enumerate(values):
        if value is not None:
            tile = tile + jnp.where((lane == j) & (row == 0), value, 0.0)
    return tile


def sum_all(x):
    return jnp.sum(jnp.sum(x, axis=1, keepdims=True), axis=0, keepdims=True)


def to_frame(values, at):
    wide = jnp.concatenate([values, jnp.zeros((1, 8 * LANES - values.shape[1]), F32)], axis=1)
    wide = pltpu.roll(wide, at, 1)
    return jnp.concatenate([wide[:, k * LANES : (k + 1) * LANES] for k in range(8)], axis=0)


def from_frame(tile, at, chunk):
    wide = jnp.concatenate([tile[k : k + 1] for k in range(8)], axis=1)
    return pltpu.roll(wide, 8 * LANES - at, 1)[:, :chunk]


def own_place(chunk):
    index = lax.axis_index("seq") * lax.axis_size("batch") + lax.axis_index("batch")
    return lax.rem(index * chunk, FRAME_ROWS * LANES)


def segment_ids(lengths, idk_ref, idq_ref, place, tokens):
    rows, length = idk_ref.shape[0], idk_ref.shape[1]
    upto = lax.broadcasted_iota(jnp.int32, (SEGS, LANES), 0) <= lax.broadcasted_iota(jnp.int32, (SEGS, LANES), 1)
    upto = jnp.where(upto, 1.0, 0.0).astype(BF)
    values = lengths.astype(F32)
    high = jnp.floor(values * (1.0 / 64))
    low = (values - 64.0 * high).astype(BF)
    high = high.astype(BF)
    ends = mm(high, upto) * 64.0 + mm(low, upto)
    ends = jnp.where(lax.broadcasted_iota(jnp.int32, (rows, LANES), 1) < SEGS, ends, 1e9)
    upto = upto[:, :SEGS]
    ends_down = lax.dot_general(upto, high, (((0,), (1,)), ((), ())), preferred_element_type=F32) * 64.0
    ends_down = ends_down + lax.dot_general(upto, low, (((0,), (1,)), ((), ())), preferred_element_type=F32)
    ones = jnp.ones((LANES, LANES), BF)
    span = 256
    for m in range(rows):

        def fill(i, carry, m=m):
            at = pl.multiple_of(i * span, span)
            places = (at + lax.broadcasted_iota(jnp.int32, (span, LANES), 0)).astype(F32)
            passed = jnp.where(ends[m : m + 1] <= places, 1.0, 0.0).astype(BF)
            seg = mm(passed, ones)
            idk_ref[m, pl.ds(at, span), :] = jnp.where(seg < SEGS, seg, SEGS + places)
            return carry

        lax.fori_loop(0, length // span, fill, 0)
        for h in range(H):
            first = ((h * place.parts + place.g) * tokens + lax.broadcasted_iota(jnp.int32, (1, tokens), 1)).astype(F32)
            seg = column_sum(jnp.where(ends_down[:, m : m + 1] <= first, 1.0, 0.0))
            group, k = h // GROUP, h % GROUP
            idq_ref[m, group, :, k * tokens : (k + 1) * tokens] = jnp.where(seg < SEGS, seg, SEGS + first)


def layer_kernel(
    groups_ref, lengths_ref, tok_ref, cot_ref, attn_ref, ffn_ref, params_ref, arows_ref, acols_ref, frows_ref,
    fcols_ref, sq_ref,
    out_hbm, du_hbm, agrad_hbm, fgrad_hbm, update_a_hbm, update_f_hbm, scales_ref, rows_new_ref, acols_new_ref,
    fcols_new_ref, own_new_ref,
    *scratch,
):
    place = Place()
    scratch = list(scratch)
    own_sems, recv_sems, send_sems = scratch.pop(), scratch.pop(), scratch.pop()
    wire = Wire(send_sems, recv_sems)

    def take(count):
        taken = scratch[:count]
        del scratch[:count]
        return taken

    pack_low, kv_low, wo_low, ffn_low, own_ref, small_ref, pack_ref, wkv_ref, wo_ref, w1_ref, w2_ref = take(11)
    idk_ref, idq_ref, q_ref, kv_ref, qsend_ref, kvsend_ref, qm_ref, dom_ref = take(8)
    peak_ref, acc_ref, ot_ref, lse_ref, delta_ref, o_ref, otile_ref, dotile_ref, do_ref = take(9)
    act_ref, slope_ref, dz_ref, sum_ref, frames_ref = take(5)
    dqt_ref, part_ref, near_ref, dkv_sum, dq_ref, dq_back, dkv_back = take(7)
    dwo_ref, dw1_ref, dw2_ref, dkv_w_ref, dq_w_ref, dsmall_ref = take(6)
    cols_plane, rows_plane, all_z, late_cols, late_rows, late_sums, all_sums = take(7)
    out_ref, du_ref, agrad_ref, fgrad_ref, update_a, update_f = take(6)
    written = [
        pltpu.make_async_copy(src, dst, own_sems.at[5 + i])
        for i, (src, dst) in enumerate(
            (
                (out_ref, out_hbm),
                (du_ref, du_hbm),
                (agrad_ref, agrad_hbm),
                (fgrad_ref, fgrad_hbm),
                (update_a, update_a_hbm),
                (update_f, update_f_hbm),
            )
        )
    ]
    n_z, n_b, parts = place.n_z, place.n_b, place.parts
    rows = 2
    count = tok_ref.shape[0]
    tokens = count // rows
    r, cols = attn_ref.shape[1:]
    cols_f = ffn_ref.shape[2]
    groups = H // GROUP
    width = GROUP * tokens
    keys = parts * tokens
    scale2 = SCALE * LOG2E
    low = low_half()

    plane = [(dx, db) for db in range(n_b) for dx in range(4) if dx or db]

    def plane_peer(dx, db):
        return (place.z * 4 + place.xc_ahead[dx], place.batch_ahead(db))

    along = [place.along_z(k) for k in range(1, n_z)]
    all_here = greet_all(place)

    chunk = params_ref.shape[0]
    own_at = own_place(chunk)
    own = to_frame(params_ref[...].reshape(1, chunk), own_at)
    own_ref[...] = own
    pack_low[0, :r] = attn_ref[0].astype(BF)
    tile = jnp.concatenate([own, jnp.zeros((8, LANES), F32)], axis=0)
    if cols < LANES:
        tile = jnp.concatenate([own[:, :cols], own[:, cols:]], axis=0)
    if cols > LANES:
        tile = jnp.concatenate([tile, jnp.zeros((16, cols - LANES), F32)], axis=1)
    pack_low[0, r:] = tile.astype(BF)
    kv_low[...] = attn_ref[1:3].astype(BF)
    all_here()
    pack = ShortGather(place, wire, pack_low, pack_ref, own_sems.at[0], n_z)
    kv_w = ShortGather(place, wire, kv_low, wkv_ref, own_sems.at[4], n_z)
    wo_low[0] = attn_ref[3].astype(BF)
    ffn_low[...] = ffn_ref[...].astype(BF)
    segment_ids(lengths_ref[...], idk_ref, idq_ref, place, tokens)
    for i in range(rows * groups):
        peak_ref[i] = jnp.full((1, width), NEG, F32)
        acc_ref[i] = jnp.zeros((HD + 16, width), F32)
    frames_ref[...] = jnp.zeros_like(frames_ref)
    dqt_ref[...] = jnp.zeros_like(dqt_ref)
    pack.to_plane()
    kv_w.to_plane()
    most = n_z - n_z // 4
    first = PairGather(place, wire, ffn_low.at[pl.ds(0, 1)], w1_ref, own_sems.at[1], most)
    out_w = PairGather(place, wire, wo_low, wo_ref, own_sems.at[2], most)
    second = PairGather(place, wire, ffn_low.at[pl.ds(1, 1)], w2_ref, own_sems.at[3], most)
    pack.to_cores()
    pack.finish()
    frame = place.n_s * n_b // FRAMES
    for f in range(FRAMES):
        total = None
        for i in range(f * frame, (f + 1) * frame):
            s, b = i // n_b, i % n_b
            tile = pack_ref[b, 0, s // 4, s % 4, r:].astype(F32)
            if cols < LANES:
                tile = jnp.concatenate([tile[:8], tile[8:]], axis=1)
            tile = tile[:8, :LANES]
            total = tile if total is None else total + tile
        small_ref[f] = total
    lang = language_rows(groups_ref, small_ref, rows)
    first.to_pair()
    out_w.to_pair()

    def inputs():
        return jnp.concatenate(
            [tok_ref[m * tokens : (m + 1) * tokens].astype(F32) + lang[m] for m in range(rows)], axis=0
        )

    def w_qkv(b, j):
        w = wkv_ref[b, j - 1] if j else pack_ref[b, 0, :, :, :r]
        return w.reshape(D, cols)

    a = inputs().astype(BF)

    def project(j, bias):
        out = jnp.concatenate([mm(a, w_qkv(b, j)) for b in range(n_b)], axis=1)
        if bias is not None:
            out = out + small_piece(small_ref, bias, 4)
        return [t.astype(BF) for t in rows_to_heads(out[:tokens], out[tokens:])]

    for h, t in enumerate(project(0, ROW_BQ)):
        qsend_ref[h] = t
    q_ref[place.h] = qsend_ref[place.h]
    def to_heads(src, dst):
        return [
            wire.send(lambda k=k: (src.at[place.head_ahead(k)], dst.at[place.h], place.across_heads(k)))
            for k in outwards(H)
        ]

    moved_q = to_heads(qsend_ref, q_ref)
    second.to_pair()
    kv_w.to_cores()
    first.to_plane()
    out_w.to_plane()
    kv_w.finish()
    for j, bias in ((0, None), (1, ROW_BV)):
        for h, t in enumerate(project(1 + j, bias)):
            kvsend_ref[h, j] = t
    kv_ref[place.s] = kvsend_ref[place.h]
    kv_sems = wire.reserve(H)
    share_sems = wire.reserve(H * (parts - 1))

    def moved_kv(i):
        k = far_first(i)
        return wire.make(
            kv_sems + i, kvsend_ref.at[place.head_ahead(k)], kv_ref.at[place.s], place.across_heads(k)
        )

    def ordered(i):
        return far_first(i) if isinstance(i, int) else jnp.where(i == 0, 0, far_first(i))

    def shared_kv(i, j):
        slot = kv_ref.at[place.head_behind(ordered(i)) * parts + place.g]
        return wire.make(share_sems + i * (parts - 1) + j - 1, slot, slot, place.across_parts(j))

    for j in range(1, parts):
        shared_kv(0, j).start()
    for k in range(1, H):
        moved_kv(k).start()
    second.to_plane()

    def masked_rows(src_ref, dst_ref):
        for g in range(groups):
            both = src_ref[g * GROUP : (g + 1) * GROUP].reshape(width, LANES)
            zero = jnp.zeros_like(both)
            dst_ref[0, g] = jnp.where(low, both, zero)
            dst_ref[1, g] = jnp.where(low, zero, both)

    received(moved_q)
    masked_rows(q_ref, qm_ref)

    def pair(h):
        kv = kv_ref[pl.ds(h * parts, parts)]
        return kv[:, 0].reshape(keys, LANES), kv[:, 1].reshape(keys, LANES)

    def key_ids(h, m):
        ids = idk_ref[m, pl.ds(pl.multiple_of(h * keys, keys), keys), :]
        return jnp.concatenate([ids] * (width // LANES), axis=1)

    def attend(k):
        h = place.head_behind(ordered(k))
        ids = [key_ids(h, m) for m in range(rows)]
        for j in range(1, parts):
            shared_kv(k, j).wait_recv()
        key, value = pair(h)
        value_t = value.T
        ones = jnp.ones((16, keys), BF)
        for g in range(groups):
            for m in range(rows):
                i = g * rows + m
                s = jnp.where(ids[m] == idq_ref[m, g], mm_nt(key, qm_ref[m, g]) * scale2, NEG)
                new = jnp.maximum(peak_ref[i], jnp.max(s, axis=0, keepdims=True))
                p = jnp.exp2(s - new).astype(BF)
                alpha = jnp.exp2(peak_ref[i] - new)
                left = jnp.concatenate([value_t[m * HD : (m + 1) * HD], ones], axis=0)
                acc_ref[i] = acc_ref[i] * alpha + mm(left, p)
                peak_ref[i] = new

    def meanwhile(k, *stages):
        for at, stage in stages:
            pl.when(k == at)(stage)

    def forward_step(k, carry):
        moved_kv(k).wait_recv()
        for j in range(1, parts):
            shared_kv(k, j).start()
        attend(k - 1)
        meanwhile(
            k,
            (2, first.to_diagonal),
            (2, out_w.to_diagonal),
            (H - 1, second.to_diagonal),
        )
        return carry

    lax.fori_loop(1, H, forward_step, 0)
    attend(H - 1)
    for g in range(groups):
        for m in range(rows):
            i = g * rows + m
            total = acc_ref[i, HD : HD + 1]
            ot_ref[g, m * HD : (m + 1) * HD] = acc_ref[i, :HD] * (1.0 / total)
            lse_ref[i] = peak_ref[i] + jnp.log2(total)
        o_ref[g * GROUP : (g + 1) * GROUP] = ot_ref[g].T.astype(BF).reshape(GROUP, tokens, LANES)
    moved = to_heads(o_ref, otile_ref)
    otile_ref[place.h] = o_ref[place.h]
    for piece in (out_w, first, second):
        piece.to_cores()

    tiles, wide = act_ref.shape[0], act_ref.shape[2]
    per_b = cols_f // wide
    bias_1 = [small_piece(small_ref, ROW_B1 + i * wide // LANES, wide // LANES) for i in range(tiles)]
    gain1, shift1 = small_piece(small_ref, ROW_G1, 4), small_piece(small_ref, ROW_S1, 4)
    gain2, shift2 = small_piece(small_ref, ROW_G2, 4), small_piece(small_ref, ROW_S2, 4)
    bias_o, bias_2 = small_piece(small_ref, ROW_BO, 4), small_piece(small_ref, ROW_B2, 4)

    def block(ref, i):
        at = i % per_b * wide
        return ref[i // per_b, 0, :, :, :, at : at + wide].reshape(D, wide)

    def joined(ref, b):
        return jnp.concatenate([ref[b * per_b + i] for i in range(per_b)], axis=1)

    live = jnp.concatenate(
        [idk_ref[m, pl.ds(pl.multiple_of(place.s * tokens, tokens), tokens), :] for m in range(rows)], axis=0
    )
    live = jnp.where(live < SEGS, 1.0, 0.0)
    u = inputs()
    out_w.finish()
    first.finish()
    received(moved)
    mixed = jnp.concatenate(heads_to_rows([otile_ref[h].astype(F32) for h in range(H)]), axis=0).astype(BF)
    attn_out = jnp.concatenate([mm(mixed, wo_ref[b, 0].reshape(D, cols)) for b in range(n_b)], axis=1)
    normed1, inverse1 = normed_of(u + (attn_out + bias_o))
    hidden = normed1 * gain1 + shift1
    hb = hidden.astype(BF)
    for i in range(tiles):
        act, slope = gelu_pair(mm(hb, block(w1_ref, i)) + bias_1[i])
        slope_ref[i] = slope
        act_ref[i] = act.astype(BF)
    second.finish()
    total = hidden + u + bias_2
    for b in range(n_b):
        total = total + mm_nt(joined(act_ref, b), w2_ref[b, 0].reshape(D, cols_f))

    normed2, inverse2 = normed_of(total)
    out_ref[...] = (normed2 * gain2 + shift2).astype(BF)
    c = cot_ref[...].astype(F32) * jnp.concatenate([live] * (D // LANES), axis=1)
    dr = norm_back(c * gain2, normed2, inverse2)
    df = dr.astype(BF)

    def scatter(part):
        return PairScatter(place, wire, part, *take(SCATTER_SCRATCH))

    g_first, g_second, g_out = scatter(dw1_ref), scatter(dw2_ref), scatter(dwo_ref)
    g_kv = Scatter(place, wire, dkv_w_ref, *take(SCATTER_SCRATCH))
    g_q = ShortScatter(place, wire, dq_w_ref, *take(SHORT_SCRATCH))
    g_small = ShortScatter(place, wire, dsmall_ref, *take(SHORT_SCRATCH))

    def weight_grad(left, right_ref, dst_ref):
        left = left.T
        for i in range(tiles):
            at = i % per_b * wide
            grad = mm(left, right_ref[i]).astype(BF).reshape(n_z, 2, 2, r, wide)
            dst_ref[i // per_b, 0, :, :, :, :, at : at + wide] = grad

    weight_grad(df, act_ref, dw2_ref)
    g_second.to_core()
    dh = dr
    for i in range(tiles):
        dz = (mm(df, block(w2_ref, i)) * slope_ref[i]).astype(BF)
        dz_ref[i] = dz
    for b in range(n_b):
        dh = dh + mm_nt(joined(dz_ref, b), w1_ref[b, 0].reshape(D, cols_f))
    dpre = norm_back(dh * gain1, normed1, inverse1)
    dattn = dpre.astype(BF)
    do = mm_nt(dattn[:, :cols], wo_ref[0, 0].reshape(D, cols))
    for b in range(1, n_b):
        do = do + mm_nt(dattn[:, b * cols : (b + 1) * cols], wo_ref[b, 0].reshape(D, cols))
    for h, t in enumerate(rows_to_heads(do[:tokens], do[tokens:])):
        dotile_ref[h] = t.astype(BF)
    moved = to_heads(dotile_ref, do_ref)
    written[0].start()
    do_ref[place.h] = dotile_ref[place.h]
    sum_ref[...] = dpre + dr

    g_second.to_diagonal()
    weight_grad(hb, dz_ref, dw1_ref)
    g_first.to_core()
    mixed_t = mixed.T
    for b in range(n_b):
        dwo = mm(mixed_t, dattn[:, b * cols : (b + 1) * cols]).astype(BF)
        dwo_ref[b, 0] = dwo.reshape(n_z, 2, 2, r, cols)
    g_out.to_core()
    for k in range(H):
        for j in range(1, parts):
            shared_kv(k, j).wait_send()
        if k:
            moved_kv(k).wait_send()
    wire.drain()

    g_first.to_diagonal()
    g_out.to_diagonal()
    add_small(frames_ref, ROW_G2, column_sum(c * normed2))
    add_small(frames_ref, ROW_S2, column_sum(c))
    add_small(frames_ref, ROW_B2, column_sum(df.astype(F32)))
    for i in range(tiles):
        add_small(frames_ref, ROW_B1 + i * wide // LANES, column_sum(dz_ref[i].astype(F32)))
    add_small(frames_ref, ROW_G1, column_sum(dh * normed1))
    add_small(frames_ref, ROW_S1, column_sum(dh))
    add_small(frames_ref, ROW_BO, column_sum(dattn.astype(F32)))
    received(moved)
    masked_rows(do_ref, dom_ref)
    g_second.to_plane()
    for g in range(groups):
        product = do_ref[g * GROUP : (g + 1) * GROUP].reshape(width, LANES).astype(F32).T * ot_ref[g]
        for m in range(rows):
            delta_ref[g * rows + m] = column_sum(product[m * HD : (m + 1) * HD])

    near_sems = wire.reserve(H * (parts - 1))
    back_sems = wire.reserve(H)

    def target(k):
        far = far_first(k) if isinstance(k, int) else jnp.where(k == H, H, far_first(k))
        return place.head_ahead(far)

    def near_kv(k, j):
        h = target(k)
        return wire.make(
            near_sems + (k - 1) * (parts - 1) + j - 1,
            part_ref.at[h, place.part_ahead(j)],
            near_ref.at[j - 1, h],
            place.across_parts(j),
        )

    def back_kv(k):
        h = target(k)
        return wire.make(back_sems + k - 1, dkv_sum.at[h], dkv_back.at[place.h], (h * parts + place.g, place.b))

    def fold(k):
        h = target(k)
        total = part_ref[h, place.g].astype(F32)
        for j in range(1, parts):
            near_kv(k, j).wait_recv()
            total = total + near_ref[j - 1, h].astype(F32)
        return total.astype(BF)

    def key_step(k):
        h = target(k)
        key, value = pair(h)
        key_t = key.T
        ids = [key_ids(h, m) for m in range(rows)]
        dk = jnp.zeros((keys, LANES), F32)
        dv = jnp.zeros((keys, LANES), F32)
        for g in range(groups):
            for m in range(rows):
                i = g * rows + m
                p = jnp.exp2(mm_nt(key, qm_ref[m, g]) * scale2 - lse_ref[i])
                p = jnp.where(ids[m] == idq_ref[m, g], p, 0.0)
                ds = (p * (mm_nt(value, dom_ref[m, g]) - delta_ref[i])).astype(BF)
                dv = dv + mm(p.astype(BF), dom_ref[m, g])
                dk = dk + mm(ds, qm_ref[m, g])
                dqt_ref[g, m * HD : (m + 1) * HD] += mm(key_t[m * HD : (m + 1) * HD], ds)
        part_ref[h, :, 0] = (dk * SCALE).astype(BF).reshape(parts, tokens, LANES)
        part_ref[h, :, 1] = dv.astype(BF).reshape(parts, tokens, LANES)
        for j in range(1, parts):
            near_kv(k, j).start()

    def backward_step(k, carry):
        key_step(k)
        dkv_sum[target(k - 1)] = fold(k - 1)
        back_kv(k - 1).start()
        meanwhile(
            k,
            (6, g_first.to_plane),
            (6, g_out.to_plane),
        )
        return carry

    token_pieces = (g_second, g_first, g_out)
    key_step(1)
    lax.fori_loop(2, H + 1, backward_step, 0)
    for g in range(groups):
        dq_ref[g * GROUP : (g + 1) * GROUP] = (dqt_ref[g] * SCALE).T.astype(BF).reshape(GROUP, tokens, LANES)
    moved = to_heads(dq_ref, dq_back)
    dq_back[place.h] = dq_ref[place.h]
    dkv_back[place.h] = fold(H)
    g_second.to_owner()

    def to_rows(parts_of):
        return jnp.concatenate(heads_to_rows([t.astype(F32) for t in parts_of]), axis=0).astype(BF)

    def grad_of(left, right, b):
        return mm(left, right[:, b * cols : (b + 1) * cols]).astype(BF).reshape(n_z, 2, 2, r, cols)

    def back_through(total, right, j):
        for b in range(n_b):
            total = total + mm_nt(right[:, b * cols : (b + 1) * cols], w_qkv(b, j))
        return total

    for k in range(1, H):
        back_kv(k).wait_recv()
    a_t = inputs().astype(BF).T
    dk = to_rows([dkv_back[h, 0] for h in range(H)])
    dv = to_rows([dkv_back[h, 1] for h in range(H)])
    for b in range(n_b):
        dkv_w_ref[b, 0] = grad_of(a_t, dk, b)
        dkv_w_ref[b, 1] = grad_of(a_t, dv, b)
    g_kv.to_core()
    add_small(frames_ref, ROW_BV, column_sum(dv.astype(F32)))
    du = back_through(back_through(sum_ref[...], dk, 1), dv, 2)
    g_kv.to_diagonal()
    g_second.to_far()
    g_first.to_owner()
    g_out.to_owner()
    received(moved)
    dq = to_rows([dq_back[h] for h in range(H)])
    for b in range(n_b):
        dq_w_ref[b, 0] = grad_of(a_t, dq, b)
    g_q.to_core()
    du = back_through(du, dq, 0)
    add_small(frames_ref, ROW_BQ, column_sum(dq.astype(F32)))
    sums = [column_sum(du[m * tokens : (m + 1) * tokens]) for m in range(rows)]
    for e in range(GROUPS):
        total = jnp.zeros_like(sums[0])
        for m in range(rows):
            total = total + jnp.where(groups_ref[m] == e, sums[m], 0.0)
        add_small(frames_ref, ROW_E + 4 * e, total)
    for s in range(place.n_s):
        for b in range(n_b):
            dsmall_ref[b, 0, s // 4, s // 2 % 2, s % 2] = frames_ref[(s * n_b + b) // frame]
    g_small.to_core()
    g_q.to_plane()
    g_kv.to_plane()
    g_small.to_plane()
    g_first.to_far()
    g_out.to_far()
    du_ref[...] = du.astype(BF)
    written[1].start()
    g_kv.to_owner()

    weights = [attn_ref.at[j] for j in range(4)] + [ffn_ref.at[j] for j in range(2)]
    outs = [agrad_ref.at[j] for j in range(4)] + [fgrad_ref.at[j] for j in range(2)]
    updates = [update_a.at[j] for j in range(4)] + [update_f.at[j] for j in range(2)]
    old_cols = [acols_ref[j : j + 1] for j in range(4)] + [fcols_ref[j : j + 1] for j in range(2)]
    owners = [(g_q, 0), (g_kv, 0), (g_kv, 1), (g_out, 0), (g_first, 0), (g_second, 0)]
    spans = [cols] * 4 + [cols_f] * 2
    places, used = [], 0
    for span in spans:
        places.append(used)
        used += -(-span // LANES)
    pad = cols_plane.shape[1]
    late = 3
    mine = cols_plane.at[place.xc]
    mine_rows = rows_plane.at[place.b, place.xc]
    mine_late = late_cols.at[place.s]
    mine_late_rows = late_rows.at[place.b]
    mine_sums = late_sums.at[place.b, place.s]
    mine[...] = jnp.zeros((pad, LANES), F32)
    mine_late[...] = jnp.zeros((8, LANES), F32)
    lane = lax.broadcasted_iota(jnp.int32, (r, LANES), 1)
    square_sums = [None] * SLABS
    old_rows = jnp.concatenate([arows_ref[...], frows_ref[...], jnp.zeros((2, r), F32)], axis=0).T
    old_rows = [old_rows[:, j : j + 1] for j in range(SLABS)]
    row_sums_old = [sum_all(x) for x in old_rows]
    weight_squares = [sum_all(w[...] * w[...]) for w in weights]
    own = own_ref[...]
    entry = lax.broadcasted_iota(jnp.int32, (8, LANES), 0) * LANES + lax.broadcasted_iota(jnp.int32, (8, LANES), 1)
    own_mask = jnp.where((entry >= own_at) & (entry < own_at + chunk), 1.0, 0.0)
    weight_squares.append(sum_all(own * own))
    rows_tiles = []

    def gradient(j):
        owner, slab = owners[j]
        grad = owner.total(slab)
        outs[j][...] = grad
        square = grad * grad + EPS_ONE
        row_sum = jnp.sum(square, axis=1, keepdims=True)
        col_sum = column_sum(square)
        ref = mine_late if j < late else mine
        for k in range(0, spans[j], LANES):
            span = min(LANES, spans[j] - k)
            ref[pl.ds(places[j] + k // LANES, 1), pl.ds(0, span)] = col_sum[:, k : k + span]
        square_sums[j] = sum_all(row_sum)
        return jnp.where(lane == j, row_sum, 0.0)

    def renewed(j, row_total, sums, square_total, old_total):
        length = D if j < 4 else FF
        new_rows = DECAY * old_rows[j] + (1.0 - DECAY) * row_total[:, j : j + 1] * (1.0 / length)
        rows_tiles.append(jnp.where(lane == j, new_rows, 0.0))
        mean_rows = (DECAY / n_b * old_total + (1.0 - DECAY) * (1.0 / length) * square_total) * (1.0 / D)
        pieces = [
            sums[places[j] + k // LANES : places[j] + k // LANES + 1, : min(LANES, spans[j] - k)]
            for k in range(0, spans[j], LANES)
        ]
        col_sum = pieces[0] if len(pieces) == 1 else jnp.concatenate(pieces, axis=1)
        new = DECAY * old_cols[j] + (1.0 - DECAY) * (1.0 / D) * col_sum
        if j < 4:
            acols_new_ref[j : j + 1, :] = new
        else:
            fcols_new_ref[j - 4 : j - 3, :] = new
        update = outs[j][...] * lax.rsqrt((new_rows / mean_rows) * new)
        updates[j][...] = update
        return sum_all(update * update)

    def pick(tile, j):
        return tile[0:1, j : j + 1]

    def fan(i, ref, offsets):
        for db in offsets:
            b = place.batch_ahead(db)

            def one(k, carry=0, b=b):
                wire.make(i, ref, ref, (wrap(place.s + k, place.n_s), b)).start()
                return carry

            if place.n_s > 16:
                lax.fori_loop(0 if db else 1, place.n_s, one, 0)
            else:
                for k in outwards(place.n_s) + [0] * (db > 0):
                    one(k)

    near, others = [0], list(range(1, n_b))
    one_peer = place.along_z(1)

    g_second.finish()
    row_tile = gradient(5)
    g_q.to_owner()
    g_small.to_owner()
    g_first.finish()
    g_out.finish()
    mine_rows[pl.ds(0, r), :] = row_tile + gradient(4) + gradient(3)
    tail = pl.ds(r, 8)
    mine_rows[tail, :] = lanes_of(square_sums + row_sums_old + weight_squares)
    moved = []
    for dx, db in plane:
        peer = plane_peer(dx, db)
        if db == 0:
            moved.append(wire.send(lambda peer=peer: (mine, mine, peer)))
        if dx == 0:
            moved.append(wire.send(lambda peer=peer: (mine_rows, mine_rows, peer)))
        else:
            moved.append(wire.send(lambda peer=peer: (mine_rows.at[tail], mine_rows.at[tail], peer)))
    g_kv.finish()
    row_tile = gradient(1) + gradient(2)
    g_q.finish()
    mine_late_rows[...] = row_tile + gradient(0)
    written[2].start()
    written[3].start()
    sums = lanes_of(square_sums[:late])[0:1]
    mine_late[7:8, :] = sums
    late_sums[place.b] = jnp.zeros((place.n_s, 1, LANES), F32)
    mine_sums[...] = sums
    late_i, sums_i, all_i = wire.reserve(1), wire.reserve(1), wire.reserve(1)
    moved_rows = [
        wire.send(lambda k=k: (mine_late_rows, mine_late_rows, place.across_batch(k))) for k in range(1, n_b)
    ]
    fan(late_i, mine_late, near)
    fan(sums_i, mine_sums, others)

    received(moved)
    mine_z = all_z.at[place.z]
    mine_z[pl.ds(0, pad), :] = cols_plane[0] + cols_plane[1] + cols_plane[2] + cols_plane[3]
    scalars = jnp.zeros((8, LANES), F32)
    row_total = jnp.zeros((r, LANES), F32)
    for b in range(n_b):
        for xc in range(4):
            scalars = scalars + rows_plane[b, xc, tail, :]
        row_total = row_total + rows_plane[b, place.xc, pl.ds(0, r), :]
    mine_z[pl.ds(pad, 8), :] = scalars
    moved = [wire.send(lambda peer=peer: (mine_z, mine_z, peer)) for peer in along]

    received(moved)
    reduced = all_z[0]
    for z in range(1, n_z):
        reduced = reduced + all_z[z]
    tile = reduced[pad:]

    def scalar(j):
        return pick(tile, j)

    update_squares = [None] * SLABS
    for j in range(late, SLABS):
        update_squares[j] = renewed(j, row_total, reduced, scalar(j), scalar(SLABS + j))
    g_small.finish()
    own_grad = g_small.total(0) * own_mask
    own_sq = DECAY * to_frame(sq_ref[...].reshape(1, chunk), own_at) + (1.0 - DECAY) * (own_grad * own_grad + EPS_ONE)
    own_update = own_grad * lax.rsqrt(own_sq)
    update_squares.append(sum_all(own_update * own_update))
    for k in range(1, H + 1):
        for j in range(1, parts):
            near_kv(k, j).wait_send()
        if k < H:
            back_kv(k).wait_send()
    wire.drain()

    late_part = late_cols.at[pl.ds(0, place.n_s - 1)]
    sums_part = late_sums.at[pl.ds(0, n_b - 1)]
    wire.make(late_i, late_part, late_part, one_peer).wait_recv()
    wire.make(sums_i, sums_part, sums_part, one_peer).wait_recv()
    received(moved_rows)
    sums = late_cols[0]
    for s in range(1, place.n_s):
        sums = sums + late_cols[s]
    totals = jnp.zeros((1, LANES), F32)
    row_total = jnp.zeros((r, LANES), F32)
    for b in range(n_b):
        other = late_sums[b, 0]
        for s in range(1, place.n_s):
            other = other + late_sums[b, s]
        totals = totals + jnp.where(place.b == b, sums[7:8], other)
        row_total = row_total + late_rows[b]
    for j in range(late):
        update_squares[j] = renewed(j, row_total, sums, pick(totals, j), scalar(SLABS + j))
    written[4].start()
    written[5].start()
    rows_new_ref[...] = sum(rows_tiles[1:], rows_tiles[0])
    mine_u = all_sums.at[place.b * place.n_s + place.s]
    mine_u[...] = lanes_of(update_squares)[0:1]
    fan(all_i, mine_u, near + others)
    wire.make(late_i, late_part, late_part, one_peer).wait_send()
    wire.make(sums_i, sums_part, sums_part, one_peer).wait_send()
    all_part = all_sums.at[pl.ds(0, place.n_s * n_b - 1)]
    copy = wire.make(all_i, all_part, all_part, one_peer)
    copy.wait_send()
    copy.wait_recv()
    update_tile = jnp.zeros((1, LANES), F32)
    for i in range(place.n_s * n_b):
        update_tile = update_tile + all_sums[i]
    sizes = [D * D] * 4 + [D * FF] * 2 + [NVEC]

    def scale(j):
        weight = jnp.sqrt(scalar(2 * SLABS + j) * (1.0 / sizes[j]))
        return LEARN * weight / jnp.maximum(1.0, jnp.sqrt(update_tile[0:1, j : j + 1] * (1.0 / sizes[j])))

    scales_ref[...] = lanes_of([scale(j) for j in range(SLABS)])
    own_new_ref[0] = own_grad
    own_new_ref[1] = own - scale(SLABS) * own_update
    own_new_ref[2] = own_sq
    for copy in written:
        copy.wait()
    wire.drain()


def layer_part(groups, lengths, tok, cot, attn, ffn, params, arows, acols, frows, fcols, sq):
    n_s, n_b = lax.axis_size("seq"), lax.axis_size("batch")
    n_z, parts = n_s // 4, n_s // H
    count = tok.shape[0]
    tokens = count // 2
    rows = 2
    _, r, cols = attn.shape
    cols_f = ffn.shape[2]
    groups_q = H // GROUP
    width = GROUP * tokens
    length = tokens * n_s
    wide = min(512, cols_f)
    tiles = FF // wide
    pad = 4 * -(-cols // LANES) + 2 * (cols_f // LANES)
    pad = -(-pad // 8) * 8
    gather = (n_z - 1) + (1 + n_b) + 2 * (n_b - 1) + 1 + (n_b - 1) + 2 * (n_b - 1)
    copies = 5 * gather + 7 * (H - 1) + 2 * H + 2 * H * (parts - 1)
    copies += 6 * (1 + 2 * (n_b - 1) + n_b + n_z - 1)
    copies += 6 + 4 * n_b + (n_z - 1) + (n_b - 1) + 3

    def shape(dims, kind):
        return jax.ShapeDtypeStruct(dims, kind)

    out = (
        shape(tok.shape, BF),
        shape(tok.shape, BF),
        shape(attn.shape, F32),
        shape(ffn.shape, F32),
        shape(attn.shape, F32),
        shape(ffn.shape, F32),
        shape((8, LANES), F32),
        shape((r, LANES), F32),
        shape(acols.shape, F32),
        shape(fcols.shape, F32),
        shape((3, 8, LANES), F32),
    )
    vmem = pltpu.VMEM
    heads = (H, tokens, LANES)
    scratch = [
        vmem((1, r + 16, cols), BF),
        vmem((2, r, cols), BF),
        vmem((1, r, cols), BF),
        vmem(ffn.shape, BF),
        vmem((8, LANES), F32),
        vmem((FRAMES, 8, LANES), F32),
        vmem((n_b, 1, n_z, 4, r + 16, cols), BF),
        vmem((n_b, 2, n_z, 4, r, cols), BF),
        vmem((n_b, 1, n_z, 4, r, cols), BF),
        vmem((n_b, 1, n_z, 4, r, cols_f), BF),
        vmem((n_b, 1, n_z, 4, r, cols_f), BF),
        vmem((rows, length, LANES), F32),
        vmem((rows, groups_q, 1, width), F32),
        vmem(heads, BF),
        vmem((n_s, 2, tokens, LANES), BF),
        vmem(heads, BF),
        vmem((H, 2, tokens, LANES), BF),
        vmem((rows, groups_q, width, LANES), BF),
        vmem((rows, groups_q, width, LANES), BF),
        vmem((rows * groups_q, 1, width), F32),
        vmem((rows * groups_q, HD + 16, width), F32),
        vmem((groups_q, LANES, width), F32),
        vmem((rows * groups_q, 1, width), F32),
        vmem((rows * groups_q, 1, width), F32),
        vmem(heads, BF),
        vmem(heads, BF),
        vmem(heads, BF),
        vmem(heads, BF),
        vmem((tiles, count, wide), BF),
        vmem((tiles, count, wide), F32),
        vmem((tiles, count, wide), BF),
        vmem((count, D), F32),
        vmem((FRAMES, 8, LANES), F32),
        vmem((groups_q, LANES, width), F32),
        vmem((H, parts, 2, tokens, LANES), BF),
        vmem((parts - 1, H, 2, tokens, LANES), BF),
        vmem((H, 2, tokens, LANES), BF),
        vmem(heads, BF),
        vmem(heads, BF),
        vmem((H, 2, tokens, LANES), BF),
        vmem((n_b, 1, n_z, 2, 2, r, cols), BF),
        vmem((n_b, 1, n_z, 2, 2, r, cols_f), BF),
        vmem((n_b, 1, n_z, 2, 2, r, cols_f), BF),
        vmem((n_b, 2, n_z, 2, 2, r, cols), BF),
        vmem((n_b, 1, n_z, 2, 2, r, cols), BF),
        vmem((n_b, 1, n_z, 2, 2, 8, LANES), F32),
        vmem((4, pad, LANES), F32),
        vmem((n_b, 4, r + 8, LANES), F32),
        vmem((n_z, pad + 8, LANES), F32),
        vmem((n_s, 8, LANES), F32),
        vmem((n_b, r, LANES), F32),
        vmem((n_b, n_s, 1, LANES), F32),
        vmem((n_b * n_s, 1, LANES), F32),
        vmem(tok.shape, BF),
        vmem(tok.shape, BF),
        vmem(attn.shape, F32),
        vmem(ffn.shape, F32),
        vmem(attn.shape, F32),
        vmem(ffn.shape, F32),
    ]
    scratch += scatter_scratch(n_b, 1, n_z, r, cols_f, BF) * 2
    scratch += scatter_scratch(n_b, 1, n_z, r, cols, BF)
    scratch += scatter_scratch(n_b, 2, n_z, r, cols, BF)
    scratch += short_scratch(n_b, 1, n_z, r, cols, BF)
    scratch += short_scratch(n_b, 1, n_z, 8, LANES, F32)
    dma = pltpu.SemaphoreType.DMA
    scratch += [dma((copies,)), dma((copies,)), dma((11,))]
    return pl.pallas_call(
        layer_kernel,
        out_shape=out,
        in_specs=[SMEM_SPEC] + [VMEM_SPEC] * 11,
        out_specs=(pl.BlockSpec(memory_space=pl.ANY),) * 6 + (VMEM_SPEC,) * 5,
        scratch_shapes=scratch,
        compiler_params=pltpu.CompilerParams(
            vmem_limit_bytes=63 * 2**20, collective_id=0, has_side_effects=True
        ),
    )(groups, lengths, tok, cot, attn, ffn, params, arows, acols, frows, fcols, sq)


def result_kernel(
    out_in, du_in, agrad_in, fgrad_in, update_a, update_f, scales_ref, rows_ref, acols_in, fcols_in, own_ref,
    attn_ref, ffn_ref,
    out_ref, du_ref, agrad_ref, fgrad_ref, grad_ref, anew_ref, fnew_ref, new_ref, acopy_ref, fcopy_ref, copy_ref,
    arows_ref, acols_ref, frows_ref, fcols_ref, sq_ref,
):
    for src, dst in ((out_in, out_ref), (du_in, du_ref), (agrad_in, agrad_ref), (fgrad_in, fgrad_ref)):
        dst[...] = src[...]
    for j in range(4):
        new = attn_ref[j] - scales_ref[0:1, j : j + 1] * update_a[j]
        anew_ref[j] = new
        acopy_ref[j] = new.astype(BF)
    for j in range(2):
        new = ffn_ref[j] - scales_ref[0:1, 4 + j : 5 + j] * update_f[j]
        fnew_ref[j] = new
        fcopy_ref[j] = new.astype(BF)
    rows = rows_ref[...].T
    arows_ref[...] = rows[0:4]
    frows_ref[...] = rows[4:6]
    acols_ref[...] = acols_in[...]
    fcols_ref[...] = fcols_in[...]
    chunk = grad_ref.shape[0]
    at = own_place(chunk)
    grad_ref[...] = from_frame(own_ref[0], at, chunk).reshape(chunk)
    new = from_frame(own_ref[1], at, chunk)
    new_ref[...] = new.reshape(chunk)
    copy_ref[...] = new.astype(BF).reshape(chunk)
    sq_ref[...] = from_frame(own_ref[2], at, chunk).reshape(chunk)


def result_part(made, attn, ffn, chunk):
    out, _, agrad, fgrad, _, _, _, rows, acols, fcols, _ = made
    r = rows.shape[0]

    def shape(dims, kind):
        return jax.ShapeDtypeStruct(dims, kind)

    shapes = (
        shape(out.shape, BF),
        shape(out.shape, BF),
        shape(attn.shape, F32),
        shape(ffn.shape, F32),
        shape((chunk,), F32),
        shape(attn.shape, F32),
        shape(ffn.shape, F32),
        shape((chunk,), F32),
        shape(attn.shape, BF),
        shape(ffn.shape, BF),
        shape((chunk,), BF),
        shape((4, r), F32),
        shape(acols.shape, F32),
        shape((2, r), F32),
        shape(fcols.shape, F32),
        shape((chunk,), F32),
    )
    return pl.pallas_call(
        result_kernel,
        out_shape=shapes,
        in_specs=[VMEM_SPEC] * 13,
        out_specs=(VMEM_SPEC,) * 16,
        compiler_params=pltpu.CompilerParams(vmem_limit_bytes=60 * 2**20),
    )(*made, attn, ffn)


def shards(
    tokens, lengths, groups, cotangent, attn_weights, ffn_weights, small_params,
    attn_rows, attn_cols, ffn_rows, ffn_cols, small_sq,
):
    micro, rb, toks, _ = tokens.shape
    rows = micro * rb
    chunk = small_params.shape[0]
    made = layer_part(
        groups.reshape(rows),
        lengths.reshape(rows, SEGS),
        tokens.reshape(rows * toks, D),
        cotangent.reshape(rows * toks, D),
        attn_weights,
        ffn_weights,
        small_params,
        attn_rows,
        attn_cols,
        ffn_rows,
        ffn_cols,
        small_sq,
    )
    results = list(result_part(made, attn_weights, ffn_weights, chunk))
    for i in (0, 1):
        results[i] = results[i].reshape(tokens.shape)
    return tuple(results)


def solution(mesh):
    acts = P(None, "batch", "seq", None)
    weights = P(None, "seq", "batch")
    small = P(("seq", "batch"))
    rows, cols = P(None, "seq"), P(None, "batch")
    return jax.shard_map(
        shards,
        mesh=mesh,
        in_specs=(acts, P(None, "batch", None), P(None, "batch"), acts, weights, weights, small)
        + (rows, cols, rows, cols, small),
        out_specs=(acts, acts, weights, weights, small, weights, weights, small, weights, weights, small)
        + (rows, cols, rows, cols, small),
        check_vma=False,
    )
```

```python
import functools

import jax
import jax.numpy as jnp
from jax import lax
from jax.experimental import pallas as pl
from jax.experimental.pallas import tpu as pltpu
from jax.sharding import PartitionSpec as P

D = 512
H = 8
HD = 64
FF = 2048
GROUPS = 8
SEGS = 64
STEP = 10
NVEC = 10240
LANES = 128

NEG = -1e30
EPS = 1e-05
EPS_ONE = 1e-30
LEARN = 1.0
DECAY = 1.0 - STEP ** (-0.8)
SCALE = HD ** (-0.5)
LOG2E = 1.4426950408889634
FRAMES = 16
FRAME_ROWS = NVEC // FRAMES // LANES
GROUP = 4
BF = jnp.bfloat16
F32 = jnp.float32
VMEM_SPEC = pl.BlockSpec(memory_space=pltpu.VMEM)
SMEM_SPEC = pl.BlockSpec(memory_space=pltpu.SMEM)

ROW_BQ, ROW_BV, ROW_BO, ROW_B1, ROW_B2 = 0, 4, 8, 12, 28
ROW_G1, ROW_S1, ROW_G2, ROW_S2, ROW_E = 32, 36, 40, 44, 48


def mm(a, b):
    return lax.dot_general(a, b, (((1,), (0,)), ((), ())), preferred_element_type=F32)


def mm_nt(a, b):
    return lax.dot_general(a, b, (((1,), (1,)), ((), ())), preferred_element_type=F32)


def mm_tn(a, b):
    return lax.dot_general(a, b, (((0,), (0,)), ((), ())), preferred_element_type=F32)


def small_piece(small_ref, row, count):
    parts = [small_ref[r // FRAME_ROWS, pl.ds(r % FRAME_ROWS, 1), :] for r in range(row, row + count)]
    return jnp.concatenate(parts, axis=1)


def add_small(ref, row, values):
    for k in range(values.shape[1] // LANES):
        r = row + k
        ref[r // FRAME_ROWS, pl.ds(r % FRAME_ROWS, 1), :] += values[:, k * LANES : (k + 1) * LANES]


def low_half():
    return lax.broadcasted_iota(jnp.int32, (1, LANES), 1) < HD


def swap_halves(x):
    return pltpu.roll(x, HD, 1)


def heads_to_rows(tiles):
    low = low_half()
    first, second = [], []
    for j in range(H // 2):
        a, b = tiles[2 * j], tiles[2 * j + 1]
        first.append(jnp.where(low, a, swap_halves(b)))
        second.append(jnp.where(low, swap_halves(a), b))
    return jnp.concatenate(first, axis=1), jnp.concatenate(second, axis=1)


def rows_to_heads(first, second):
    low = low_half()
    tiles = []
    for j in range(H // 2):
        a = first[:, j * LANES : (j + 1) * LANES]
        b = second[:, j * LANES : (j + 1) * LANES]
        tiles.append(jnp.where(low, a, swap_halves(b)))
        tiles.append(jnp.where(low, swap_halves(a), b))
    return tiles


def wrap(value, count):
    return value - jnp.where(value >= count, count, 0)


def outwards(count):
    return sorted(range(1, count), key=lambda k: (abs(2 * k - count), k))


class Place:
    def __init__(self):
        self.n_s, self.n_b = lax.axis_size("seq"), lax.axis_size("batch")
        self.s, self.b = lax.axis_index("seq"), lax.axis_index("batch")
        self.n_z, self.parts = self.n_s // 4, self.n_s // H
        self.z, self.xc = self.s // 4, self.s % 4
        self.x, self.c = self.xc // 2, self.xc % 2
        self.other_x = (1 - self.x) * 2 + self.c
        self.other_c = self.x * 2 + 1 - self.c
        self.h, self.g = self.s // self.parts, self.s % self.parts
        self.z_ahead = [wrap(self.z + k, self.n_z) for k in range(self.n_z)]
        self.b_ahead = [wrap(self.b + k, self.n_b) for k in range(self.n_b)]
        self.xc_ahead = [wrap(self.xc + k, 4) for k in range(4)]
        self.h_ahead = [wrap(self.h + k, H) for k in range(H)]
        self.g_ahead = [wrap(self.g + k, self.parts) for k in range(self.parts)]
        self.z_pair = self.z + 1 - self.z % 2 * 2
        self.z_pair_ahead = [wrap(self.z_pair + k, self.n_z) for k in range(self.n_z)]
        self.at_z = [z * 4 + self.xc for z in self.z_ahead]
        self.at_x, self.at_core = self.z * 4 + self.other_x, self.z * 4 + self.other_c
        self.at_head = [h * self.parts + self.g for h in self.h_ahead]
        self.at_part = [self.h * self.parts + g for g in self.g_ahead]

    def along_z(self, k):
        return (self.at_z[k], self.b)

    def across_z(self):
        return (self.z_pair * 4 + self.xc, self.b)

    def across_x(self):
        return (self.at_x, self.b)

    def across_core(self):
        return (self.at_core, self.b)

    def batch_ahead(self, k):
        return self.b_ahead[k]

    def batch_behind(self, k):
        return self.b_ahead[(self.n_b - k) % self.n_b]

    def across_batch(self, k):
        return (self.s, self.b_ahead[k])

    def head_ahead(self, k):
        return self.h_ahead[k % H] if isinstance(k, int) else wrap(self.h + k, H)

    def head_behind(self, k):
        return self.h_ahead[(H - k) % H] if isinstance(k, int) else wrap(self.h + H - k, H)

    def across_heads(self, k):
        return (self.at_head[k] if isinstance(k, int) else self.head_ahead(k) * self.parts + self.g, self.b)

    def part_ahead(self, k):
        return self.g_ahead[k]

    def across_parts(self, k):
        return (self.at_part[k], self.b)


def greet(peers):
    barrier = pltpu.get_barrier_semaphore()
    for peer in peers:
        pl.semaphore_signal(barrier, inc=1, device_id=peer, device_id_type=pl.DeviceIdType.MESH)
    pl.semaphore_wait(barrier, len(peers))


def greet_all(place):
    barrier = pltpu.get_barrier_semaphore()

    def hello(b, i, carry):
        peer = (wrap(place.s + i, place.n_s), b)
        pl.semaphore_signal(barrier, inc=1, device_id=peer, device_id_type=pl.DeviceIdType.MESH)
        return carry

    for k, b in enumerate(place.b_ahead):
        lax.fori_loop(0 if k else 1, place.n_s, functools.partial(hello, b), 0)
    return lambda: pl.semaphore_wait(barrier, place.n_s * place.n_b - 1)


def far_first(i):
    if isinstance(i, int) and i in (0, H):
        return i
    return H // 2 + i // 2 * (1 - i % 2 * 2)


class Copy:
    def __init__(self, wire, i, build):
        self.wire, self.i, self.build = wire, i, build

    def made(self):
        return self.wire.make(self.i, *self.build())

    def start(self):
        self.made().start()

    def wait_recv(self):
        self.made().wait_recv()

    def wait_send(self):
        self.made().wait_send()


class Wire:
    def __init__(self, send_sems, recv_sems):
        self.send_sems, self.recv_sems, self.copies, self.used = send_sems, recv_sems, [], 0

    def reserve(self, count):
        self.used += count
        return self.used - count

    def make(self, i, src, dst, peer):
        return pltpu.make_async_remote_copy(
            src_ref=src,
            dst_ref=dst,
            send_sem=self.send_sems.at[i],
            recv_sem=self.recv_sems.at[i],
            device_id=peer,
            device_id_type=pl.DeviceIdType.MESH,
        )

    def plan(self, build):
        return Copy(self, self.reserve(1), build)

    def send(self, build):
        copy = self.plan(build)
        copy.start()
        self.copies.append(copy)
        return copy

    def drain(self):
        for copy in self.copies:
            copy.wait_send()
        self.copies = []


def received(copies):
    for copy in copies:
        copy.wait_recv()


class Gather:
    def __init__(self, place, wire, src, dst, own_sem, cut):
        self.place, self.wire, self.src, self.dst, self.cut, self.own_sem = place, wire, src, dst, cut, own_sem
        self.own().start()
        self.begin()

    def begin(self):
        p = self.place
        self.along = [self.wire.send(lambda k=k: (self.src, self.slot(p.z), p.along_z(k))) for k in range(1, p.n_z)]

    def slot(self, z):
        return self.dst.at[self.place.b, :, z, self.place.xc]

    def own(self):
        return pltpu.make_async_copy(self.src, self.slot(self.place.z), self.own_sem)

    def forward(self, part, *peers):
        return [self.wire.send(lambda peer=peer: (part(), part(), peer())) for peer in peers]

    def column(self, b, xc):
        return lambda: self.dst.at[b(), :, :, xc]

    def half(self, b, xc, second):
        span = pl.ds(self.cut, self.place.n_z - self.cut) if second else pl.ds(0, self.cut)
        return lambda: self.dst.at[b(), :, span, xc]

    def batch_peers(self):
        return [lambda k=k: self.place.across_batch(k) for k in range(1, self.place.n_b)]

    def to_plane(self):
        p = self.place
        self.own().wait()
        received(self.along)
        peers = [p.across_x, p.across_core] + self.batch_peers()
        self.plane = self.forward(self.column(lambda: p.b, p.xc), *peers)

    def to_diagonal(self):
        p = self.place
        self.plane[0].wait_recv()
        self.diagonal = self.forward(self.half(lambda: p.b, p.other_x, 0), *self.batch_peers())
        self.cores = [self.plane[1]] + self.forward(self.column(lambda: p.b, p.other_x), p.across_core)
        for k in range(1, p.n_b):
            b = lambda k=k: p.batch_behind(k)
            self.plane[1 + k].wait_recv()
            self.diagonal += self.forward(self.half(b, p.xc, 1), p.across_x)
            self.cores += self.forward(self.column(b, p.xc), p.across_core)

    def to_cores(self):
        p = self.place
        for k in range(1, p.n_b):
            for second in range(2):
                self.diagonal[(p.n_b - 1) * second + k - 1].wait_recv()
                part = self.half(lambda k=k: p.batch_behind(k), p.other_x, second)
                self.cores += self.forward(part, p.across_core)

    def finish(self):
        received(self.cores)


class PairGather(Gather):

    def begin(self):
        p, self.far = self.place, range(2, self.place.n_z, 2)
        self.along = [self.wire.send(lambda: (self.src, self.slot(p.z), p.across_z()))]
        self.arriving = [self.wire.send(lambda k=k: (self.src, self.slot(p.z), p.along_z(k))) for k in self.far]

    def to_pair(self):
        p = self.place
        for copy, k in zip(self.arriving, self.far):
            copy.wait_recv()
            z = p.z_ahead[p.n_z - k]
            self.along.append(self.wire.send(lambda z=z: (self.slot(z), self.slot(z), p.across_z())))


class ShortGather(Gather):
    def to_plane(self):
        p = self.place
        self.own().wait()
        received(self.along)
        diagonal = [
            lambda k=k: (p.z * 4 + p.other_x, p.batch_ahead(k)) for k in range(1, p.n_b)
        ]
        peers = [p.across_core, p.across_x] + self.batch_peers() + diagonal
        self.plane = self.forward(self.column(lambda: p.b, p.xc), *peers)

    def to_cores(self):
        p = self.place
        behind = [lambda k=k: p.batch_behind(k) for k in range(1, p.n_b)]
        columns = [(lambda: p.b, p.other_x)] + [(b, p.xc) for b in behind] + [(b, p.other_x) for b in behind]
        self.cores = [self.plane[0]]
        for copy, (b, xc) in zip(self.plane[1:], columns):
            copy.wait_recv()
            self.cores += self.forward(self.column(b, xc), p.across_core)


def normed_of(values):
    center = values - jnp.mean(values, axis=-1, keepdims=True)
    inverse = lax.rsqrt(jnp.mean(center * center, axis=-1, keepdims=True) + EPS)
    return center * inverse, inverse


def norm_back(grad_norm, normed, inverse):
    return inverse * (
        grad_norm
        - jnp.mean(grad_norm, axis=-1, keepdims=True)
        - normed * jnp.mean(grad_norm * normed, axis=-1, keepdims=True)
    )


def gelu_pair(z):
    c = 0.7978845608028654
    z2 = z * z
    t = jnp.tanh(c * z * (1.0 + 0.044715 * z2))
    half = 0.5 * (1.0 + t)
    slope = half + 0.5 * z * (1.0 - t * t) * (c * (1.0 + 3 * 0.044715 * z2))
    return z * half, slope


def language_rows(groups_ref, small_ref, rows):
    table = [small_piece(small_ref, ROW_E + 4 * e, 4) for e in range(GROUPS)]
    out = []
    for m in range(rows):
        acc = jnp.zeros_like(table[0])
        for e in range(GROUPS):
            acc = acc + jnp.where(groups_ref[m] == e, table[e], 0.0)
        out.append(acc)
    return out


def column_sum(x):
    return jnp.sum(x, axis=0, keepdims=True)


class Scatter:
    def __init__(self, place, wire, part, core, acc, far, near, plane_x, plane_b, column):
        self.begin(place, wire, part, core, acc, column)
        self.far, self.near, self.plane_x, self.plane_b = far, near, plane_x, plane_b
        self.cut = far.shape[2]

    def begin(self, place, wire, part, core, acc, column):
        self.place, self.wire = place, wire
        self.part, self.core, self.acc, self.column = part, core, acc, column
        self.kind = part.dtype
        self.x, self.c = place.x, place.c
        self.slabs = part.shape[1]

    def add(self, target, *others):
        total = target[...].astype(F32)
        for other in others:
            total = total + other[...].astype(F32)
        target[...] = total.astype(self.kind)

    def each(self, body, first=0, last=None):
        for j in range(self.slabs):

            def step(z, carry, j=j):
                body(j, z)
                return carry

            lax.fori_loop(first, self.place.n_z if last is None else last, step, 0)

    def to_core(self):
        p = self.place
        self.moved = [self.wire.send(lambda: (self.part.at[:, :, :, :, 1 - self.c], self.core, p.across_core()))]

    def join(self):
        p = self.place
        received(self.moved)
        for j in range(self.slabs):

            def body(b, carry, j=j):
                def at_z(z, carry):
                    for x in range(2):
                        total = self.part[b, j, z, x, self.c].astype(F32) + self.core[b, j, z, x].astype(F32)
                        self.acc[b, j, z, x] = total.astype(self.kind)
                    return carry

                return lax.fori_loop(0, p.n_z, at_z, carry)

            lax.fori_loop(0, p.n_b, body, 0)

    def to_diagonal(self):
        p = self.place
        self.join()
        cut, rest = pl.ds(0, self.cut), pl.ds(self.cut, p.n_z - self.cut)
        self.moved_far, self.moved_near = [], []
        for k in range(1, p.n_b):
            diagonal = lambda k=k: self.acc.at[p.batch_ahead(k), :, :, 1 - self.x]
            self.moved_far.append(
                self.wire.send(
                    lambda k=k, part=diagonal: (part().at[:, cut], self.far.at[k - 1], p.across_batch(k))
                )
            )
            self.moved_near.append(
                self.wire.send(lambda k=k, part=diagonal: (part().at[:, rest], self.near.at[k - 1], p.across_x()))
            )

    def to_plane(self):
        p = self.place
        for k in range(1, p.n_b):
            self.moved_near[k - 1].wait_recv()
            self.each(
                lambda j, z, k=k: self.add(
                    self.acc.at[p.batch_ahead(k), j, z, self.x], self.near.at[k - 1, j, z - self.cut]
                ),
                self.cut,
            )
        received(self.moved_far)
        self.each(
            lambda j, z: self.add(
                self.acc.at[p.b, j, z, 1 - self.x], *[self.far.at[k - 1, j, z] for k in range(1, p.n_b)]
            ),
            0,
            self.cut,
        )
        self.moved = [self.wire.send(lambda: (self.acc.at[p.b, :, :, 1 - self.x], self.plane_x, p.across_x()))]
        self.moved += [
            self.wire.send(
                lambda k=k: (
                    self.acc.at[p.batch_ahead(k), :, :, self.x],
                    self.plane_b.at[k - 1],
                    p.across_batch(k),
                )
            )
            for k in range(1, p.n_b)
        ]

    def others(self, j, z):
        return [self.plane_x.at[j, z]] + [self.plane_b.at[k - 1, j, z] for k in range(1, self.place.n_b)]

    def to_owner(self):
        p = self.place
        received(self.moved)
        self.each(lambda j, z: self.add(self.acc.at[p.b, j, z, self.x], *self.others(j, z)))
        self.moved = [
            self.wire.send(
                lambda k=k: (
                    self.acc.at[p.b, :, p.z_ahead[k], self.x],
                    self.column.at[k - 1],
                    p.along_z(k),
                )
            )
            for k in range(1, p.n_z)
        ]

    def total(self, j):
        p = self.place
        out = self.acc[p.b, j, p.z, self.x].astype(F32)
        for k in range(1, p.n_z):
            out = out + self.column[k - 1, j].astype(F32)
        return out

    def finish(self):
        received(self.moved)


class PairScatter(Scatter):

    def to_owner(self):
        p = self.place
        received(self.moved)
        self.each(lambda j, z: self.add(self.acc.at[p.b, j, z, self.x], *self.others(j, z)))
        self.moved = [
            self.wire.send(
                lambda i=i: (
                    self.acc.at[p.b, :, p.z_pair_ahead[2 * i], self.x],
                    self.column.at[i],
                    p.across_z(),
                )
            )
            for i in range(p.n_z // 2)
        ]

    def to_far(self):
        p = self.place
        half = p.n_z // 2
        received(self.moved)
        for i in range(half):
            for j in range(self.slabs):
                self.add(self.acc.at[p.b, j, p.z_ahead[2 * i], self.x], self.column.at[i, j])
        self.moved = [
            self.wire.send(
                lambda i=i: (
                    self.acc.at[p.b, :, p.z_ahead[2 * i], self.x],
                    self.column.at[half + i - 1],
                    p.along_z(2 * i),
                )
            )
            for i in range(1, half)
        ]

    def total(self, j):
        p = self.place
        out = self.acc[p.b, j, p.z, self.x].astype(F32)
        for k in range(p.n_z // 2, p.n_z - 1):
            out = out + self.column[k, j].astype(F32)
        return out


class ShortScatter(Scatter):
    def __init__(self, place, wire, part, core, acc, plane, column):
        self.begin(place, wire, part, core, acc, column)
        self.plane = plane

    def to_plane(self):
        p = self.place
        self.join()
        self.moved = []
        for k in range(p.n_b):
            for dx in range(2):
                if k or dx:

                    def build(k=k, dx=dx, slot=len(self.moved)):
                        x = self.x if dx == 0 else 1 - self.x
                        to = p.z * 4 + (p.other_x if dx else p.xc)
                        b = p.batch_ahead(k)
                        return (self.acc.at[b, :, :, x], self.plane.at[slot], (to, b))

                    self.moved.append(self.wire.send(build))

    def others(self, j, z):
        return [self.plane.at[k, j, z] for k in range(2 * self.place.n_b - 1)]


def short_scratch(n_b, slabs, n_z, r, cols, kind):
    return [
        pltpu.VMEM((n_b, slabs, n_z, 2, r, cols), kind),
        pltpu.VMEM((n_b, slabs, n_z, 2, r, cols), kind),
        pltpu.VMEM((2 * n_b - 1, slabs, n_z, r, cols), kind),
        pltpu.VMEM((n_z - 1, slabs, r, cols), kind),
    ]


def scatter_scratch(n_b, slabs, n_z, r, cols, kind):
    return [
        pltpu.VMEM((n_b, slabs, n_z, 2, r, cols), kind),
        pltpu.VMEM((n_b, slabs, n_z, 2, r, cols), kind),
        pltpu.VMEM((n_b - 1, slabs, n_z - n_z // 4, r, cols), kind),
        pltpu.VMEM((n_b - 1, slabs, n_z // 4, r, cols), kind),
        pltpu.VMEM((slabs, n_z, r, cols), kind),
        pltpu.VMEM((n_b - 1, slabs, n_z, r, cols), kind),
        pltpu.VMEM((n_z - 1, slabs, r, cols), kind),
    ]


SCATTER_SCRATCH, SHORT_SCRATCH = 7, 4
SLABS = 6


def lanes_of(values):
    lane = lax.broadcasted_iota(jnp.int32, (8, LANES), 1)
    row = lax.broadcasted_iota(jnp.int32, (8, LANES), 0)
    tile = jnp.zeros((8, LANES), F32)
    for j, value in enumerate(values):
        if value is not None:
            tile = tile + jnp.where((lane == j) & (row == 0), value, 0.0)
    return tile


def sum_all(x):
    return jnp.sum(jnp.sum(x, axis=1, keepdims=True), axis=0, keepdims=True)


def to_frame(values, at):
    wide = jnp.concatenate([values, jnp.zeros((1, 8 * LANES - values.shape[1]), F32)], axis=1)
    wide = pltpu.roll(wide, at, 1)
    return jnp.concatenate([wide[:, k * LANES : (k + 1) * LANES] for k in range(8)], axis=0)


def from_frame(tile, at, chunk):
    wide = jnp.concatenate([tile[k : k + 1] for k in range(8)], axis=1)
    return pltpu.roll(wide, 8 * LANES - at, 1)[:, :chunk]


def own_place(chunk):
    index = lax.axis_index("seq") * lax.axis_size("batch") + lax.axis_index("batch")
    return lax.rem(index * chunk, FRAME_ROWS * LANES)


def segment_ids(lengths, idk_ref, idq_ref, place, tokens):
    rows, length = idk_ref.shape[0], idk_ref.shape[1]
    upto = lax.broadcasted_iota(jnp.int32, (SEGS, LANES), 0) <= lax.broadcasted_iota(jnp.int32, (SEGS, LANES), 1)
    upto = jnp.where(upto, 1.0, 0.0).astype(BF)
    values = lengths.astype(F32)
    high = jnp.floor(values * (1.0 / 64))
    low = (values - 64.0 * high).astype(BF)
    high = high.astype(BF)
    ends = mm(high, upto) * 64.0 + mm(low, upto)
    ends = jnp.where(lax.broadcasted_iota(jnp.int32, (rows, LANES), 1) < SEGS, ends, 1e9)
    upto = upto[:, :SEGS]
    ends_down = lax.dot_general(upto, high, (((0,), (1,)), ((), ())), preferred_element_type=F32) * 64.0
    ends_down = ends_down + lax.dot_general(upto, low, (((0,), (1,)), ((), ())), preferred_element_type=F32)
    ones = jnp.ones((LANES, LANES), BF)
    span = 256
    for m in range(rows):

        def fill(i, carry, m=m):
            at = pl.multiple_of(i * span, span)
            places = (at + lax.broadcasted_iota(jnp.int32, (span, LANES), 0)).astype(F32)
            passed = jnp.where(ends[m : m + 1] <= places, 1.0, 0.0).astype(BF)
            seg = mm(passed, ones)
            idk_ref[m, pl.ds(at, span), :] = jnp.where(seg < SEGS, seg, SEGS + places)
            return carry

        lax.fori_loop(0, length // span, fill, 0)
        for h in range(H):
            first = ((h * place.parts + place.g) * tokens + lax.broadcasted_iota(jnp.int32, (1, tokens), 1)).astype(F32)
            seg = column_sum(jnp.where(ends_down[:, m : m + 1] <= first, 1.0, 0.0))
            group, k = h // GROUP, h % GROUP
            idq_ref[m, group, :, k * tokens : (k + 1) * tokens] = jnp.where(seg < SEGS, seg, SEGS + first)


def layer_kernel(
    groups_ref, lengths_ref, tok_ref, cot_ref, attn_ref, ffn_ref, params_ref, arows_ref, acols_ref, frows_ref,
    fcols_ref, sq_ref,
    out_hbm, du_hbm, agrad_hbm, fgrad_hbm, update_a_hbm, update_f_hbm, scales_ref, rows_new_ref, acols_new_ref,
    fcols_new_ref, own_new_ref,
    *scratch,
):
    place = Place()
    scratch = list(scratch)
    own_sems, recv_sems, send_sems = scratch.pop(), scratch.pop(), scratch.pop()
    wire = Wire(send_sems, recv_sems)

    def take(count):
        taken = scratch[:count]
        del scratch[:count]
        return taken

    pack_low, kv_low, wo_low, ffn_low, own_ref, small_ref, pack_ref, wkv_ref, wo_ref, w1_ref, w2_ref = take(11)
    idk_ref, idq_ref, q_ref, kv_ref, qsend_ref, kvsend_ref, qm_ref, dom_ref = take(8)
    peak_ref, acc_ref, ot_ref, lse_ref, delta_ref, o_ref, otile_ref, dotile_ref, do_ref = take(9)
    act_ref, slope_ref, dz_ref, sum_ref, frames_ref = take(5)
    dqt_ref, part_ref, near_ref, dkv_sum, dq_ref, dq_back, dkv_back = take(7)
    dwo_ref, dw1_ref, dw2_ref, dkv_w_ref, dq_w_ref, dsmall_ref = take(6)
    cols_plane, rows_plane, all_z, late_cols, late_rows, late_sums, all_sums = take(7)
    out_ref, du_ref, agrad_ref, fgrad_ref, update_a, update_f = take(6)
    written = [
        pltpu.make_async_copy(src, dst, own_sems.at[5 + i])
        for i, (src, dst) in enumerate(
            (
                (out_ref, out_hbm),
                (du_ref, du_hbm),
                (agrad_ref, agrad_hbm),
                (fgrad_ref, fgrad_hbm),
                (update_a, update_a_hbm),
                (update_f, update_f_hbm),
            )
        )
    ]
    n_z, n_b, parts = place.n_z, place.n_b, place.parts
    rows = 2
    count = tok_ref.shape[0]
    tokens = count // rows
    r, cols = attn_ref.shape[1:]
    cols_f = ffn_ref.shape[2]
    groups = H // GROUP
    width = GROUP * tokens
    keys = parts * tokens
    scale2 = SCALE * LOG2E
    low = low_half()

    plane = [(dx, db) for db in range(n_b) for dx in range(4) if dx or db]

    def plane_peer(dx, db):
        return (place.z * 4 + place.xc_ahead[dx], place.batch_ahead(db))

    along = [place.along_z(k) for k in range(1, n_z)]
    all_here = greet_all(place)

    chunk = params_ref.shape[0]
    own_at = own_place(chunk)
    own = to_frame(params_ref[...].reshape(1, chunk), own_at)
    own_ref[...] = own
    pack_low[0, :r] = attn_ref[0].astype(BF)
    tile = jnp.concatenate([own, jnp.zeros((8, LANES), F32)], axis=0)
    if cols < LANES:
        tile = jnp.concatenate([own[:, :cols], own[:, cols:]], axis=0)
    if cols > LANES:
        tile = jnp.concatenate([tile, jnp.zeros((16, cols - LANES), F32)], axis=1)
    pack_low[0, r:] = tile.astype(BF)
    kv_low[...] = attn_ref[1:3].astype(BF)
    all_here()
    pack = ShortGather(place, wire, pack_low, pack_ref, own_sems.at[0], n_z)
    kv_w = ShortGather(place, wire, kv_low, wkv_ref, own_sems.at[4], n_z)
    wo_low[0] = attn_ref[3].astype(BF)
    ffn_low[...] = ffn_ref[...].astype(BF)
    segment_ids(lengths_ref[...], idk_ref, idq_ref, place, tokens)
    for i in range(rows * groups):
        peak_ref[i] = jnp.full((1, width), NEG, F32)
        acc_ref[i] = jnp.zeros((HD + 16, width), F32)
    frames_ref[...] = jnp.zeros_like(frames_ref)
    dqt_ref[...] = jnp.zeros_like(dqt_ref)
    pack.to_plane()
    kv_w.to_plane()
    most = n_z - n_z // 4
    first = PairGather(place, wire, ffn_low.at[pl.ds(0, 1)], w1_ref, own_sems.at[1], most)
    out_w = PairGather(place, wire, wo_low, wo_ref, own_sems.at[2], most)
    second = PairGather(place, wire, ffn_low.at[pl.ds(1, 1)], w2_ref, own_sems.at[3], most)
    pack.to_cores()
    pack.finish()
    frame = place.n_s * n_b // FRAMES
    for f in range(FRAMES):
        total = None
        for i in range(f * frame, (f + 1) * frame):
            s, b = i // n_b, i % n_b
            tile = pack_ref[b, 0, s // 4, s % 4, r:].astype(F32)
            if cols < LANES:
                tile = jnp.concatenate([tile[:8], tile[8:]], axis=1)
            tile = tile[:8, :LANES]
            total = tile if total is None else total + tile
        small_ref[f] = total
    lang = language_rows(groups_ref, small_ref, rows)
    first.to_pair()
    out_w.to_pair()

    def inputs():
        return jnp.concatenate(
            [tok_ref[m * tokens : (m + 1) * tokens].astype(F32) + lang[m] for m in range(rows)], axis=0
        )

    def w_qkv(b, j):
        w = wkv_ref[b, j - 1] if j else pack_ref[b, 0, :, :, :r]
        return w.reshape(D, cols)

    a = inputs().astype(BF)

    def project(j, bias):
        out = jnp.concatenate([mm(a, w_qkv(b, j)) for b in range(n_b)], axis=1)
        if bias is not None:
            out = out + small_piece(small_ref, bias, 4)
        return [t.astype(BF) for t in rows_to_heads(out[:tokens], out[tokens:])]

    for h, t in enumerate(project(0, ROW_BQ)):
        qsend_ref[h] = t
    q_ref[place.h] = qsend_ref[place.h]
    def to_heads(src, dst):
        return [
            wire.send(lambda k=k: (src.at[place.head_ahead(k)], dst.at[place.h], place.across_heads(k)))
            for k in outwards(H)
        ]

    moved_q = to_heads(qsend_ref, q_ref)
    second.to_pair()
    kv_w.to_cores()
    first.to_plane()
    out_w.to_plane()
    kv_w.finish()
    for j, bias in ((0, None), (1, ROW_BV)):
        for h, t in enumerate(project(1 + j, bias)):
            kvsend_ref[h, j] = t
    kv_ref[place.s] = kvsend_ref[place.h]
    kv_sems = wire.reserve(H)
    share_sems = wire.reserve(H * (parts - 1))

    def moved_kv(i):
        k = far_first(i)
        return wire.make(
            kv_sems + i, kvsend_ref.at[place.head_ahead(k)], kv_ref.at[place.s], place.across_heads(k)
        )

    def ordered(i):
        return far_first(i) if isinstance(i, int) else jnp.where(i == 0, 0, far_first(i))

    def shared_kv(i, j):
        slot = kv_ref.at[place.head_behind(ordered(i)) * parts + place.g]
        return wire.make(share_sems + i * (parts - 1) + j - 1, slot, slot, place.across_parts(j))

    for j in range(1, parts):
        shared_kv(0, j).start()
    for k in range(1, H):
        moved_kv(k).start()
    second.to_plane()

    def masked_rows(src_ref, dst_ref):
        for g in range(groups):
            both = src_ref[g * GROUP : (g + 1) * GROUP].reshape(width, LANES)
            zero = jnp.zeros_like(both)
            dst_ref[0, g] = jnp.where(low, both, zero)
            dst_ref[1, g] = jnp.where(low, zero, both)

    received(moved_q)
    masked_rows(q_ref, qm_ref)

    def pair(h):
        kv = kv_ref[pl.ds(h * parts, parts)]
        return kv[:, 0].reshape(keys, LANES), kv[:, 1].reshape(keys, LANES)

    def key_ids(h, m):
        ids = idk_ref[m, pl.ds(pl.multiple_of(h * keys, keys), keys), :]
        return jnp.concatenate([ids] * (width // LANES), axis=1)

    def attend(k):
        h = place.head_behind(ordered(k))
        ids = [key_ids(h, m) for m in range(rows)]
        for j in range(1, parts):
            shared_kv(k, j).wait_recv()
        key, value = pair(h)
        value_t = value.T
        ones = jnp.ones((16, keys), BF)
        for g in range(groups):
            for m in range(rows):
                i = g * rows + m
                s = jnp.where(ids[m] == idq_ref[m, g], mm_nt(key, qm_ref[m, g]) * scale2, NEG)
                new = jnp.maximum(peak_ref[i], jnp.max(s, axis=0, keepdims=True))
                p = jnp.exp2(s - new).astype(BF)
                alpha = jnp.exp2(peak_ref[i] - new)
                left = jnp.concatenate([value_t[m * HD : (m + 1) * HD], ones], axis=0)
                acc_ref[i] = acc_ref[i] * alpha + mm(left, p)
                peak_ref[i] = new

    def meanwhile(k, *stages):
        for at, stage in stages:
            pl.when(k == at)(stage)

    def forward_step(k, carry):
        moved_kv(k).wait_recv()
        for j in range(1, parts):
            shared_kv(k, j).start()
        attend(k - 1)
        meanwhile(
            k,
            (2, first.to_diagonal),
            (2, out_w.to_diagonal),
            (H - 1, second.to_diagonal),
        )
        return carry

    lax.fori_loop(1, H, forward_step, 0)
    attend(H - 1)
    for g in range(groups):
        for m in range(rows):
            i = g * rows + m
            total = acc_ref[i, HD : HD + 1]
            ot_ref[g, m * HD : (m + 1) * HD] = acc_ref[i, :HD] * (1.0 / total)
            lse_ref[i] = peak_ref[i] + jnp.log2(total)
        o_ref[g * GROUP : (g + 1) * GROUP] = ot_ref[g].T.astype(BF).reshape(GROUP, tokens, LANES)
    moved = to_heads(o_ref, otile_ref)
    otile_ref[place.h] = o_ref[place.h]
    for piece in (out_w, first, second):
        piece.to_cores()

    tiles, wide = act_ref.shape[0], act_ref.shape[2]
    per_b = cols_f // wide
    bias_1 = [small_piece(small_ref, ROW_B1 + i * wide // LANES, wide // LANES) for i in range(tiles)]
    gain1, shift1 = small_piece(small_ref, ROW_G1, 4), small_piece(small_ref, ROW_S1, 4)
    gain2, shift2 = small_piece(small_ref, ROW_G2, 4), small_piece(small_ref, ROW_S2, 4)
    bias_o, bias_2 = small_piece(small_ref, ROW_BO, 4), small_piece(small_ref, ROW_B2, 4)

    def block(ref, i):
        at = i % per_b * wide
        return ref[i // per_b, 0, :, :, :, at : at + wide].reshape(D, wide)

    def joined(ref, b):
        return jnp.concatenate([ref[b * per_b + i] for i in range(per_b)], axis=1)

    live = jnp.concatenate(
        [idk_ref[m, pl.ds(pl.multiple_of(place.s * tokens, tokens), tokens), :] for m in range(rows)], axis=0
    )
    live = jnp.where(live < SEGS, 1.0, 0.0)
    u = inputs()
    out_w.finish()
    first.finish()
    received(moved)
    mixed = jnp.concatenate(heads_to_rows([otile_ref[h].astype(F32) for h in range(H)]), axis=0).astype(BF)
    attn_out = jnp.concatenate([mm(mixed, wo_ref[b, 0].reshape(D, cols)) for b in range(n_b)], axis=1)
    normed1, inverse1 = normed_of(u + (attn_out + bias_o))
    hidden = normed1 * gain1 + shift1
    hb = hidden.astype(BF)
    for i in range(tiles):
        act, slope = gelu_pair(mm(hb, block(w1_ref, i)) + bias_1[i])
        slope_ref[i] = slope
        act_ref[i] = act.astype(BF)
    second.finish()
    total = hidden + u + bias_2
    for b in range(n_b):
        total = total + mm_nt(joined(act_ref, b), w2_ref[b, 0].reshape(D, cols_f))

    normed2, inverse2 = normed_of(total)
    out_ref[...] = (normed2 * gain2 + shift2).astype(BF)
    c = cot_ref[...].astype(F32) * jnp.concatenate([live] * (D // LANES), axis=1)
    dr = norm_back(c * gain2, normed2, inverse2)
    df = dr.astype(BF)

    def scatter(part):
        return PairScatter(place, wire, part, *take(SCATTER_SCRATCH))

    g_first, g_second, g_out = scatter(dw1_ref), scatter(dw2_ref), scatter(dwo_ref)
    g_kv = ShortScatter(place, wire, dkv_w_ref, *take(SHORT_SCRATCH))
    g_q = ShortScatter(place, wire, dq_w_ref, *take(SHORT_SCRATCH))
    g_small = ShortScatter(place, wire, dsmall_ref, *take(SHORT_SCRATCH))

    def weight_grad(left, right_ref, dst_ref):
        left = left.T
        for i in range(tiles):
            at = i % per_b * wide
            grad = mm(left, right_ref[i]).astype(BF).reshape(n_z, 2, 2, r, wide)
            dst_ref[i // per_b, 0, :, :, :, :, at : at + wide] = grad

    weight_grad(df, act_ref, dw2_ref)
    g_second.to_core()
    dh = dr
    for i in range(tiles):
        dz = (mm(df, block(w2_ref, i)) * slope_ref[i]).astype(BF)
        dz_ref[i] = dz
    for b in range(n_b):
        dh = dh + mm_nt(joined(dz_ref, b), w1_ref[b, 0].reshape(D, cols_f))
    dpre = norm_back(dh * gain1, normed1, inverse1)
    dattn = dpre.astype(BF)
    do = mm_nt(dattn[:, :cols], wo_ref[0, 0].reshape(D, cols))
    for b in range(1, n_b):
        do = do + mm_nt(dattn[:, b * cols : (b + 1) * cols], wo_ref[b, 0].reshape(D, cols))
    for h, t in enumerate(rows_to_heads(do[:tokens], do[tokens:])):
        dotile_ref[h] = t.astype(BF)
    moved = to_heads(dotile_ref, do_ref)
    written[0].start()
    do_ref[place.h] = dotile_ref[place.h]
    sum_ref[...] = dpre + dr

    g_second.to_diagonal()
    weight_grad(hb, dz_ref, dw1_ref)
    g_first.to_core()
    mixed_t = mixed.T
    for b in range(n_b):
        dwo = mm(mixed_t, dattn[:, b * cols : (b + 1) * cols]).astype(BF)
        dwo_ref[b, 0] = dwo.reshape(n_z, 2, 2, r, cols)
    g_out.to_core()
    for k in range(H):
        for j in range(1, parts):
            shared_kv(k, j).wait_send()
        if k:
            moved_kv(k).wait_send()
    wire.drain()

    g_first.to_diagonal()
    g_out.to_diagonal()
    add_small(frames_ref, ROW_G2, column_sum(c * normed2))
    add_small(frames_ref, ROW_S2, column_sum(c))
    add_small(frames_ref, ROW_B2, column_sum(df.astype(F32)))
    for i in range(tiles):
        add_small(frames_ref, ROW_B1 + i * wide // LANES, column_sum(dz_ref[i].astype(F32)))
    add_small(frames_ref, ROW_G1, column_sum(dh * normed1))
    add_small(frames_ref, ROW_S1, column_sum(dh))
    add_small(frames_ref, ROW_BO, column_sum(dattn.astype(F32)))
    received(moved)
    masked_rows(do_ref, dom_ref)
    g_second.to_plane()
    for g in range(groups):
        product = do_ref[g * GROUP : (g + 1) * GROUP].reshape(width, LANES).astype(F32).T * ot_ref[g]
        for m in range(rows):
            delta_ref[g * rows + m] = column_sum(product[m * HD : (m + 1) * HD])

    near_sems = wire.reserve(H * (parts - 1))
    back_sems = wire.reserve(H)

    def target(k):
        far = far_first(k) if isinstance(k, int) else jnp.where(k == H, H, far_first(k))
        return place.head_ahead(far)

    def near_kv(k, j):
        h = target(k)
        return wire.make(
            near_sems + (k - 1) * (parts - 1) + j - 1,
            part_ref.at[h, place.part_ahead(j)],
            near_ref.at[j - 1, h],
            place.across_parts(j),
        )

    def back_kv(k):
        h = target(k)
        return wire.make(back_sems + k - 1, dkv_sum.at[h], dkv_back.at[place.h], (h * parts + place.g, place.b))

    def fold(k):
        h = target(k)
        total = part_ref[h, place.g].astype(F32)
        for j in range(1, parts):
            near_kv(k, j).wait_recv()
            total = total + near_ref[j - 1, h].astype(F32)
        return total.astype(BF)

    def key_step(k):
        h = target(k)
        key, value = pair(h)
        key_t = key.T
        ids = [key_ids(h, m) for m in range(rows)]
        dk = jnp.zeros((keys, LANES), F32)
        dv = jnp.zeros((keys, LANES), F32)
        for g in range(groups):
            for m in range(rows):
                i = g * rows + m
                p = jnp.exp2(mm_nt(key, qm_ref[m, g]) * scale2 - lse_ref[i])
                p = jnp.where(ids[m] == idq_ref[m, g], p, 0.0)
                ds = (p * (mm_nt(value, dom_ref[m, g]) - delta_ref[i])).astype(BF)
                dv = dv + mm(p.astype(BF), dom_ref[m, g])
                dk = dk + mm(ds, qm_ref[m, g])
                dqt_ref[g, m * HD : (m + 1) * HD] += mm(key_t[m * HD : (m + 1) * HD], ds)
        part_ref[h, :, 0] = (dk * SCALE).astype(BF).reshape(parts, tokens, LANES)
        part_ref[h, :, 1] = dv.astype(BF).reshape(parts, tokens, LANES)
        for j in range(1, parts):
            near_kv(k, j).start()

    def backward_step(k, carry):
        key_step(k)
        dkv_sum[target(k - 1)] = fold(k - 1)
        back_kv(k - 1).start()
        meanwhile(
            k,
            (6, g_first.to_plane),
            (6, g_out.to_plane),
        )
        return carry

    token_pieces = (g_second, g_first, g_out)
    key_step(1)
    lax.fori_loop(2, H + 1, backward_step, 0)
    for g in range(groups):
        dq_ref[g * GROUP : (g + 1) * GROUP] = (dqt_ref[g] * SCALE).T.astype(BF).reshape(GROUP, tokens, LANES)
    moved = to_heads(dq_ref, dq_back)
    dq_back[place.h] = dq_ref[place.h]
    dkv_back[place.h] = fold(H)
    g_second.to_owner()

    def to_rows(parts_of):
        return jnp.concatenate(heads_to_rows([t.astype(F32) for t in parts_of]), axis=0).astype(BF)

    def grad_of(left, right, b):
        return mm(left, right[:, b * cols : (b + 1) * cols]).astype(BF).reshape(n_z, 2, 2, r, cols)

    def back_through(total, right, j):
        for b in range(n_b):
            total = total + mm_nt(right[:, b * cols : (b + 1) * cols], w_qkv(b, j))
        return total

    for k in range(1, H):
        back_kv(k).wait_recv()
    a_t = inputs().astype(BF).T
    dk = to_rows([dkv_back[h, 0] for h in range(H)])
    dv = to_rows([dkv_back[h, 1] for h in range(H)])
    for b in range(n_b):
        dkv_w_ref[b, 0] = grad_of(a_t, dk, b)
        dkv_w_ref[b, 1] = grad_of(a_t, dv, b)
    g_kv.to_core()
    add_small(frames_ref, ROW_BV, column_sum(dv.astype(F32)))
    du = back_through(back_through(sum_ref[...], dk, 1), dv, 2)
    g_kv.to_plane()
    g_second.to_far()
    g_first.to_owner()
    g_out.to_owner()
    received(moved)
    dq = to_rows([dq_back[h] for h in range(H)])
    for b in range(n_b):
        dq_w_ref[b, 0] = grad_of(a_t, dq, b)
    g_q.to_core()
    du = back_through(du, dq, 0)
    add_small(frames_ref, ROW_BQ, column_sum(dq.astype(F32)))
    sums = [column_sum(du[m * tokens : (m + 1) * tokens]) for m in range(rows)]
    for e in range(GROUPS):
        total = jnp.zeros_like(sums[0])
        for m in range(rows):
            total = total + jnp.where(groups_ref[m] == e, sums[m], 0.0)
        add_small(frames_ref, ROW_E + 4 * e, total)
    for s in range(place.n_s):
        for b in range(n_b):
            dsmall_ref[b, 0, s // 4, s // 2 % 2, s % 2] = frames_ref[(s * n_b + b) // frame]
    g_small.to_core()
    g_q.to_plane()
    g_small.to_plane()
    g_first.to_far()
    g_out.to_far()
    du_ref[...] = du.astype(BF)
    written[1].start()
    g_kv.to_owner()

    weights = [attn_ref.at[j] for j in range(4)] + [ffn_ref.at[j] for j in range(2)]
    outs = [agrad_ref.at[j] for j in range(4)] + [fgrad_ref.at[j] for j in range(2)]
    updates = [update_a.at[j] for j in range(4)] + [update_f.at[j] for j in range(2)]
    old_cols = [acols_ref[j : j + 1] for j in range(4)] + [fcols_ref[j : j + 1] for j in range(2)]
    owners = [(g_q, 0), (g_kv, 0), (g_kv, 1), (g_out, 0), (g_first, 0), (g_second, 0)]
    spans = [cols] * 4 + [cols_f] * 2
    places, used = [], 0
    for span in spans:
        places.append(used)
        used += -(-span // LANES)
    pad = cols_plane.shape[1]
    late = 3
    mine = cols_plane.at[place.xc]
    mine_rows = rows_plane.at[place.b, place.xc]
    mine_late = late_cols.at[place.s]
    mine_late_rows = late_rows.at[place.b]
    mine_sums = late_sums.at[place.b, place.s]
    mine[...] = jnp.zeros((pad, LANES), F32)
    mine_late[...] = jnp.zeros((8, LANES), F32)
    lane = lax.broadcasted_iota(jnp.int32, (r, LANES), 1)
    square_sums = [None] * SLABS
    old_rows = jnp.concatenate([arows_ref[...], frows_ref[...], jnp.zeros((2, r), F32)], axis=0).T
    old_rows = [old_rows[:, j : j + 1] for j in range(SLABS)]
    row_sums_old = [sum_all(x) for x in old_rows]
    weight_squares = [sum_all(w[...] * w[...]) for w in weights]
    own = own_ref[...]
    entry = lax.broadcasted_iota(jnp.int32, (8, LANES), 0) * LANES + lax.broadcasted_iota(jnp.int32, (8, LANES), 1)
    own_mask = jnp.where((entry >= own_at) & (entry < own_at + chunk), 1.0, 0.0)
    weight_squares.append(sum_all(own * own))
    rows_tiles = []

    def gradient(j):
        owner, slab = owners[j]
        grad = owner.total(slab)
        outs[j][...] = grad
        square = grad * grad + EPS_ONE
        row_sum = jnp.sum(square, axis=1, keepdims=True)
        col_sum = column_sum(square)
        ref = mine_late if j < late else mine
        for k in range(0, spans[j], LANES):
            span = min(LANES, spans[j] - k)
            ref[pl.ds(places[j] + k // LANES, 1), pl.ds(0, span)] = col_sum[:, k : k + span]
        square_sums[j] = sum_all(row_sum)
        return jnp.where(lane == j, row_sum, 0.0)

    def renewed(j, row_total, sums, square_total, old_total):
        length = D if j < 4 else FF
        new_rows = DECAY * old_rows[j] + (1.0 - DECAY) * row_total[:, j : j + 1] * (1.0 / length)
        rows_tiles.append(jnp.where(lane == j, new_rows, 0.0))
        mean_rows = (DECAY / n_b * old_total + (1.0 - DECAY) * (1.0 / length) * square_total) * (1.0 / D)
        pieces = [
            sums[places[j] + k // LANES : places[j] + k // LANES + 1, : min(LANES, spans[j] - k)]
            for k in range(0, spans[j], LANES)
        ]
        col_sum = pieces[0] if len(pieces) == 1 else jnp.concatenate(pieces, axis=1)
        new = DECAY * old_cols[j] + (1.0 - DECAY) * (1.0 / D) * col_sum
        if j < 4:
            acols_new_ref[j : j + 1, :] = new
        else:
            fcols_new_ref[j - 4 : j - 3, :] = new
        update = outs[j][...] * lax.rsqrt((new_rows / mean_rows) * new)
        updates[j][...] = update
        return sum_all(update * update)

    def pick(tile, j):
        return tile[0:1, j : j + 1]

    def fan(i, ref, offsets):
        for db in offsets:
            b = place.batch_ahead(db)

            def one(k, carry=0, b=b):
                wire.make(i, ref, ref, (wrap(place.s + k, place.n_s), b)).start()
                return carry

            if place.n_s > 16:
                lax.fori_loop(0 if db else 1, place.n_s, one, 0)
            else:
                for k in outwards(place.n_s) + [0] * (db > 0):
                    one(k)

    near, others = [0], list(range(1, n_b))
    one_peer = place.along_z(1)

    g_second.finish()
    row_tile = gradient(5)
    g_q.to_owner()
    g_small.to_owner()
    g_first.finish()
    g_out.finish()
    mine_rows[pl.ds(0, r), :] = row_tile + gradient(4) + gradient(3)
    tail = pl.ds(r, 8)
    mine_rows[tail, :] = lanes_of(square_sums + row_sums_old + weight_squares)
    moved = []
    for dx, db in plane:
        peer = plane_peer(dx, db)
        if db == 0:
            moved.append(wire.send(lambda peer=peer: (mine, mine, peer)))
        if dx == 0:
            moved.append(wire.send(lambda peer=peer: (mine_rows, mine_rows, peer)))
        else:
            moved.append(wire.send(lambda peer=peer: (mine_rows.at[tail], mine_rows.at[tail], peer)))
    g_kv.finish()
    row_tile = gradient(1) + gradient(2)
    g_q.finish()
    mine_late_rows[...] = row_tile + gradient(0)
    written[2].start()
    written[3].start()
    sums = lanes_of(square_sums[:late])[0:1]
    mine_late[7:8, :] = sums
    late_sums[place.b] = jnp.zeros((place.n_s, 1, LANES), F32)
    mine_sums[...] = sums
    late_i, sums_i, all_i = wire.reserve(1), wire.reserve(1), wire.reserve(1)
    moved_rows = [
        wire.send(lambda k=k: (mine_late_rows, mine_late_rows, place.across_batch(k))) for k in range(1, n_b)
    ]
    fan(late_i, mine_late, near)
    fan(sums_i, mine_sums, others)

    received(moved)
    mine_z = all_z.at[place.z]
    mine_z[pl.ds(0, pad), :] = cols_plane[0] + cols_plane[1] + cols_plane[2] + cols_plane[3]
    scalars = jnp.zeros((8, LANES), F32)
    row_total = jnp.zeros((r, LANES), F32)
    for b in range(n_b):
        for xc in range(4):
            scalars = scalars + rows_plane[b, xc, tail, :]
        row_total = row_total + rows_plane[b, place.xc, pl.ds(0, r), :]
    mine_z[pl.ds(pad, 8), :] = scalars
    moved = [wire.send(lambda peer=peer: (mine_z, mine_z, peer)) for peer in along]

    received(moved)
    reduced = all_z[0]
    for z in range(1, n_z):
        reduced = reduced + all_z[z]
    tile = reduced[pad:]

    def scalar(j):
        return pick(tile, j)

    update_squares = [None] * SLABS
    for j in range(late, SLABS):
        update_squares[j] = renewed(j, row_total, reduced, scalar(j), scalar(SLABS + j))
    g_small.finish()
    own_grad = g_small.total(0) * own_mask
    own_sq = DECAY * to_frame(sq_ref[...].reshape(1, chunk), own_at) + (1.0 - DECAY) * (own_grad * own_grad + EPS_ONE)
    own_update = own_grad * lax.rsqrt(own_sq)
    update_squares.append(sum_all(own_update * own_update))
    for k in range(1, H + 1):
        for j in range(1, parts):
            near_kv(k, j).wait_send()
        if k < H:
            back_kv(k).wait_send()
    wire.drain()

    late_part = late_cols.at[pl.ds(0, place.n_s - 1)]
    sums_part = late_sums.at[pl.ds(0, n_b - 1)]
    wire.make(late_i, late_part, late_part, one_peer).wait_recv()
    wire.make(sums_i, sums_part, sums_part, one_peer).wait_recv()
    received(moved_rows)
    sums = late_cols[0]
    for s in range(1, place.n_s):
        sums = sums + late_cols[s]
    totals = jnp.zeros((1, LANES), F32)
    row_total = jnp.zeros((r, LANES), F32)
    for b in range(n_b):
        other = late_sums[b, 0]
        for s in range(1, place.n_s):
            other = other + late_sums[b, s]
        totals = totals + jnp.where(place.b == b, sums[7:8], other)
        row_total = row_total + late_rows[b]
    for j in range(late):
        update_squares[j] = renewed(j, row_total, sums, pick(totals, j), scalar(SLABS + j))
    written[4].start()
    written[5].start()
    rows_new_ref[...] = sum(rows_tiles[1:], rows_tiles[0])
    mine_u = all_sums.at[place.b * place.n_s + place.s]
    mine_u[...] = lanes_of(update_squares)[0:1]
    fan(all_i, mine_u, near + others)
    wire.make(late_i, late_part, late_part, one_peer).wait_send()
    wire.make(sums_i, sums_part, sums_part, one_peer).wait_send()
    all_part = all_sums.at[pl.ds(0, place.n_s * n_b - 1)]
    copy = wire.make(all_i, all_part, all_part, one_peer)
    copy.wait_send()
    copy.wait_recv()
    update_tile = jnp.zeros((1, LANES), F32)
    for i in range(place.n_s * n_b):
        update_tile = update_tile + all_sums[i]
    sizes = [D * D] * 4 + [D * FF] * 2 + [NVEC]

    def scale(j):
        weight = jnp.sqrt(scalar(2 * SLABS + j) * (1.0 / sizes[j]))
        return LEARN * weight / jnp.maximum(1.0, jnp.sqrt(update_tile[0:1, j : j + 1] * (1.0 / sizes[j])))

    scales_ref[...] = lanes_of([scale(j) for j in range(SLABS)])
    own_new_ref[0] = own_grad
    own_new_ref[1] = own - scale(SLABS) * own_update
    own_new_ref[2] = own_sq
    for copy in written:
        copy.wait()
    wire.drain()


def layer_part(groups, lengths, tok, cot, attn, ffn, params, arows, acols, frows, fcols, sq):
    n_s, n_b = lax.axis_size("seq"), lax.axis_size("batch")
    n_z, parts = n_s // 4, n_s // H
    count = tok.shape[0]
    tokens = count // 2
    rows = 2
    _, r, cols = attn.shape
    cols_f = ffn.shape[2]
    groups_q = H // GROUP
    width = GROUP * tokens
    length = tokens * n_s
    wide = min(512, cols_f)
    tiles = FF // wide
    pad = 4 * -(-cols // LANES) + 2 * (cols_f // LANES)
    pad = -(-pad // 8) * 8
    gather = (n_z - 1) + (1 + n_b) + 2 * (n_b - 1) + 1 + (n_b - 1) + 2 * (n_b - 1)
    copies = 5 * gather + 7 * (H - 1) + 2 * H + 2 * H * (parts - 1)
    copies += 6 * (1 + 2 * (n_b - 1) + n_b + n_z - 1)
    copies += 6 + 4 * n_b + (n_z - 1) + (n_b - 1) + 3

    def shape(dims, kind):
        return jax.ShapeDtypeStruct(dims, kind)

    out = (
        shape(tok.shape, BF),
        shape(tok.shape, BF),
        shape(attn.shape, F32),
        shape(ffn.shape, F32),
        shape(attn.shape, F32),
        shape(ffn.shape, F32),
        shape((8, LANES), F32),
        shape((r, LANES), F32),
        shape(acols.shape, F32),
        shape(fcols.shape, F32),
        shape((3, 8, LANES), F32),
    )
    vmem = pltpu.VMEM
    heads = (H, tokens, LANES)
    scratch = [
        vmem((1, r + 16, cols), BF),
        vmem((2, r, cols), BF),
        vmem((1, r, cols), BF),
        vmem(ffn.shape, BF),
        vmem((8, LANES), F32),
        vmem((FRAMES, 8, LANES), F32),
        vmem((n_b, 1, n_z, 4, r + 16, cols), BF),
        vmem((n_b, 2, n_z, 4, r, cols), BF),
        vmem((n_b, 1, n_z, 4, r, cols), BF),
        vmem((n_b, 1, n_z, 4, r, cols_f), BF),
        vmem((n_b, 1, n_z, 4, r, cols_f), BF),
        vmem((rows, length, LANES), F32),
        vmem((rows, groups_q, 1, width), F32),
        vmem(heads, BF),
        vmem((n_s, 2, tokens, LANES), BF),
        vmem(heads, BF),
        vmem((H, 2, tokens, LANES), BF),
        vmem((rows, groups_q, width, LANES), BF),
        vmem((rows, groups_q, width, LANES), BF),
        vmem((rows * groups_q, 1, width), F32),
        vmem((rows * groups_q, HD + 16, width), F32),
        vmem((groups_q, LANES, width), F32),
        vmem((rows * groups_q, 1, width), F32),
        vmem((rows * groups_q, 1, width), F32),
        vmem(heads, BF),
        vmem(heads, BF),
        vmem(heads, BF),
        vmem(heads, BF),
        vmem((tiles, count, wide), BF),
        vmem((tiles, count, wide), F32),
        vmem((tiles, count, wide), BF),
        vmem((count, D), F32),
        vmem((FRAMES, 8, LANES), F32),
        vmem((groups_q, LANES, width), F32),
        vmem((H, parts, 2, tokens, LANES), BF),
        vmem((parts - 1, H, 2, tokens, LANES), BF),
        vmem((H, 2, tokens, LANES), BF),
        vmem(heads, BF),
        vmem(heads, BF),
        vmem((H, 2, tokens, LANES), BF),
        vmem((n_b, 1, n_z, 2, 2, r, cols), BF),
        vmem((n_b, 1, n_z, 2, 2, r, cols_f), BF),
        vmem((n_b, 1, n_z, 2, 2, r, cols_f), BF),
        vmem((n_b, 2, n_z, 2, 2, r, cols), BF),
        vmem((n_b, 1, n_z, 2, 2, r, cols), BF),
        vmem((n_b, 1, n_z, 2, 2, 8, LANES), F32),
        vmem((4, pad, LANES), F32),
        vmem((n_b, 4, r + 8, LANES), F32),
        vmem((n_z, pad + 8, LANES), F32),
        vmem((n_s, 8, LANES), F32),
        vmem((n_b, r, LANES), F32),
        vmem((n_b, n_s, 1, LANES), F32),
        vmem((n_b * n_s, 1, LANES), F32),
        vmem(tok.shape, BF),
        vmem(tok.shape, BF),
        vmem(attn.shape, F32),
        vmem(ffn.shape, F32),
        vmem(attn.shape, F32),
        vmem(ffn.shape, F32),
    ]
    scratch += scatter_scratch(n_b, 1, n_z, r, cols_f, BF) * 2
    scratch += scatter_scratch(n_b, 1, n_z, r, cols, BF)
    scratch += short_scratch(n_b, 2, n_z, r, cols, BF)
    scratch += short_scratch(n_b, 1, n_z, r, cols, BF)
    scratch += short_scratch(n_b, 1, n_z, 8, LANES, F32)
    dma = pltpu.SemaphoreType.DMA
    scratch += [dma((copies,)), dma((copies,)), dma((11,))]
    return pl.pallas_call(
        layer_kernel,
        out_shape=out,
        in_specs=[SMEM_SPEC] + [VMEM_SPEC] * 11,
        out_specs=(pl.BlockSpec(memory_space=pl.ANY),) * 6 + (VMEM_SPEC,) * 5,
        scratch_shapes=scratch,
        compiler_params=pltpu.CompilerParams(
            vmem_limit_bytes=63 * 2**20, collective_id=0, has_side_effects=True
        ),
    )(groups, lengths, tok, cot, attn, ffn, params, arows, acols, frows, fcols, sq)


def result_kernel(
    out_in, du_in, agrad_in, fgrad_in, update_a, update_f, scales_ref, rows_ref, acols_in, fcols_in, own_ref,
    attn_ref, ffn_ref,
    out_ref, du_ref, agrad_ref, fgrad_ref, grad_ref, anew_ref, fnew_ref, new_ref, acopy_ref, fcopy_ref, copy_ref,
    arows_ref, acols_ref, frows_ref, fcols_ref, sq_ref,
):
    for src, dst in ((out_in, out_ref), (du_in, du_ref), (agrad_in, agrad_ref), (fgrad_in, fgrad_ref)):
        dst[...] = src[...]
    for j in range(4):
        new = attn_ref[j] - scales_ref[0:1, j : j + 1] * update_a[j]
        anew_ref[j] = new
        acopy_ref[j] = new.astype(BF)
    for j in range(2):
        new = ffn_ref[j] - scales_ref[0:1, 4 + j : 5 + j] * update_f[j]
        fnew_ref[j] = new
        fcopy_ref[j] = new.astype(BF)
    rows = rows_ref[...].T
    arows_ref[...] = rows[0:4]
    frows_ref[...] = rows[4:6]
    acols_ref[...] = acols_in[...]
    fcols_ref[...] = fcols_in[...]
    chunk = grad_ref.shape[0]
    at = own_place(chunk)
    grad_ref[...] = from_frame(own_ref[0], at, chunk).reshape(chunk)
    new = from_frame(own_ref[1], at, chunk)
    new_ref[...] = new.reshape(chunk)
    copy_ref[...] = new.astype(BF).reshape(chunk)
    sq_ref[...] = from_frame(own_ref[2], at, chunk).reshape(chunk)


def result_part(made, attn, ffn, chunk):
    out, _, agrad, fgrad, _, _, _, rows, acols, fcols, _ = made
    r = rows.shape[0]

    def shape(dims, kind):
        return jax.ShapeDtypeStruct(dims, kind)

    shapes = (
        shape(out.shape, BF),
        shape(out.shape, BF),
        shape(attn.shape, F32),
        shape(ffn.shape, F32),
        shape((chunk,), F32),
        shape(attn.shape, F32),
        shape(ffn.shape, F32),
        shape((chunk,), F32),
        shape(attn.shape, BF),
        shape(ffn.shape, BF),
        shape((chunk,), BF),
        shape((4, r), F32),
        shape(acols.shape, F32),
        shape((2, r), F32),
        shape(fcols.shape, F32),
        shape((chunk,), F32),
    )
    return pl.pallas_call(
        result_kernel,
        out_shape=shapes,
        in_specs=[VMEM_SPEC] * 13,
        out_specs=(VMEM_SPEC,) * 16,
        compiler_params=pltpu.CompilerParams(vmem_limit_bytes=60 * 2**20),
    )(*made, attn, ffn)


def shards(
    tokens, lengths, groups, cotangent, attn_weights, ffn_weights, small_params,
    attn_rows, attn_cols, ffn_rows, ffn_cols, small_sq,
):
    micro, rb, toks, _ = tokens.shape
    rows = micro * rb
    chunk = small_params.shape[0]
    made = layer_part(
        groups.reshape(rows),
        lengths.reshape(rows, SEGS),
        tokens.reshape(rows * toks, D),
        cotangent.reshape(rows * toks, D),
        attn_weights,
        ffn_weights,
        small_params,
        attn_rows,
        attn_cols,
        ffn_rows,
        ffn_cols,
        small_sq,
    )
    results = list(result_part(made, attn_weights, ffn_weights, chunk))
    for i in (0, 1):
        results[i] = results[i].reshape(tokens.shape)
    return tuple(results)


def solution(mesh):
    acts = P(None, "batch", "seq", None)
    weights = P(None, "seq", "batch")
    small = P(("seq", "batch"))
    rows, cols = P(None, "seq"), P(None, "batch")
    return jax.shard_map(
        shards,
        mesh=mesh,
        in_specs=(acts, P(None, "batch", None), P(None, "batch"), acts, weights, weights, small)
        + (rows, cols, rows, cols, small),
        out_specs=(acts, acts, weights, weights, small, weights, weights, small, weights, weights, small)
        + (rows, cols, rows, cols, small),
        check_vma=False,
    )
```
